32 devices in a mesh: dp: 8 (over z, x), mp: 4 (over y, core).
Axes of the slice: x: 2, y: 2, z: 4, core: 2. Of those that a mesh axis runs over, the one named last changes fastest.
Arguments:
- patches: bfloat16 [8192, 768], P('dp'), may hold values from -6 to 6
- patch_keep: int32 [8, 1024], P('dp'), may hold values 0 or 1
- patch_segment: int32 [8, 1024], P('dp'), may hold values from 0 to 7, never falling along the last dimension, each value on 1 to 256 neighbouring positions
- cotangent: bfloat16 [8192, 768], P('dp'), may hold values from -6 to 6
- w_qkv: bfloat16 [2, 3, 768, 768], P(None, None, None, 'mp'), may hold values from -0.21875 to 0.21875
- w_out: bfloat16 [2, 768, 768], P(None, 'mp'), may hold values from -1.75 to 1.75
- w_up: bfloat16 [2, 768, 3072], P(None, None, 'mp'), may hold values from -0.21875 to 0.21875
- w_down: bfloat16 [2, 3072, 768], P(None, 'mp'), may hold values from -0.109375 to 0.109375
- head_vectors: float32 [2, 6, 768], P(None, None, 'mp'), may hold values from -0.75 to 0.75
- up_bias: float32 [2, 3072], P(None, 'mp'), may hold values from -0.75 to 0.75
- row_vectors: float32 [2, 6, 768], replicated, may hold values from -0.75 to 0.75
Outputs:
- packed_out: bfloat16 [8192, 768], P('dp')
- grad_patches: float32 [8192, 768], P('dp')
- grad_qkv: float32 [2, 3, 768, 768], P(None, None, 'dp', 'mp')
- grad_out: float32 [2, 768, 768], P(None, 'mp', 'dp')
- grad_up: float32 [2, 768, 3072], P(None, 'dp', 'mp')
- grad_down: float32 [2, 3072, 768], P(None, 'mp', 'dp')
- grad_head_vectors: float32 [2, 6, 768], P(None, None, ('mp', 'dp'))
- grad_up_bias: float32 [2, 3072], P(None, ('mp', 'dp'))
- grad_row_vectors: float32 [2, 6, 768], P(None, None, 'dp')
The draws below stay inside these ranges and needn't reach their ends.
Inputs may be any that keep to these rules, and one draw needn't show every extreme that they name: `patch_segment`: along each row the image numbers never fall; each of the 8 images has 1 to 256 patches.
All inputs are finite; a program needn't handle non-finite values. No bound on the sum of `patch_keep` on one device may be relied on, other than what follows from the above.
Results may differ from the reference program's by a relative error of at most 0.013.
Values sent between devices are 32-bit elements; how exact they have to be, the bound alone decides.
A program may use at most 192 MiB of HBM per device.

```python
import math
import jax
import jax.numpy as jnp
import numpy as np
from jax import lax

HEADS = 12
HEAD = 64
D = 768
FF = 3072
SEQ = 1024
LAYERS = 2
TOKENS = 8192
N_DP = 8


def touch_ends(values, own_key, low, largest):
    shape = values.shape
    spot = [jax.random.randint(jax.random.fold_in(own_key, axis), (), 0, shape[axis]) for axis in range(len(shape))]
    values = values.at[tuple(spot)].set(low)
    longest = shape.index(max(shape))
    spot[longest] = (spot[longest] + 1) % shape[longest]
    return values.at[tuple(spot)].set(largest)


def raised(values, key, source, target, shards_of, factor):
    owner, partner = [(jnp.arange(values.shape[position]) // (values.shape[position] // shards_of)).reshape([-1 if axis == position else 1 for axis in range(values.ndim)]) for position in (source, target)]
    chosen = jax.random.permutation(key, shards_of)[partner]
    strong = (owner == chosen) | (owner == (partner + shards_of // 2) % shards_of)
    return jnp.where(strong, factor * values, values)


def block_levels(stream_key, dims, pieces, smallest, top_value):
    level = 1.0
    for position, shards_of in pieces:
        heights = jax.random.uniform(jax.random.fold_in(jax.random.fold_in(stream_key, 6), position), (shards_of,), jnp.float32, smallest / len(pieces), top_value / len(pieces))
        level = level * jnp.repeat(jnp.exp(heights), dims[position] // shards_of).reshape((-1,) + (1,) * (len(dims) - 1 - position))
    return level


def split_up(count, total, bound, lean):
    weights = [(1 << 20) // math.isqrt(rank ** lean) + 1 for rank in range(2, count + 1)]
    rest, counts = total - bound - (count - 1), [1] * (count - 1)
    while rest > 0:
        free = [i for i in range(count - 1) if counts[i] < bound]
        whole, budget = sum([weights[i] for i in free]), rest
        for i in free:
            addition = min(bound - counts[i], max(1, budget * weights[i] // whole), rest)
            counts[i] = counts[i] + addition
            rest = rest - addition
    return np.array([bound] + counts)


def ragged_sizes(stream_key, number_of, total, reach, slope):
    if number_of == 2:
        one = jax.random.randint(stream_key, (), max(1, total - reach), min(reach, total - 1) + 1)
        return jnp.stack([one, total - one])
    lengths = jnp.asarray(split_up(number_of, total, reach, slope), jnp.int32)
    twos = (number_of - 1) // 2
    giver, receiver = lengths[1:1 + 2 * twos:2], lengths[2:2 + 2 * twos:2]
    slack = jnp.minimum(giver - 1, reach - receiver)
    moved = jax.random.randint(jax.random.fold_in(stream_key, 1), (twos,), 0, 1 << 20) % (slack + 1)
    lengths = lengths.at[1:1 + 2 * twos:2].set(giver - moved).at[2:2 + 2 * twos:2].set(receiver + moved)
    return lengths[jax.random.permutation(jax.random.fold_in(stream_key, 2), number_of)]


def gaussian(stream_key, extent, spread, bound, shards=(), kind=jnp.bfloat16):
    gain = block_levels(stream_key, extent, shards, -0.22, 0.18) if shards else 1.0
    entries = jax.random.normal(stream_key, extent, jnp.float32) * spread * gain
    return jnp.minimum(jnp.maximum(entries, -bound), bound).astype(kind)


def heavy_noise(stream_key, dims, deviation, most, split, heavy, kind=jnp.bfloat16):
    values = deviation * jax.random.normal(stream_key, dims, jnp.float32)
    if split:
        values = values * block_levels(stream_key, dims, split, -0.22, 0.18)
    return jnp.clip(raised(values, jax.random.fold_in(stream_key, 3), *heavy), -most, most).astype(kind)


def setup_inputs(seed: int = 0) -> dict:
    key_list = jax.random.split(jax.random.key(seed), 12)
    return {
        "patches": gaussian(key_list[0], (TOKENS, D), 1.0, 6.0, ((0, 8),)),
        "patch_keep": touch_ends((jax.random.randint(key_list[1], (N_DP, SEQ), 0, 5) < 4).astype(jnp.int32), jax.random.fold_in(key_list[1], 1), 0, 1),
        "patch_segment": jax.vmap(lambda own: jnp.searchsorted(jnp.cumsum(ragged_sizes(own, 8, SEQ, SEQ // 4, 1)), jnp.arange(SEQ), side="right"))(jax.random.split(key_list[2], N_DP)).reshape((N_DP, SEQ)).astype(jnp.int32),
        "cotangent": heavy_noise(key_list[3], (TOKENS, D), 1.0, 6.0, ((0, 8),), (0, 1, 8, 2.0)),
        "w_qkv": gaussian(key_list[4], (LAYERS, 3, D, D), D ** -0.5, 0.21875, ((3, 4),)),
        "w_out": gaussian(key_list[5], (LAYERS, D, D), (D // 64) ** -0.5, 1.75, ((1, 4),)),
        "w_up": gaussian(key_list[6], (LAYERS, D, FF), D ** -0.5, 0.21875, ((2, 4),)),
        "w_down": gaussian(key_list[7], (LAYERS, FF, D), FF ** -0.5, 0.109375, ((1, 4),)),
        "head_vectors": gaussian(key_list[8], (LAYERS, 6, D), 0.3, 0.75, ((2, 4),), jnp.float32),
        "up_bias": gaussian(key_list[9], (LAYERS, FF), 0.3, 0.75, ((1, 4),), jnp.float32),
        "row_vectors": gaussian(key_list[10], (LAYERS, 6, D), 0.3, 0.75, (), jnp.float32),
    }


EPS = 1e-06
HIGH = lax.Precision.HIGHEST

@jax.custom_vjp
def low(v):
    return lax.optimization_barrier(v.astype(jnp.bfloat16)).astype(jnp.float32)

@jax.custom_vjp
def low_back(v):
    return v

def low_keep(v):
    return (low(v), None)

def low_pass(kept, grad):
    return (grad,)

def back_keep(v):
    return (v, None)

def back_low(kept, grad):
    return (low(grad),)
low.defvjp(low_keep, low_pass)
low_back.defvjp(back_keep, back_low)

def normalize(values):
    center = values - lax.optimization_barrier(jnp.mean(values, axis=-1, keepdims=True))
    return center * lax.rsqrt(lax.optimization_barrier(jnp.mean(center * center, axis=-1, keepdims=True)) + EPS)

def pack_rows(patch_rows, keep_row, segment_row):
    count_len = keep_row.shape[0]
    positions = jnp.arange(count_len, dtype=jnp.int32)
    slot_index = (jnp.cumsum(keep_row) - 1).astype(jnp.int32)
    target = jnp.where(keep_row > 0, slot_index, count_len).astype(jnp.int32)
    source = jnp.zeros((count_len,), jnp.int32).at[target].set(positions, mode='drop')
    live_mask = positions < jnp.sum(keep_row).astype(jnp.int32)
    image_slot = jnp.where(live_mask, segment_row[source], -1).astype(jnp.int32)
    packed = patch_rows[source] * live_mask[:, None].astype(jnp.float32)
    return (packed, live_mask, image_slot)

def layer(resid, same_image, w_qkv, w_out, w_up, w_down, head_vec, up_bias, row_vec):
    length = resid.shape[0]
    shaped = (length, HEADS, HEAD)
    normed = low(normalize(resid) * (1.0 + row_vec[0]) + row_vec[1])
    raw_qkv = low_back(jnp.einsum('sd,kde->kse', normed, w_qkv, precision=HIGH))
    query = normalize((raw_qkv[0] + head_vec[0]).reshape(shaped))
    query = low(query * (1.0 + head_vec[3]).reshape(HEADS, HEAD) + head_vec[5].reshape(HEADS, HEAD))
    keys = normalize((raw_qkv[1] + head_vec[1]).reshape(shaped))
    keys = low(keys * (1.0 + head_vec[4]).reshape(HEADS, HEAD))
    values = low((raw_qkv[2] + head_vec[2]).reshape(shaped))
    scores = low_back(jnp.einsum('qhe,khe->hqk', query, keys, precision=HIGH) * HEAD ** (-0.5))
    scores = jnp.where(same_image[None], scores, -1e+30)
    shifted = scores - lax.optimization_barrier(jnp.max(scores, axis=-1, keepdims=True))
    expo = jnp.exp(shifted)
    probs = low(expo / lax.optimization_barrier(jnp.sum(expo, axis=-1, keepdims=True)))
    attended = jnp.einsum('hqk,khe->qhe', probs, values, precision=HIGH)
    attended = low(low_back(attended)).reshape(length, D)
    branch = low_back(jnp.dot(attended, w_out, precision=HIGH) + row_vec[4])
    middle = resid + branch
    second = low(normalize(middle) * (1.0 + row_vec[2]) + row_vec[3])
    before = low_back(jnp.dot(second, w_up, precision=HIGH) + up_bias)
    hidden = low(jax.nn.gelu(before, approximate=False))
    return middle + low_back(jnp.dot(hidden, w_down, precision=HIGH) + row_vec[5])

def reference(patches, patch_keep, patch_segment, cotangent, w_qkv, w_out, w_up, w_down, head_vectors, up_bias, row_vectors):
    floats = tuple((item.astype(jnp.float32) for item in (patches, w_qkv, w_out, w_up, w_down, head_vectors, up_bias, row_vectors)))

    def forward(patch_all, wq_all, wo_all, wu_all, wd_all, hv_all, ub_all, rv_all):
        blocks = patch_all.reshape(N_DP, SEQ, D)

        def one_sequence(inputs):
            patch_rows, keep_row, segment_row = inputs
            packed, live_mask, image_slot = pack_rows(patch_rows, keep_row, segment_row)
            same_image = image_slot[:, None] == image_slot[None, :]
            resid = packed
            for layer_index in range(LAYERS):
                resid = layer(resid, same_image, wq_all[layer_index], wo_all[layer_index], wu_all[layer_index], wd_all[layer_index], hv_all[layer_index], ub_all[layer_index], rv_all[layer_index])
            return resid * live_mask[:, None].astype(jnp.float32)
        result = lax.map(jax.checkpoint(one_sequence), (blocks, patch_keep, patch_segment))
        return result.reshape(N_DP * SEQ, D)
    output, backward = jax.vjp(forward, *floats)
    grads = backward(cotangent.astype(jnp.float32))
    return (output.astype(jnp.bfloat16), grads[0], grads[1], grads[2], grads[3], grads[4], grads[5], grads[6], grads[7])
```

```python
import math

import jax
import jax.numpy as jnp
from jax import lax
from jax.experimental import pallas as pl
from jax.experimental.pallas import tpu as pltpu
from jax.sharding import PartitionSpec as P

MESH = pl.DeviceIdType.MESH
F32, BF16 = jnp.float32, jnp.bfloat16
HEAD = 64
LANES = 128
EPS = 1e-6
SCALE = HEAD**-0.5
EXP2_SCALE = SCALE / math.log(2.0)
CHUNK = 256
HALF = CHUNK // 2
WINDOW = 3
IMAGES = 8
EMPTY = HEAD + IMAGES
PAD = EMPTY + 1
APART = 2048.0
ROW_VECTORS, HEAD_VECTORS = 6, 6
UP_BIAS_ROW, HEAD_ROW, VEC_ROWS = 8, 9, 16


def mm(left, right):
    return jnp.dot(left, right, preferred_element_type=F32)


def mt(left, right):
    return lax.dot_general(left, right, (((1,), (1,)), ((), ())), preferred_element_type=F32)


def tm(left, right):
    return lax.dot_general(left, right, (((0,), (0,)), ((), ())), preferred_element_type=F32)


def norm_rows(values):
    center = values - jnp.mean(values, axis=-1, keepdims=True)
    rstd = lax.rsqrt(jnp.mean(center * center, axis=-1, keepdims=True) + EPS)
    return center * rstd, rstd


def norm_back(grad, hat, rstd):
    mean_grad = jnp.mean(grad, axis=-1, keepdims=True)
    mean_cross = jnp.mean(grad * hat, axis=-1, keepdims=True)
    return rstd * (grad - mean_grad - hat * mean_cross)


def head_mean(values):
    return jnp.sum(values, axis=-1, keepdims=True) * (1.0 / HEAD)


def norm_head(values, real):
    center = (values - head_mean(values)) * real
    rstd = lax.rsqrt(head_mean(center * center) + EPS)
    return center * rstd, rstd


def norm_head_back(grad, hat, rstd, real):
    return (rstd * real) * (grad - head_mean(grad) - hat * head_mean(grad * hat))


def column_sum(values):
    return jnp.sum(values, axis=0, keepdims=True)


def bit_of(index, bit):
    return (index // (1 << bit)) % 2


def flipped(index, bits):
    for bit in bits:
        index = index + (1 << bit) * (1 - 2 * bit_of(index, bit))
    return index


class GradSum:
    def __init__(self, n_dp, me, mp, order, grad, landing, send_sem, recv_sem, credit, first, out, out_sem):
        self.me, self.mp, self.order = me, mp, order
        self.steps = len(order)
        self.counts = [n_dp >> (k + 1) for k in range(self.steps)]
        self.offsets = [sum(self.counts[:k]) for k in range(self.steps)]
        self.grad, self.landing = grad, landing
        self.send_sem, self.recv_sem, self.credit = send_sem, recv_sem, credit
        self.first, self.out, self.out_sem = first, out, out_sem
        self.opened = set()
        self.taken = [0] * self.steps

    def turn(self, k):
        return sorted(range(self.counts[k]), key=lambda m: (m % 2 == 0, -m))

    def events(self):
        found = [(k, m) for k in range(self.steps) for m in self.turn(k)]
        if self.steps == 3:
            found = [(0, 3), (0, 1), (0, 2), (1, 1), (0, 0), (1, 0), (2, 0)]
        return found

    def later_bits(self, k, m):
        return [self.order[k + 1 + t] for t in range(self.steps - k - 1) if (m >> t) & 1]

    def copy(self, k, m):
        slot = self.offsets[k] + m
        block = flipped(self.me, [self.order[k]] + self.later_bits(k, m))
        return pltpu.make_async_remote_copy(
            src_ref=self.grad.at[block],
            dst_ref=self.landing.at[slot],
            send_sem=self.send_sem.at[slot],
            recv_sem=self.recv_sem.at[slot],
            device_id=(flipped(self.me, [self.order[k]]), self.mp),
            device_id_type=MESH,
        )

    def send(self, k, m):
        if not self.first and k not in self.opened:
            pl.semaphore_wait(self.credit.at[k], 1)
        self.opened.add(k)
        self.copy(k, m).start()

    def start(self):
        for m in self.turn(0):
            self.send(0, m)

    def result(self):
        return pltpu.make_async_copy(self.grad.at[self.me], self.out, self.out_sem)

    def take(self, k, m):
        self.copy(k, m).wait()
        block = flipped(self.me, self.later_bits(k, m))
        self.grad[block] += self.landing[self.offsets[k] + m]
        if k + 1 < self.steps and m % 2 == 1:
            self.send(k + 1, m // 2)
        self.taken[k] += 1
        if self.first and self.taken[k] == self.counts[k]:
            pl.semaphore_signal(
                self.credit.at[k], inc=1, device_id=(flipped(self.me, [self.order[k]]), self.mp), device_id_type=MESH
            )
        if sum(self.taken) == sum(self.counts):
            self.result().start()


def spread(grad_sum, places, plan):
    events = grad_sum.events()
    for position, event in enumerate(events):
        place = places[position * len(places) // len(events)]
        plan.setdefault(place, []).append((grad_sum, event))


def make_kernel(n_dp, tokens, width, hidden, heads, layers):
    chunks = tokens // CHUNK
    bits = n_dp.bit_length() - 1
    block = width // n_dp
    slots = heads * LANES
    qkv_cols = 3 * heads * HEAD
    last = layers - 1

    def kernel(
        keep_ref,
        seg_ref,
        hv_ref,
        ub_ref,
        rv_ref,
        patches_in,
        cot_in,
        wq_in,
        wo_in,
        wu_in,
        wd_in,
        packed_out,
        gpatch_out,
        gm_out,
        ga_out,
        vec_out,
        spill_q,
        spill_k,
        spill_v,
        spill_o,
        spill_a,
        spill_y,
        INP,
        WQ,
        WO,
        WU,
        WD,
        X,
        X1,
        A,
        C0,
        CT,
        Q,
        K,
        V,
        O,
        LSE,
        G0,
        GP0,
        QA,
        KA,
        LIVE,
        TROW,
        TCOL,
        PART,
        DBUF,
        YBUF,
        CBUF,
        CSEND,
        DX,
        DQ,
        DK,
        DV,
        GM,
        GA,
        RM,
        RA,
        VEC,
        VLAND,
        STAGE,
        load_sem,
        spill_sem,
        stage_sem,
        d_send,
        d_recv,
        y_send,
        y_recv,
        c_send,
        c_recv,
        m_send,
        m_recv,
        a_send,
        a_recv,
        credit_m,
        credit_a,
        v_send,
        v_recv,
        out_sem,
    ):
        dp = lax.axis_index("dp")
        mp = lax.axis_index("mp")
        core = mp % 2
        sibling = mp + 1 - 2 * core
        across = (mp + 2) % 4

        barrier = pltpu.get_barrier_semaphore()
        for other in (sibling, across):
            pl.semaphore_signal(barrier, inc=1, device_id=(dp, other), device_id_type=MESH)
        for bit in range(bits):
            pl.semaphore_signal(barrier, inc=1, device_id=(flipped(dp, [bit]), mp), device_id_type=MESH)

        lane = lax.broadcasted_iota(jnp.int32, (1, LANES), 1)
        real = (lane < HEAD).astype(F32)

        def load(source, target, index):
            return pltpu.make_async_copy(source, target, load_sem.at[index])

        def load_attn(layer):
            return [load(wq_in.at[layer], WQ, 0), load(wo_in.at[layer], WO, 1)]

        def load_mlp(layer):
            return [load(wu_in.at[layer], WU, 2), load(wd_in.at[layer], WD, 3)]

        def spills(back):
            pairs = [(Q, spill_q), (K, spill_k), (V, spill_v), (O, spill_o), (A, spill_a)]
            return [
                pltpu.make_async_copy(*((far, near) if back else (near, far)), spill_sem.at[index])
                for index, (near, far) in enumerate(pairs)
            ]

        def start(copies):
            for copy in copies:
                copy.start()

        def wait(copies):
            for copy in copies:
                copy.wait()

        def to_sibling(chunk):
            slot = chunk % 2
            return pltpu.make_async_remote_copy(
                src_ref=PART.at[chunk, 1 - core],
                dst_ref=DBUF.at[slot],
                send_sem=d_send.at[slot],
                recv_sem=d_recv.at[slot],
                device_id=(dp, sibling),
                device_id_type=MESH,
            )

        def to_across(phase, chunk):
            slot = phase % 2
            return pltpu.make_async_remote_copy(
                src_ref=PART.at[chunk, core],
                dst_ref=YBUF.at[slot, chunk],
                send_sem=y_send.at[slot, chunk],
                recv_sem=y_recv.at[slot, chunk],
                device_id=(dp, across),
                device_id_type=MESH,
            )

        def to_gather(chunk):
            slot = chunk % 2
            return pltpu.make_async_remote_copy(
                src_ref=CSEND,
                dst_ref=CBUF.at[slot],
                send_sem=c_send.at[slot],
                recv_sem=c_recv.at[slot],
                device_id=(dp, sibling),
                device_id_type=MESH,
            )

        def put_part(chunk, values):
            PART[chunk] = values.reshape(2, HALF, width)

        def send_part(phase, chunk):
            copy = to_sibling(chunk)
            copy.start()
            copy.wait()
            PART[chunk, core] += DBUF[chunk % 2]
            to_across(phase, chunk).start()

        def total_of(phase, chunk):
            to_across(phase, chunk).wait()
            return PART[chunk, core] + YBUF[phase % 2, chunk]

        def gather(chunk, own, target):
            CSEND[...] = own
            copy = to_gather(chunk)
            copy.start()
            target[core] = own.astype(target.dtype)
            copy.wait()
            target[1 - core] = CBUF[chunk % 2].astype(target.dtype)

        def whole(ref, chunk):
            return ref[chunk].reshape(CHUNK, width)

        def add_vec(layer, row, values):
            VEC[layer, row : row + 1, 0 : values.shape[1]] += values

        def rv(layer, row):
            return rv_ref[layer, row : row + 1, :]

        def hv(layer, row, head):
            return hv_ref[layer, row : row + 1, head * LANES : (head + 1) * LANES]

        def head_cols(values, head, first=0):
            return values[:, first + head * LANES : first + (head + 1) * LANES]

        def pack(chunk):
            rows = lax.broadcasted_iota(jnp.int32, (CHUNK, tokens), 0) + chunk * CHUNK
            chosen = (TROW[0:1, :].astype(jnp.int32) == rows).astype(F32).astype(BF16)
            values = mm(chosen, INP[...])
            classes = mm(chosen, QA[...].reshape(tokens, LANES))
            alive = jnp.sum(classes, axis=-1, keepdims=True)
            LIVE[chunk] = jnp.broadcast_to(alive, (CHUNK, LANES))
            KA[chunk] = (classes + jnp.where(lane == EMPTY, 1.0 - alive, 0.0)).astype(BF16)
            put_part(chunk, values)
            X[0, chunk] = PART[chunk, core]
            hat, _ = norm_rows(values)
            A[chunk] = (hat * (1.0 + rv(0, 0)) + rv(0, 1)).astype(BF16).reshape(2, HALF, width)

        def apart_of(chunk):
            is_class = (lane >= HEAD) & (lane <= PAD)
            return jnp.where(is_class, -APART * (1.0 - KA[chunk].astype(F32)), 0.0)

        def project(layer, chunk):
            raw = mm(whole(A, chunk), WQ[...])
            apart = apart_of(chunk)
            classes = KA[chunk].astype(F32)
            ones = (lane == HEAD).astype(F32)
            for head in range(heads):
                hat, _ = norm_head(head_cols(raw, head) + hv(layer, 0, head), real)
                Q[head, chunk] = (
                    (hat * (1.0 + hv(layer, 3, head)) + hv(layer, 5, head)).astype(BF16) + apart.astype(BF16)
                )
                hat, _ = norm_head(head_cols(raw, head, slots) + hv(layer, 1, head), real)
                K[head, chunk + 1] = (hat * (1.0 + hv(layer, 4, head))).astype(BF16) + classes.astype(BF16)
                V[head, chunk + 1] = (head_cols(raw, head, 2 * slots) + hv(layer, 2, head) + ones).astype(BF16)

        def window(ref, head, chunk):
            return ref[head, pl.ds(chunk, WINDOW)].reshape(WINDOW * CHUNK, LANES)

        def attend(layer, chunk):
            for head in range(heads):
                keys, values = window(K, head, chunk), window(V, head, chunk)
                scores = mt(keys, Q[head, chunk])
                expo = jnp.exp2(scores * EXP2_SCALE).astype(BF16)
                out = tm(values, expo)
                total = out[HEAD : HEAD + 1, :]
                LSE[layer, head, chunk] = jnp.log(total) * (1.0 / math.log(2.0))
                out = (out * (1.0 / total)).T
                O[head, chunk] = jnp.where(lane < HEAD, out, 0.0).astype(BF16)
            joined = jnp.concatenate([O[head, chunk] for head in range(heads)], axis=1)
            put_part(chunk, mm(joined, WO[...]))

        def attn_forward(layer, phase):
            def slot(i, carry):
                @pl.when(i < chunks)
                def _():
                    if layer == 0:
                        pack(i)
                    else:
                        x = X1[layer - 1, i] + total_of(phase - 1, i) + rv(layer - 1, 5)
                        X[layer, i] = x
                        hat, _ = norm_rows(x)
                        own = (hat * (1.0 + rv(layer, 0)) + rv(layer, 1)).astype(BF16).astype(F32)
                        gather(i, own, A.at[i])
                    project(layer, i)

                @pl.when(i > 0)
                def _():
                    attend(layer, i - 1)
                    send_part(phase, i - 1)

                return carry

            lax.fori_loop(0, chunks + 1, slot, 0)

        def middle(layer, phase, chunk, target):
            x1 = X[layer, chunk] + total_of(phase - 1, chunk) + rv(layer, 4)
            X1[layer, chunk] = x1
            hat, _ = norm_rows(x1)
            own = (hat * (1.0 + rv(layer, 2)) + rv(layer, 3)).astype(BF16).astype(F32)
            gather(chunk, own, target)

        def up(layer, second):
            before = mm(second, WU[...]) + ub_ref[layer : layer + 1, :]
            cdf = 0.5 * (1.0 + lax.erf(before * math.sqrt(0.5)))
            density = jnp.exp(before * before * -0.5) * (1.0 / math.sqrt(2.0 * math.pi))
            return (before * cdf).astype(BF16), cdf + before * density

        def mlp_forward(layer, phase):
            def slot(i, carry):
                middle(layer, phase, i, C0.at[i])
                act, slope = up(layer, whole(C0, i))
                G0[i] = act
                GP0[i] = slope.astype(BF16)
                put_part(i, mm(act, WD[...]))
                send_part(phase, i)
                return carry

            lax.fori_loop(0, chunks, slot, 0)

        def mlp_grads(layer, second, act, grad_out, grad_before):
            GM[layer, :, :, 0:hidden] += tm(second, grad_before).reshape(n_dp, block, hidden)
            GM[layer, :, :, hidden:] += tm(grad_out, act).reshape(n_dp, block, hidden)
            add_vec(layer, UP_BIAS_ROW, column_sum(grad_before.astype(F32)))

        def pump(name, i):
            for (where, index), events in plan.items():
                if where == name:

                    @pl.when(i == index)
                    def _():
                        for grad_sum, event in events:
                            grad_sum.take(*event)

        def mlp_turn(layer, phase):
            GM[layer] = jnp.zeros((n_dp, block, 2 * hidden), F32)

            def slot(i, carry):
                middle(layer, phase, i, CT.at[0])
                second = whole(CT, 0)
                act, slope = up(layer, second)

                @pl.when(i > 0)
                def _():
                    pltpu.make_async_copy(STAGE.at[0], spill_y.at[i - 1], stage_sem.at[0]).wait()

                STAGE[0] = mm(act, WD[...]).reshape(2, HALF, width)
                pltpu.make_async_copy(STAGE.at[0], spill_y.at[i], stage_sem.at[0]).start()
                grad = INP[pl.ds(i * CHUNK, CHUNK), :].astype(F32) * LIVE[i, :, 0:1]
                CT[1] = grad.astype(BF16).reshape(2, HALF, width)
                own = CT[1, core].astype(F32)
                DX[i] = own
                add_vec(layer, 5, column_sum(own))
                grad = grad.astype(BF16)
                grad_before = (mt(grad, WD[...]) * slope).astype(BF16)
                put_part(i, mt(grad_before, WU[...]))
                send_part(phase, i)
                mlp_grads(layer, second, act, grad, grad_before)
                return carry

            lax.fori_loop(0, chunks, slot, 0)
            pltpu.make_async_copy(STAGE.at[0], spill_y.at[chunks - 1], stage_sem.at[0]).wait()

        def input_back(layer, phase, chunk):
            grad_normed = total_of(phase - 1, chunk)
            hat, rstd = norm_rows(X[layer, chunk])
            add_vec(layer, 0, column_sum(grad_normed * hat))
            add_vec(layer, 1, column_sum(grad_normed))
            return DX[chunk] + norm_back(grad_normed * (1.0 + rv(layer, 0)), hat, rstd)

        def mlp_backward(layer, phase, name):
            GM[layer] = jnp.zeros((n_dp, block, 2 * hidden), F32)

            def slot(i, carry):
                grad = input_back(layer + 1, phase, i)
                DX[i] = grad
                own = grad.astype(BF16).astype(F32)
                add_vec(layer, 5, column_sum(own))
                gather(i, own, CT.at[0])
                grad = whole(CT, 0)
                grad_before = (mt(grad, WD[...]) * GP0[i].astype(F32)).astype(BF16)
                put_part(i, mt(grad_before, WU[...]))
                send_part(phase, i)
                mlp_grads(layer, whole(C0, i), G0[i], grad, grad_before)
                pump(name, i)
                return carry

            lax.fori_loop(0, chunks, slot, 0)

        def attend_back(layer, chunk):
            grad = whole(CT, 0)
            grad_heads = mt(grad, WO[...]).astype(BF16)
            ring = chunk % WINDOW
            for head in range(heads):
                grad_o = head_cols(grad_heads, head)
                query = Q[head, chunk]
                keys, values = window(K, head, chunk), window(V, head, chunk)
                delta = column_sum((O[head, chunk].astype(F32) * grad_o.astype(F32)).T)
                probs = jnp.exp2(mt(keys, query) * EXP2_SCALE - LSE[layer, head, chunk])
                grad_scores = (probs * (mt(values, grad_o) - delta)).astype(BF16)
                grad_v = mm(probs.astype(BF16), grad_o)
                grad_k = mm(grad_scores, query)
                DQ[chunk % 2, head] = tm(grad_scores, keys) * SCALE
                for part in range(WINDOW):
                    place = (ring + part + WINDOW - 1) % WINDOW
                    rows = slice(part * CHUNK, (part + 1) * CHUNK)
                    if part < WINDOW - 1:
                        DV[head, place] += grad_v[rows]
                        DK[head, place] += grad_k[rows]
                    else:
                        DV[head, place] = grad_v[rows]
                        DK[head, place] = grad_k[rows]
            out = [O[head, chunk].astype(F32) for head in range(heads)]
            pairs = [pltpu.roll(out[0], HEAD, 1), out[1] + pltpu.roll(out[2], HEAD, 1)]
            packed = jnp.concatenate(pairs, axis=1).astype(BF16)
            GA[layer, :, :, qkv_cols - HEAD :] += tm(grad, packed).reshape(n_dp, block, 2 * LANES)

        def project_back(layer, chunk):
            normed = whole(A, chunk)
            raw = mm(normed, WQ[:, 0 : 2 * slots])
            ring, turn = chunk % WINDOW, chunk % 2
            parts = [None] * (3 * heads)
            for head in range(heads):
                cols = head * LANES
                for kind, grad in ((0, DQ[turn, head]), (1, DK[head, ring] * SCALE)):
                    hat, rstd = norm_head(head_cols(raw, head, kind * slots) + hv(layer, kind, head), real)
                    gain = (1.0 + hv(layer, 3 + kind, head)) * real
                    inner = norm_head_back(grad * gain, hat, rstd, real)
                    sums = [(HEAD_ROW + kind, inner), (HEAD_ROW + 3 + kind, grad * hat)]
                    if kind == 0:
                        sums.append((HEAD_ROW + 5, grad))
                    for row, values in sums:
                        VEC[layer, row : row + 1, cols : cols + LANES] += column_sum(values)
                    parts[kind * heads + head] = inner
                grad_v = DV[head, ring]
                VEC[layer, HEAD_ROW + 2 : HEAD_ROW + 3, cols : cols + LANES] += column_sum(grad_v)
                parts[2 * heads + head] = grad_v
            padded = jnp.concatenate([part.astype(BF16) for part in parts], axis=1)
            put_part(chunk, mt(padded, WQ[...]))
            pairs = []
            for first in range(0, len(parts), 2):
                if first + 1 < len(parts):
                    pairs.append(parts[first] + pltpu.roll(parts[first + 1], HEAD, 1))
                else:
                    pairs.append(parts[first])
            dense = jnp.concatenate([pair.astype(BF16) for pair in pairs], axis=1)
            cols = len(pairs) * LANES
            GA[layer, :, :, 0:cols] += tm(normed, dense).reshape(n_dp, block, cols)

        def attn_backward(layer, phase, name):
            GA[layer] = jnp.zeros((n_dp, block, qkv_cols + heads * HEAD), F32)
            DK[...] = jnp.zeros_like(DK)
            DV[...] = jnp.zeros_like(DV)

            def slot(i, carry):
                @pl.when(i < chunks)
                def _():
                    grad_second = total_of(phase - 1, i)
                    hat, rstd = norm_rows(X1[layer, i])
                    add_vec(layer, 2, column_sum(grad_second * hat))
                    add_vec(layer, 3, column_sum(grad_second))
                    grad = DX[i] + norm_back(grad_second * (1.0 + rv(layer, 2)), hat, rstd)
                    DX[i] = grad
                    own = grad.astype(BF16).astype(F32)
                    add_vec(layer, 4, column_sum(own))
                    gather(i, own, CT.at[0])
                    attend_back(layer, i)

                @pl.when(i > 0)
                def _():
                    project_back(layer, i - 1)
                    send_part(phase, i - 1)

                pump(name, i)
                return carry

            lax.fori_loop(0, chunks + 1, slot, 0)

        near_first = [1, 0] + list(range(2, bits)) if bits > 1 else list(range(bits))

        def grad_sum(kind, layer):
            if kind == 0:
                parts = (list(range(bits)), GM, RM, m_send, m_recv, credit_m, gm_out)
            else:
                parts = (near_first, GA, RA, a_send, a_recv, credit_a, ga_out)
            order, grad, landing, sends, recvs, credit, out = parts
            return GradSum(
                n_dp, dp, mp, order, grad.at[layer], landing, sends, recvs, credit, layer == last,
                out.at[layer], out_sem.at[2 * layer + kind],
            )

        mlp_last, attn_last = grad_sum(0, last), grad_sum(1, last)
        mlp_first, attn_first = grad_sum(0, 0), grad_sum(1, 0)
        plan = {}
        spread(mlp_last, [("a1", 2), ("a1", 3), ("a1", 4), ("m0", 0), ("m0", 1), ("m0", 2), ("m0", 3)], plan)
        spread(attn_last, [("m0", 2), ("m0", 3), ("a0", 0), ("a0", 1), ("a0", 2)], plan)
        spread(mlp_first, [("a0", 3), ("a0", 4), ("end", 0), ("end", 1), ("end", 2), ("end", 3)], plan)

        first_loads = [load(patches_in, INP, 4)]
        start(first_loads + load_attn(0) + load_mlp(0))
        VEC[...] = jnp.zeros_like(VEC)
        keep = jnp.broadcast_to(keep_ref[...].astype(F32), (8, tokens))
        earlier = lax.broadcasted_iota(jnp.int32, (tokens, tokens), 0)
        later = lax.broadcasted_iota(jnp.int32, (tokens, tokens), 1)
        count = mm(keep.astype(BF16), (earlier <= later).astype(F32).astype(BF16))
        place = jnp.where(keep > 0.0, count - 1.0, 2.0 * tokens)
        TROW[...] = place
        TCOL[...] = jnp.broadcast_to(place[0:1, :], (LANES, tokens)).T
        segment = jnp.broadcast_to(seg_ref[...].astype(F32), (LANES, tokens)).T
        QA[...] = (segment.astype(jnp.int32) == lane - HEAD).astype(F32).astype(BF16).reshape(chunks, CHUNK, LANES)
        padding = jnp.broadcast_to((lane == PAD).astype(F32), (CHUNK, LANES)).astype(BF16)
        for head in range(heads):
            for edge in (0, chunks + 1):
                K[head, edge] = padding
                V[head, edge] = jnp.zeros((CHUNK, LANES), BF16)
        wait(first_loads + load_attn(0))
        pl.semaphore_wait(barrier, 2 + bits)

        attn_forward(0, 0)
        cot_load = [load(cot_in, INP, 4)]
        start(spills(False) + load_attn(1) + cot_load)
        wait(load_mlp(0))
        mlp_forward(0, 1)
        wait(spills(False) + load_attn(1))
        start(load_mlp(1))
        attn_forward(1, 2)
        wait(load_mlp(1) + cot_load)
        mlp_turn(1, 3)
        start(load_mlp(0))
        mlp_last.start()
        attn_backward(1, 4, "a1")
        attn_last.start()
        start(spills(True) + load_attn(0))
        wait(load_mlp(0))
        mlp_backward(0, 5, "m0")
        mlp_first.start()
        wait(spills(True) + load_attn(0))
        attn_backward(0, 6, "a0")
        attn_first.start()

        def end_slot(i, carry):
            rows = input_back(0, 7, i)
            reload = pltpu.make_async_copy(spill_y.at[i], PART.at[i], stage_sem.at[0])
            reload.start()
            CSEND[...] = rows
            copy = to_gather(i)
            copy.start()
            X1[0, i] = rows
            copy.wait()
            X[last, i] = CBUF[i % 2]
            reload.wait()
            send_part(7, i)
            pump("end", i)
            return carry

        lax.fori_loop(0, chunks, end_slot, 0)

        def vec_copy(step, target):
            return pltpu.make_async_remote_copy(
                src_ref=VEC,
                dst_ref=VLAND.at[step],
                send_sem=v_send.at[step],
                recv_sem=v_recv.at[step],
                device_id=target,
                device_id_type=MESH,
            )

        copy = vec_copy(0, (dp, sibling))
        copy.start()
        copy.wait()
        VEC[:, 0:UP_BIAS_ROW, :] += VLAND[0, :, 0:UP_BIAS_ROW, :]

        def unpack(patch_chunk, stage):
            stage[...] = jnp.zeros(stage.shape, F32)
            place = TCOL[pl.ds(patch_chunk * CHUNK, CHUNK), 0:1].astype(jnp.int32)

            def add_slots(chunk, carry):
                slot = lax.broadcasted_iota(jnp.int32, (CHUNK, CHUNK), 1) + chunk * CHUNK
                chosen = (place == slot).astype(F32).astype(BF16)
                own, other = X1[0, chunk], X[last, chunk]
                rest = jnp.concatenate([jnp.where(core == 0, own, other), jnp.where(core == 0, other, own)], axis=0)
                for _ in range(3):
                    piece = rest.astype(BF16)
                    stage[...] += mm(chosen, piece).reshape(stage.shape)
                    rest = rest - piece.astype(F32)
                return carry

            lax.fori_loop(0, patch_chunk + 1, add_slots, 0)

        def patch_copy(patch_chunk, turn):
            return pltpu.make_async_copy(STAGE.at[turn], gpatch_out.at[patch_chunk], stage_sem.at[turn])

        for patch_chunk in range(chunks):
            turn = patch_chunk % 2
            if patch_chunk >= 2:
                patch_copy(patch_chunk - 2, turn).wait()
            unpack(patch_chunk, STAGE.at[turn])
            patch_copy(patch_chunk, turn).start()
            if patch_chunk < bits:
                copy = vec_copy(1 + patch_chunk, (flipped(dp, [patch_chunk]), mp))
                copy.start()
                copy.wait()
                VEC[...] += VLAND[1 + patch_chunk]
        for step in range(chunks, bits):
            copy = vec_copy(1 + step, (flipped(dp, [step]), mp))
            copy.start()
            copy.wait()
            VEC[...] += VLAND[1 + step]
        vec_done = pltpu.make_async_copy(VEC, vec_out, out_sem.at[2 * layers])
        vec_done.start()
        for patch_chunk in range(max(0, chunks - 2), chunks):
            patch_copy(patch_chunk, patch_chunk % 2).wait()

        events = attn_first.events()

        def out_copy(chunk):
            return pltpu.make_async_copy(A.at[chunk], packed_out.at[chunk], spill_sem.at[0])

        def out_slot(i, carry):
            rows = (X1[last, i] + total_of(7, i) + rv(last, 5)) * LIVE[i, pl.ds(core * HALF, HALF), 0:1]
            gather(i, rows.astype(BF16).astype(F32), A.at[i])
            out_copy(i).start()
            return carry

        lax.fori_loop(0, chunks, out_slot, 0)
        for event in events:
            attn_first.take(*event)

        def out_wait(i, carry):
            out_copy(i).wait()
            return carry

        lax.fori_loop(0, chunks, out_wait, 0)
        vec_done.wait()
        for finished in (mlp_last, attn_last, mlp_first, attn_first):
            assert finished.taken == finished.counts
            finished.result().wait()

    return kernel


def body(n_dp, patches, patch_keep, patch_segment, cotangent, w_qkv, w_out, w_up, w_down, head_vectors, up_bias, row_vectors):
    tokens, width = patches.shape
    layers = w_qkv.shape[0]
    channels = w_qkv.shape[3]
    heads = channels // HEAD
    hidden = w_up.shape[2]
    chunks = tokens // CHUNK
    slots = heads * LANES
    bits = n_dp.bit_length() - 1
    block = width // n_dp
    attn_cols = 4 * channels

    def padded(values, axis):
        shape = values.shape
        split = values.reshape(shape[:axis] + (heads, HEAD) + shape[axis + 1 :])
        pads = [(0, 0)] * split.ndim
        pads[axis + 1] = (0, LANES - HEAD)
        return jnp.pad(split, pads).reshape(shape[:axis] + (slots,) + shape[axis + 1 :])

    wq = padded(w_qkv, 3).transpose(0, 2, 1, 3).reshape(layers, width, 3 * slots)
    wo = padded(w_out, 1)
    hv = padded(head_vectors, 2)
    any_space = pl.BlockSpec(memory_space=pl.ANY)
    vmem = pl.BlockSpec(memory_space=pltpu.VMEM)
    sds = jax.ShapeDtypeStruct
    half = (HALF, width)
    head_chunks = (heads, chunks, CHUNK, LANES)
    head_window = (heads, chunks + 2, CHUNK, LANES)
    out_shape = [
        sds((chunks, 2) + half, BF16),
        sds((chunks, 2) + half, F32),
        sds((layers, block, 2 * hidden), F32),
        sds((layers, block, attn_cols), F32),
        sds((layers, VEC_ROWS, width), F32),
        sds(head_chunks, BF16),
        sds(head_window, BF16),
        sds(head_window, BF16),
        sds(head_chunks, BF16),
        sds((chunks, 2) + half, BF16),
        sds((chunks, 2) + half, F32),
    ]
    v = pltpu.VMEM
    dma = pltpu.SemaphoreType.DMA
    scratch = [
        v((tokens, width), BF16),
        v((width, 3 * slots), BF16),
        v((slots, width), BF16),
        v((width, hidden), BF16),
        v((hidden, width), BF16),
        v((layers, chunks) + half, F32),
        v((layers, chunks) + half, F32),
        v((chunks, 2) + half, BF16),
        v((chunks, 2) + half, BF16),
        v((2, 2) + half, BF16),
        v(head_chunks, BF16),
        v(head_window, BF16),
        v(head_window, BF16),
        v(head_chunks, BF16),
        v((layers, heads, chunks, 1, CHUNK), F32),
        v((chunks, CHUNK, hidden), BF16),
        v((chunks, CHUNK, hidden), BF16),
        v((chunks, CHUNK, LANES), BF16),
        v((chunks, CHUNK, LANES), BF16),
        v((chunks, CHUNK, LANES), F32),
        v((8, tokens), F32),
        v((tokens, LANES), F32),
        v((chunks, 2) + half, F32),
        v((2,) + half, F32),
        v((2, chunks) + half, F32),
        v((2,) + half, F32),
        v(half, F32),
        v((chunks,) + half, F32),
        v((2, heads, CHUNK, LANES), F32),
        v((heads, WINDOW, CHUNK, LANES), F32),
        v((heads, WINDOW, CHUNK, LANES), F32),
        v((layers, n_dp, block, 2 * hidden), F32),
        v((layers, n_dp, block, attn_cols), F32),
        v((n_dp - 1, block, 2 * hidden), F32),
        v((n_dp - 1, block, attn_cols), F32),
        v((layers, VEC_ROWS, width), F32),
        v((bits + 1, layers, VEC_ROWS, width), F32),
        v((2, 2) + half, F32),
        dma((5,)),
        dma((5,)),
        dma((2,)),
        dma((2,)),
        dma((2,)),
        dma((2, chunks)),
        dma((2, chunks)),
        dma((2,)),
        dma((2,)),
        dma((n_dp - 1,)),
        dma((n_dp - 1,)),
        dma((n_dp - 1,)),
        dma((n_dp - 1,)),
        pltpu.SemaphoreType.REGULAR((bits,)),
        pltpu.SemaphoreType.REGULAR((bits,)),
        dma((bits + 1,)),
        dma((bits + 1,)),
        dma((2 * layers + 1,)),
    ]
    results = pl.pallas_call(
        make_kernel(n_dp, tokens, width, hidden, heads, layers),
        out_shape=out_shape,
        in_specs=[vmem] * 5 + [any_space] * 6,
        out_specs=[any_space] * len(out_shape),
        scratch_shapes=scratch,
        compiler_params=pltpu.CompilerParams(
            collective_id=0, has_side_effects=True, vmem_limit_bytes=64 * 2**20 - 2**16
        ),
    )(patch_keep, patch_segment, hv, up_bias, row_vectors, patches, cotangent, wq, wo, w_up, w_down)
    packed, grad_patches, gm, ga, vec = results[:5]

    place = lax.axis_index("dp")

    def mine(values):
        share = values.shape[-1] // n_dp
        return lax.dynamic_slice_in_dim(values, place * share, share, axis=values.ndim - 1)

    grad_qkv = ga[:, :, : 3 * channels].reshape(layers, block, 3, channels).transpose(0, 2, 1, 3)
    grad_out = ga[:, :, 3 * channels :].transpose(0, 2, 1)
    grad_up = gm[:, :, :hidden]
    grad_down = gm[:, :, hidden:].transpose(0, 2, 1)
    head_rows = vec[:, HEAD_ROW : HEAD_ROW + HEAD_VECTORS, :slots].reshape(layers, HEAD_VECTORS, heads, LANES)
    head_grads = mine(head_rows[..., :HEAD].reshape(layers, HEAD_VECTORS, channels))
    return (
        packed.reshape(tokens, width),
        grad_patches.reshape(tokens, width),
        grad_qkv,
        grad_out,
        grad_up,
        grad_down,
        head_grads,
        mine(vec[:, UP_BIAS_ROW, :hidden]),
        mine(vec[:, 0:ROW_VECTORS, :]),
    )


def solution(mesh):
    n_dp = mesh.shape["dp"]

    def step(*args):
        return body(n_dp, *args)

    return jax.shard_map(
        step,
        mesh=mesh,
        in_specs=(
            P("dp", None),
            P("dp", None),
            P("dp", None),
            P("dp", None),
            P(None, None, None, "mp"),
            P(None, "mp", None),
            P(None, None, "mp"),
            P(None, "mp", None),
            P(None, None, "mp"),
            P(None, "mp"),
            P(),
        ),
        out_specs=(
            P("dp", None),
            P("dp", None),
            P(None, None, "dp", "mp"),
            P(None, "mp", "dp"),
            P(None, "dp", "mp"),
            P(None, "mp", "dp"),
            P(None, None, ("mp", "dp")),
            P(None, ("mp", "dp")),
            P(None, None, "dp"),
        ),
        check_vma=False,
    )
```

```python
import math

import jax
import jax.numpy as jnp
from jax import lax
from jax.experimental import pallas as pl
from jax.experimental.pallas import tpu as pltpu
from jax.sharding import PartitionSpec as P

MESH = pl.DeviceIdType.MESH
F32, BF16 = jnp.float32, jnp.bfloat16
HEAD = 64
LANES = 128
EPS = 1e-6
SCALE = HEAD**-0.5
EXP2_SCALE = SCALE / math.log(2.0)
CHUNK = 256
HALF = CHUNK // 2
WINDOW = 3
IMAGES = 8
EMPTY = HEAD + IMAGES
PAD = EMPTY + 1
APART = 2048.0
ROW_VECTORS, HEAD_VECTORS = 6, 6
UP_BIAS_ROW, HEAD_ROW, VEC_ROWS = 8, 9, 16


def mm(left, right):
    return jnp.dot(left, right, preferred_element_type=F32)


def mt(left, right):
    return lax.dot_general(left, right, (((1,), (1,)), ((), ())), preferred_element_type=F32)


def tm(left, right):
    return lax.dot_general(left, right, (((0,), (0,)), ((), ())), preferred_element_type=F32)


def norm_rows(values):
    center = values - jnp.mean(values, axis=-1, keepdims=True)
    rstd = lax.rsqrt(jnp.mean(center * center, axis=-1, keepdims=True) + EPS)
    return center * rstd, rstd


def norm_back(grad, hat, rstd):
    mean_grad = jnp.mean(grad, axis=-1, keepdims=True)
    mean_cross = jnp.mean(grad * hat, axis=-1, keepdims=True)
    return rstd * (grad - mean_grad - hat * mean_cross)


def head_mean(values):
    return jnp.sum(values, axis=-1, keepdims=True) * (1.0 / HEAD)


def norm_head(values, real):
    center = (values - head_mean(values)) * real
    rstd = lax.rsqrt(head_mean(center * center) + EPS)
    return center * rstd, rstd


def norm_head_back(grad, hat, rstd, real):
    return (rstd * real) * (grad - head_mean(grad) - hat * head_mean(grad * hat))


def column_sum(values):
    return jnp.sum(values, axis=0, keepdims=True)


def bit_of(index, bit):
    return (index // (1 << bit)) % 2


def flipped(index, bits):
    for bit in bits:
        index = index + (1 << bit) * (1 - 2 * bit_of(index, bit))
    return index


class GradSum:
    def __init__(self, n_dp, me, mp, order, grad, landing, send_sem, recv_sem, credit, next_order, finish):
        self.me, self.mp, self.order = me, mp, order
        self.steps = len(order)
        self.counts = [n_dp >> (k + 1) for k in range(self.steps)]
        self.offsets = [sum(self.counts[:k]) for k in range(self.steps)]
        self.grad, self.landing = grad, landing
        self.send_sem, self.recv_sem, self.credit = send_sem, recv_sem, credit
        self.next_order, self.finish = next_order, finish
        self.opened = set()
        self.taken = [0] * self.steps

    def turn(self, k):
        return sorted(range(self.counts[k]), key=lambda m: (m % 2 == 0, -m))

    def events(self):
        found = [(k, m) for k in range(self.steps) for m in self.turn(k)]
        if self.steps == 3:
            found = [(0, 3), (0, 1), (0, 2), (1, 1), (0, 0), (1, 0), (2, 0)]
        return found

    def later_bits(self, k, m):
        return [self.order[k + 1 + t] for t in range(self.steps - k - 1) if (m >> t) & 1]

    def copy(self, k, m):
        slot = self.offsets[k] + m
        block = flipped(self.me, [self.order[k]] + self.later_bits(k, m))
        return pltpu.make_async_remote_copy(
            src_ref=self.grad.at[block],
            dst_ref=self.landing.at[slot],
            send_sem=self.send_sem.at[slot],
            recv_sem=self.recv_sem.at[slot],
            device_id=(flipped(self.me, [self.order[k]]), self.mp),
            device_id_type=MESH,
        )

    def send(self, k, m):
        if self.next_order is None and k not in self.opened:
            pl.semaphore_wait(self.credit.at[k], 1)
        self.opened.add(k)
        self.copy(k, m).start()

    def start(self):
        for m in self.turn(0):
            self.send(0, m)

    def take(self, k, m):
        self.copy(k, m).wait()
        block = flipped(self.me, self.later_bits(k, m))
        self.grad[block] += self.landing[self.offsets[k] + m]
        if k + 1 < self.steps and m % 2 == 1:
            self.send(k + 1, m // 2)
        self.taken[k] += 1
        if self.next_order is not None and self.taken[k] == self.counts[k]:
            pl.semaphore_signal(
                self.credit.at[k], inc=1, device_id=(flipped(self.me, [self.next_order[k]]), self.mp), device_id_type=MESH
            )
        if sum(self.taken) == sum(self.counts):
            self.finish(self.grad)


def spread(grad_sum, places, plan):
    events = grad_sum.events()
    for position, event in enumerate(events):
        place = places[position * len(places) // len(events)]
        plan.setdefault(place, []).append((grad_sum, event))


def make_kernel(n_dp, tokens, width, hidden, heads, layers):
    chunks = tokens // CHUNK
    bits = n_dp.bit_length() - 1
    block = width // n_dp
    slots = heads * LANES
    channels = heads * HEAD
    attn_cols = 4 * channels
    last = layers - 1

    def kernel(
        keep_ref,
        seg_ref,
        hv_ref,
        ub_ref,
        rv_ref,
        patches_in,
        cot_in,
        wq_in,
        wo_in,
        wu_in,
        wd_in,
        packed_out,
        gpatch_out,
        qkv_out,
        wo_out,
        up_out,
        down_out,
        head_out,
        bias_out,
        row_out,
        spill_q,
        spill_k,
        spill_v,
        spill_o,
        spill_a,
        spill_y,
        INP,
        WQ,
        WO,
        WU,
        WD,
        X,
        X1,
        A,
        C0,
        CT,
        Q,
        K,
        V,
        O,
        LSE,
        HV,
        G0,
        GP0,
        QA,
        KA,
        LIVE,
        TROW,
        TCOL,
        PART,
        DBUF,
        YBUF,
        CBUF,
        CSEND,
        DX,
        DQ,
        HATS,
        DK,
        DV,
        GM,
        GA,
        RM,
        RA,
        VEC,
        VLAND,
        STAGE,
        QKV_STAGE,
        WO_STAGE,
        load_sem,
        spill_sem,
        stage_sem,
        d_send,
        d_recv,
        y_send,
        y_recv,
        c_send,
        c_recv,
        m_send,
        m_recv,
        a_send,
        a_recv,
        credit_m,
        credit_a,
        v_send,
        v_recv,
        out_sem,
    ):
        dp = lax.axis_index("dp")
        mp = lax.axis_index("mp")
        core = mp % 2
        sibling = mp + 1 - 2 * core
        across = (mp + 2) % 4

        barrier = pltpu.get_barrier_semaphore()
        for other in (sibling, across):
            pl.semaphore_signal(barrier, inc=1, device_id=(dp, other), device_id_type=MESH)
        for bit in range(bits):
            pl.semaphore_signal(barrier, inc=1, device_id=(flipped(dp, [bit]), mp), device_id_type=MESH)

        lane = lax.broadcasted_iota(jnp.int32, (1, LANES), 1)
        real = (lane < HEAD).astype(F32)

        def load(source, target, index):
            return pltpu.make_async_copy(source, target, load_sem.at[index])

        def load_attn(layer):
            return [
                load(wq_in.at[layer], WQ.at[:, 0:channels], 0),
                load(wo_in.at[layer], WO.at[0:channels], 1),
            ]

        def load_mlp(layer):
            return [load(wu_in.at[layer], WU, 2), load(wd_in.at[layer], WD, 3)]

        def spills(back):
            pairs = [(Q, spill_q), (K, spill_k), (V, spill_v), (O, spill_o), (A, spill_a)]
            return [
                pltpu.make_async_copy(*((far, near) if back else (near, far)), spill_sem.at[index])
                for index, (near, far) in enumerate(pairs)
            ]

        def start(copies):
            for copy in copies:
                copy.start()

        def wait(copies):
            for copy in copies:
                copy.wait()

        def to_sibling(chunk):
            slot = chunk % 2
            return pltpu.make_async_remote_copy(
                src_ref=PART.at[chunk, 1 - core],
                dst_ref=DBUF.at[slot],
                send_sem=d_send.at[slot],
                recv_sem=d_recv.at[slot],
                device_id=(dp, sibling),
                device_id_type=MESH,
            )

        def to_across(phase, chunk):
            slot = phase % 2
            return pltpu.make_async_remote_copy(
                src_ref=PART.at[chunk, core],
                dst_ref=YBUF.at[slot, chunk],
                send_sem=y_send.at[slot, chunk],
                recv_sem=y_recv.at[slot, chunk],
                device_id=(dp, across),
                device_id_type=MESH,
            )

        def to_gather(turn):
            return pltpu.make_async_remote_copy(
                src_ref=CSEND,
                dst_ref=CBUF.at[turn],
                send_sem=c_send.at[turn],
                recv_sem=c_recv.at[turn],
                device_id=(dp, sibling),
                device_id_type=MESH,
            )

        def put_part(chunk, values):
            PART[chunk] = values.reshape(2, HALF, width)
            to_sibling(chunk).start()

        def send_part(phase, chunk):
            to_sibling(chunk).wait()
            PART[chunk, core] += DBUF[chunk % 2]
            to_across(phase, chunk).start()

        def total_of(phase, chunk):
            to_across(phase, chunk).wait()
            return PART[chunk, core] + YBUF[phase % 2, chunk]

        def open_gather(turn, own, target):
            CSEND[...] = own
            to_gather(turn).start()
            target[core] = own.astype(target.dtype)

        def close_gather(turn, target):
            to_gather(turn).wait()
            target[1 - core] = CBUF[turn].astype(target.dtype)

        def whole(ref, chunk):
            return ref[chunk].reshape(CHUNK, width)

        def add_vec(layer, row, values):
            VEC[layer, row : row + 1, 0 : values.shape[1]] += values

        def rv(layer, row):
            return rv_ref[row, layer : layer + 1, :]

        def hv(layer, row, head):
            return HV[row, layer : layer + 1, head * LANES : (head + 1) * LANES]

        def swap_halves(tile):
            return pltpu.roll(tile, HEAD, 1)

        def apart_heads(values):
            tiles = []
            for head in range(heads):
                tile = values[:, head // 2 * LANES : (head // 2 + 1) * LANES]
                tiles.append((swap_halves(tile) if head % 2 else tile) * real)
            return tiles

        def joined_heads(tiles):
            pairs = [
                tiles[first] + swap_halves(tiles[first + 1]) if first + 1 < len(tiles) else tiles[first]
                for first in range(0, len(tiles), 2)
            ]
            return jnp.concatenate([pair.astype(BF16) for pair in pairs], axis=1)

        def pack(chunk):
            rows = lax.broadcasted_iota(jnp.int32, (CHUNK, tokens), 0) + chunk * CHUNK
            chosen = (TROW[0:1, :].astype(jnp.int32) == rows).astype(F32).astype(BF16)
            values = mm(chosen, INP[...])
            classes = mm(chosen, QA[...].reshape(tokens, LANES))
            alive = jnp.sum(classes, axis=-1, keepdims=True)
            LIVE[chunk] = jnp.broadcast_to(alive, (CHUNK, LANES))
            KA[chunk] = (classes + jnp.where(lane == EMPTY, 1.0 - alive, 0.0)).astype(BF16)
            PART[chunk] = values.reshape(2, HALF, width)
            X[0, chunk] = PART[chunk, core]
            hat, _ = norm_rows(values)
            A[chunk] = (hat * (1.0 + rv(0, 0)) + rv(0, 1)).astype(BF16).reshape(2, HALF, width)

        def apart_of(chunk):
            is_class = (lane >= HEAD) & (lane <= PAD)
            return jnp.where(is_class, -APART * (1.0 - KA[chunk].astype(F32)), 0.0)

        def project(layer, chunk):
            normed = whole(A, chunk)
            raw_q, raw_k, raw_v = (apart_heads(mt(normed, WQ[kind])) for kind in range(3))
            apart = apart_of(chunk).astype(BF16)
            classes = KA[chunk]
            ones = (lane == HEAD).astype(F32)
            for head in range(heads):
                hat, _ = norm_head(raw_q[head] + hv(layer, 0, head), real)
                Q[head, chunk] = (hat * (1.0 + hv(layer, 3, head)) + hv(layer, 5, head)).astype(BF16) + apart
                hat, _ = norm_head(raw_k[head] + hv(layer, 1, head), real)
                K[head, chunk + 1] = (hat * (1.0 + hv(layer, 4, head))).astype(BF16) + classes
                V[head, chunk + 1] = (raw_v[head] + hv(layer, 2, head) + ones).astype(BF16)

        def window(ref, head, chunk):
            return ref[head, pl.ds(chunk, WINDOW)].reshape(WINDOW * CHUNK, LANES)

        def attend(layer, chunk):
            for head in range(heads):
                keys, values = window(K, head, chunk), window(V, head, chunk)
                scores = mt(keys, Q[head, chunk])
                expo = jnp.exp2(scores * EXP2_SCALE).astype(BF16)
                out = tm(values, expo)
                total = out[HEAD : HEAD + 1, :]
                LSE[layer, head, chunk] = jnp.log(total) * (1.0 / math.log(2.0))
                out = (out * (1.0 / total)).T
                O[head, chunk] = jnp.where(lane < HEAD, out, 0.0).astype(BF16)
            joined = joined_heads([O[head, chunk].astype(F32) for head in range(heads)])
            put_part(chunk, mm(joined, WO[...]))

        def attn_forward(layer, phase):
            def slot(i, carry):
                @pl.when(i < chunks)
                def _():
                    if layer == 0:
                        pack(i)
                    else:
                        x = X1[layer - 1, i] + total_of(phase - 1, i) + rv(layer - 1, 5)
                        X[layer, i] = x
                        hat, _ = norm_rows(x)
                        own = (hat * (1.0 + rv(layer, 0)) + rv(layer, 1)).astype(BF16).astype(F32)
                        open_gather(i % 2, own, A.at[i])
                        close_gather(i % 2, A.at[i])
                    project(layer, i)

                @pl.when(i > 0)
                def _():
                    attend(layer, i - 1)
                    send_part(phase, i - 1)

                return carry

            lax.fori_loop(0, chunks + 1, slot, 0)

        def middle(layer, phase, chunk, target):
            x1 = X[layer, chunk] + total_of(phase - 1, chunk) + rv(layer, 4)
            X1[layer, chunk] = x1
            hat, _ = norm_rows(x1)
            own = (hat * (1.0 + rv(layer, 2)) + rv(layer, 3)).astype(BF16).astype(F32)
            open_gather(chunk % 2, own, target)
            close_gather(chunk % 2, target)

        def up(layer, second):
            before = mm(second, WU[...]) + ub_ref[layer : layer + 1, :]
            cdf = 0.5 * (1.0 + lax.erf(before * math.sqrt(0.5)))
            density = jnp.exp(before * before * -0.5) * (1.0 / math.sqrt(2.0 * math.pi))
            return (before * cdf).astype(BF16), cdf + before * density

        def mlp_forward(layer, phase):
            def slot(i, carry):
                middle(layer, phase, i, C0.at[i])
                act, slope = up(layer, whole(C0, i))
                G0[i] = act
                GP0[i] = slope.astype(BF16)
                put_part(i, mm(act, WD[...]))
                send_part(phase, i)
                return carry

            lax.fori_loop(0, chunks, slot, 0)

        def up_grads(layer, second, grad_before):
            GM[layer, :, :, 0:hidden] += tm(second, grad_before).reshape(n_dp, block, hidden)
            add_vec(layer, UP_BIAS_ROW, column_sum(grad_before.astype(F32)))

        def down_grads(layer, act, grad_out):
            GM[layer, :, :, hidden:] += tm(grad_out, act).reshape(n_dp, block, hidden)

        def pump(name, i):
            for (where, index), events in plan.items():
                if where == name:

                    @pl.when(i == index)
                    def _():
                        for grad_sum, event in events:
                            grad_sum.take(*event)

        def mlp_turn(layer, phase):
            GM[layer] = jnp.zeros((n_dp, block, 2 * hidden), F32)

            def slot(i, carry):
                middle(layer, phase, i, CT.at[0])
                second = whole(CT, 0)
                act, slope = up(layer, second)

                @pl.when(i > 0)
                def _():
                    pltpu.make_async_copy(STAGE.at[0], spill_y.at[i - 1], stage_sem.at[0]).wait()

                STAGE[0] = mm(act, WD[...]).reshape(2, HALF, width)
                pltpu.make_async_copy(STAGE.at[0], spill_y.at[i], stage_sem.at[0]).start()
                grad = INP[pl.ds(i * CHUNK, CHUNK), :].astype(F32) * LIVE[i, :, 0:1]
                CT[1] = grad.astype(BF16).reshape(2, HALF, width)
                own = CT[1, core].astype(F32)
                DX[i] = own
                add_vec(layer, 5, column_sum(own))
                grad = grad.astype(BF16)
                grad_before = (mt(grad, WD[...]) * slope).astype(BF16)
                put_part(i, mt(grad_before, WU[...]))
                up_grads(layer, second, grad_before)
                down_grads(layer, act, grad)
                send_part(phase, i)
                return carry

            lax.fori_loop(0, chunks, slot, 0)
            pltpu.make_async_copy(STAGE.at[0], spill_y.at[chunks - 1], stage_sem.at[0]).wait()

        def input_back(layer, phase, chunk):
            grad_normed = total_of(phase - 1, chunk)
            hat, rstd = norm_rows(X[layer, chunk])
            add_vec(layer, 0, column_sum(grad_normed * hat))
            add_vec(layer, 1, column_sum(grad_normed))
            return DX[chunk] + norm_back(grad_normed * (1.0 + rv(layer, 0)), hat, rstd)

        def mlp_backward(layer, phase, name):
            GM[layer] = jnp.zeros((n_dp, block, 2 * hidden), F32)

            def slot(i, carry):
                grad = input_back(layer + 1, phase, i)
                DX[i] = grad
                own = grad.astype(BF16).astype(F32)
                add_vec(layer, 5, column_sum(own))
                turn = i % 2
                open_gather(turn, own, CT.at[turn])

                @pl.when(i > 0)
                def _():
                    down_grads(layer, G0[i - 1], whole(CT, 1 - turn))

                close_gather(turn, CT.at[turn])
                grad_before = (mt(whole(CT, turn), WD[...]) * GP0[i].astype(F32)).astype(BF16)
                put_part(i, mt(grad_before, WU[...]))
                up_grads(layer, whole(C0, i), grad_before)
                send_part(phase, i)
                pump(name, i)
                return carry

            lax.fori_loop(0, chunks, slot, 0)
            down_grads(layer, G0[chunks - 1], whole(CT, (chunks - 1) % 2))

        def attend_back(layer, chunk):
            grad = whole(CT, chunk % 2)
            grad_heads = [tile.astype(BF16) for tile in apart_heads(mt(grad, WO[...]))]
            ring = chunk % WINDOW
            for head in range(heads):
                grad_o = grad_heads[head]
                query = Q[head, chunk]
                keys, values = window(K, head, chunk), window(V, head, chunk)
                delta = column_sum((O[head, chunk].astype(F32) * grad_o.astype(F32)).T)
                probs = jnp.exp2(mt(keys, query) * EXP2_SCALE - LSE[layer, head, chunk])
                grad_scores = (probs * (mt(values, grad_o) - delta)).astype(BF16)
                grad_v = mm(probs.astype(BF16), grad_o)
                grad_k = mm(grad_scores, query)
                DQ[chunk % 2, head] = tm(grad_scores, keys) * SCALE
                for part in range(WINDOW):
                    place = (ring + part + WINDOW - 1) % WINDOW
                    rows = slice(part * CHUNK, (part + 1) * CHUNK)
                    if part < WINDOW - 1:
                        DV[head, place] += grad_v[rows]
                        DK[head, place] += grad_k[rows]
                    else:
                        DV[head, place] = grad_v[rows]
                        DK[head, place] = grad_k[rows]

        def between_back(layer, chunk):
            out = [O[head, chunk].astype(F32) for head in range(heads)]
            packed = joined_heads([jnp.zeros_like(out[0])] + out)
            grad = whole(CT, chunk % 2)
            GA[layer, :, :, attn_cols - 2 * LANES :] += tm(grad, packed).reshape(n_dp, block, 2 * LANES)
            normed = whole(A, chunk)
            for kind in range(2):
                for head, raw in enumerate(apart_heads(mt(normed, WQ[kind]))):
                    hat, rstd = norm_head(raw + hv(layer, kind, head), real)
                    HATS[kind, head] = jnp.where(lane < HEAD, hat, rstd)

        def project_back(layer, chunk):
            ring, turn = chunk % WINDOW, chunk % 2
            parts = [[], [], []]
            for head in range(heads):
                cols = head * LANES
                for kind, grad in ((0, DQ[turn, head]), (1, DK[head, ring] * SCALE)):
                    both = HATS[kind, head]
                    hat, rstd = both * real, both[:, HEAD : HEAD + 1]
                    gain = (1.0 + hv(layer, 3 + kind, head)) * real
                    inner = norm_head_back(grad * gain, hat, rstd, real)
                    sums = [(HEAD_ROW + kind, inner), (HEAD_ROW + 3 + kind, grad * hat)]
                    if kind == 0:
                        sums.append((HEAD_ROW + 5, grad))
                    for row, values in sums:
                        VEC[layer, row : row + 1, cols : cols + LANES] += column_sum(values)
                    parts[kind].append(inner)
                grad_v = DV[head, ring]
                VEC[layer, HEAD_ROW + 2 : HEAD_ROW + 3, cols : cols + LANES] += column_sum(grad_v)
                parts[2].append(grad_v)
            dense = [joined_heads(tiles) for tiles in parts]
            put_part(chunk, sum(mm(dense[kind], WQ[kind]) for kind in range(3)))
            pairs = [tiles[0] + swap_halves(tiles[1]) for tiles in parts]
            pairs += [parts[0][2] + swap_halves(parts[1][2]), parts[2][2]]
            cols = len(pairs) * LANES
            packed = jnp.concatenate([pair.astype(BF16) for pair in pairs], axis=1)
            GA[layer, :, :, 0:cols] += tm(whole(A, chunk), packed).reshape(n_dp, block, cols)

        def attn_backward(layer, phase, name):
            GA[layer] = jnp.zeros((n_dp, block, attn_cols), F32)
            DK[...] = jnp.zeros_like(DK)
            DV[...] = jnp.zeros_like(DV)

            def slot(i, carry):
                @pl.when(i < chunks)
                def _():
                    grad_second = total_of(phase - 1, i)
                    hat, rstd = norm_rows(X1[layer, i])
                    add_vec(layer, 2, column_sum(grad_second * hat))
                    add_vec(layer, 3, column_sum(grad_second))
                    grad = DX[i] + norm_back(grad_second * (1.0 + rv(layer, 2)), hat, rstd)
                    DX[i] = grad
                    own = grad.astype(BF16).astype(F32)
                    add_vec(layer, 4, column_sum(own))
                    open_gather(i % 2, own, CT.at[i % 2])

                @pl.when(i > 0)
                def _():
                    between_back(layer, i - 1)

                @pl.when(i < chunks)
                def _():
                    close_gather(i % 2, CT.at[i % 2])
                    attend_back(layer, i)

                @pl.when(i > 0)
                def _():
                    project_back(layer, i - 1)
                    send_part(phase, i - 1)

                pump(name, i)
                return carry

            lax.fori_loop(0, chunks + 1, slot, 0)

        near_first = [1, 0] + list(range(2, bits)) if bits > 1 else list(range(bits))

        def mlp_results(layer):
            return [
                pltpu.make_async_copy(GM.at[layer, dp, :, 0:hidden], up_out.at[layer], out_sem.at[layer, 0]),
                pltpu.make_async_copy(GM.at[layer, dp, :, hidden:], down_out.at[layer], out_sem.at[layer, 1]),
            ]

        def attn_results(layer):
            return [
                pltpu.make_async_copy(QKV_STAGE.at[layer], qkv_out.at[layer], out_sem.at[layer, 2]),
                pltpu.make_async_copy(WO_STAGE.at[layer], wo_out.at[layer], out_sem.at[layer, 3]),
            ]

        def finish_mlp(layer):
            start(mlp_results(layer))

        def finish_attn(layer):
            tiles = [GA[layer, dp, :, t * LANES : (t + 1) * LANES] for t in range(attn_cols // LANES)]
            thirds = [tiles[3], swap_halves(tiles[3]), tiles[4]]
            for kind in range(3):
                QKV_STAGE[layer, kind, :, 0:LANES] = tiles[kind]
                QKV_STAGE[layer, kind, :, LANES:channels] = thirds[kind][:, 0 : channels - LANES]
            later = swap_halves(tiles[5])
            WO_STAGE[layer, 0:LANES, :] = jnp.where(lane < HEAD, swap_halves(tiles[4]), later).T
            WO_STAGE[layer, LANES:channels, :] = later.T[0 : channels - LANES]
            start(attn_results(layer))

        low_first = list(range(bits))

        def grad_sum(kind, layer, order, next_order):
            if kind == 0:
                parts = (GM, RM, m_send, m_recv, credit_m, finish_mlp)
            else:
                parts = (GA, RA, a_send, a_recv, credit_a, finish_attn)
            grad, landing, sends, recvs, credit, finish = parts
            return GradSum(
                n_dp, dp, mp, order, grad.at[layer], landing, sends, recvs, credit, next_order,
                lambda _: finish(layer),
            )

        mlp_last = grad_sum(0, last, low_first, low_first)
        attn_last = grad_sum(1, last, low_first, low_first)
        mlp_first = grad_sum(0, 0, low_first, None)
        attn_first = grad_sum(1, 0, low_first, None)
        plan = {}
        spread(mlp_last, [("a1", 1), ("a1", 3), ("m0", 0), ("m0", 0), ("m0", 2), ("m0", 2), ("a0", 0)], plan)
        spread(attn_last, [("m0", 3), ("m0", 3), ("a0", 1), ("a0", 1), ("a0", 1), ("a0", 1), ("a0", 3)], plan)
        spread(mlp_first, [("a0", 2), ("a0", 3), ("end", 1), ("end", 1), ("end", 3), ("end", 3), ("tail", 1)], plan)
        spread(attn_first, [('end', 3), ('tail', 0), ('tail', 1), ('tail', 1), ('tail', 2), ('tail', 2), ('tail', 3)], plan)

        first_loads = [load(patches_in, INP, 4)]
        start(first_loads + load_attn(0) + load_mlp(0))
        VEC[...] = jnp.zeros_like(VEC)
        WQ[:, channels:] = jnp.zeros((3, WQ.shape[1] - channels, width), BF16)
        WO[channels:] = jnp.zeros((WO.shape[0] - channels, width), BF16)
        for row in range(HEAD_VECTORS):
            STAGE[0, 0, 0:layers, 0 : 2 * LANES] = jnp.zeros((layers, 2 * LANES), F32)
            STAGE[0, 0, 0:layers, 0:channels] = hv_ref[row]
            for head, tile in enumerate(apart_heads(STAGE[0, 0, 0:layers, 0 : 2 * LANES])):
                HV[row, :, head * LANES : (head + 1) * LANES] = tile
        keep = jnp.broadcast_to(keep_ref[...].astype(F32), (8, tokens))
        earlier = lax.broadcasted_iota(jnp.int32, (tokens, tokens), 0)
        later = lax.broadcasted_iota(jnp.int32, (tokens, tokens), 1)
        count = mm(keep.astype(BF16), (earlier <= later).astype(F32).astype(BF16))
        place = jnp.where(keep > 0.0, count - 1.0, 2.0 * tokens)
        TROW[...] = place
        TCOL[...] = jnp.broadcast_to(place[0:1, :], (LANES, tokens)).T
        segment = jnp.broadcast_to(seg_ref[...].astype(F32), (LANES, tokens)).T
        QA[...] = (segment.astype(jnp.int32) == lane - HEAD).astype(F32).astype(BF16).reshape(chunks, CHUNK, LANES)
        padding = jnp.broadcast_to((lane == PAD).astype(F32), (CHUNK, LANES)).astype(BF16)
        for head in range(heads):
            for edge in (0, chunks + 1):
                K[head, edge] = padding
                V[head, edge] = jnp.zeros((CHUNK, LANES), BF16)
        wait(first_loads + load_attn(0))
        pl.semaphore_wait(barrier, 2 + bits)

        attn_forward(0, 0)
        cot_load = [load(cot_in, INP, 4)]
        start(spills(False) + load_attn(1) + cot_load)
        wait(load_mlp(0))
        mlp_forward(0, 1)
        wait(spills(False) + load_attn(1))
        start(load_mlp(1))
        attn_forward(1, 2)
        wait(load_mlp(1) + cot_load)
        mlp_turn(1, 3)
        start(load_mlp(0))
        mlp_last.start()
        attn_backward(1, 4, "a1")
        attn_last.start()
        start(spills(True) + load_attn(0))
        wait(load_mlp(0))
        mlp_backward(0, 5, "m0")
        mlp_first.start()
        wait(spills(True) + load_attn(0))
        attn_backward(0, 6, "a0")
        attn_first.start()

        def end_slot(i, carry):
            rows = input_back(0, 7, i)
            reload = pltpu.make_async_copy(spill_y.at[i], PART.at[i], stage_sem.at[0])
            reload.start()
            halves = X.at[:, i]
            open_gather(i % 2, rows, halves)
            reload.wait()
            to_sibling(i).start()
            close_gather(i % 2, halves)
            send_part(7, i)
            pump("end", i)
            return carry

        lax.fori_loop(0, chunks, end_slot, 0)

        def vec_copy(step, target):
            return pltpu.make_async_remote_copy(
                src_ref=VEC,
                dst_ref=VLAND.at[step],
                send_sem=v_send.at[step],
                recv_sem=v_recv.at[step],
                device_id=target,
                device_id_type=MESH,
            )

        def unpack(patch_chunk, stage):
            stage[...] = jnp.zeros(stage.shape, F32)
            place = TCOL[pl.ds(patch_chunk * CHUNK, CHUNK), 0:1].astype(jnp.int32)

            def add_slots(chunk, carry):
                slot = lax.broadcasted_iota(jnp.int32, (CHUNK, CHUNK), 1) + chunk * CHUNK
                chosen = (place == slot).astype(F32).astype(BF16)
                rest = jnp.concatenate([X[0, chunk], X[1, chunk]], axis=0)
                for _ in range(3):
                    piece = rest.astype(BF16)
                    stage[...] += mm(chosen, piece).reshape(stage.shape)
                    rest = rest - piece.astype(F32)
                return carry

            lax.fori_loop(0, patch_chunk + 1, add_slots, 0)

        def patch_copy(patch_chunk, turn):
            return pltpu.make_async_copy(STAGE.at[turn], gpatch_out.at[patch_chunk], stage_sem.at[turn])

        def out_copy(chunk):
            return pltpu.make_async_copy(A.at[chunk], packed_out.at[chunk], spill_sem.at[chunk])

        def chosen_part(values, share):
            column = lax.broadcasted_iota(jnp.int32, (values.shape[1], LANES), 0)
            wanted = lax.broadcasted_iota(jnp.int32, (values.shape[1], LANES), 1)
            chosen = ((column == wanted + dp * share) & (wanted < share)).astype(F32).astype(BF16)
            total, rest = 0.0, values
            for _ in range(3):
                piece = rest.astype(BF16)
                total = total + mm(piece, chosen)
                rest = rest - piece.astype(F32)
            return total[:, 0:share]

        def vec_results():
            for layer in range(layers):
                rows = chosen_part(VEC[layer, 0:UP_BIAS_ROW, :], block)
                for row in range(ROW_VECTORS):
                    row_out[row, layer : layer + 1, :] = rows[row : row + 1]
                rows = chosen_part(VEC[layer, UP_BIAS_ROW : 2 * UP_BIAS_ROW, 0:hidden], hidden // n_dp)
                bias_out[layer : layer + 1, :] = rows[0:1]
                heads_joined = [
                    VEC[layer, UP_BIAS_ROW : 2 * UP_BIAS_ROW, head * LANES : (head + 1) * LANES] * real for head in range(heads)
                ]
                heads_joined = jnp.concatenate(
                    [heads_joined[0] + swap_halves(heads_joined[1]), heads_joined[2]], axis=1
                )
                rows = chosen_part(heads_joined, channels // n_dp)
                for row in range(HEAD_VECTORS):
                    place = HEAD_ROW - UP_BIAS_ROW + row
                    head_out[row, layer : layer + 1, :] = rows[place : place + 1]

        def vec_partner(step):
            return (dp, sibling) if step == 0 else (flipped(dp, [step - 1]), mp)

        def vec_step(step):
            vec_copy(step, vec_partner(step)).wait()
            if step == 0:
                VEC[:, 0:UP_BIAS_ROW, :] += VLAND[0, :, 0:UP_BIAS_ROW, :]
            else:
                VEC[...] += VLAND[step]
            if step < bits:
                vec_copy(step + 1, vec_partner(step + 1)).start()
            else:
                vec_results()

        def unpack_next(step):
            turn = step % 2
            if step >= 2:
                patch_copy(step - 2, turn).wait()
            unpack(step, STAGE.at[turn])
            patch_copy(step, turn).start()

        vec_copy(0, vec_partner(0)).start()
        unpack_next(0)
        for step in range(chunks):
            if step <= bits:
                vec_step(step)
            for job, event in plan.get(("tail", step), []):
                job.take(*event)
            rows = (X1[last, step] + total_of(7, step) + rv(last, 5)) * LIVE[step, pl.ds(core * HALF, HALF), 0:1]
            open_gather(step % 2, rows.astype(BF16).astype(F32), A.at[step])
            if step + 1 < chunks:
                unpack_next(step + 1)
            close_gather(step % 2, A.at[step])
            out_copy(step).start()
        for step in range(chunks, bits + 1):
            vec_step(step)

        for step in range(max(0, chunks - 2), chunks):
            patch_copy(step, step % 2).wait()
        for step in range(chunks):
            out_copy(step).wait()
        for job in (mlp_last, attn_last, mlp_first, attn_first):
            assert job.taken == job.counts
        for layer in range(layers):
            wait(mlp_results(layer) + attn_results(layer))

    return kernel


def body(n_dp, patches, patch_keep, patch_segment, cotangent, w_qkv, w_out, w_up, w_down, head_vectors, up_bias, row_vectors):
    tokens, width = patches.shape
    layers = w_qkv.shape[0]
    channels = w_qkv.shape[3]
    heads = channels // HEAD
    hidden = w_up.shape[2]
    chunks = tokens // CHUNK
    slots = heads * LANES
    bits = n_dp.bit_length() - 1
    block = width // n_dp
    attn_cols = 4 * channels

    channels_up = (heads + 1) // 2 * LANES
    wq = jnp.transpose(w_qkv, (0, 1, 3, 2))
    hv = jnp.transpose(head_vectors, (1, 0, 2))
    rv = jnp.transpose(row_vectors, (1, 0, 2))
    any_space = pl.BlockSpec(memory_space=pl.ANY)
    vmem = pl.BlockSpec(memory_space=pltpu.VMEM)
    sds = jax.ShapeDtypeStruct
    half = (HALF, width)
    head_chunks = (heads, chunks, CHUNK, LANES)
    head_window = (heads, chunks + 2, CHUNK, LANES)
    out_shape = [
        sds((chunks, 2) + half, BF16),
        sds((chunks, 2) + half, F32),
        sds((layers, 3, block, channels), F32),
        sds((layers, channels, block), F32),
        sds((layers, block, hidden), F32),
        sds((layers, block, hidden), F32),
        sds((HEAD_VECTORS, layers, channels // n_dp), F32),
        sds((layers, hidden // n_dp), F32),
        sds((ROW_VECTORS, layers, block), F32),
        sds(head_chunks, BF16),
        sds(head_window, BF16),
        sds(head_window, BF16),
        sds(head_chunks, BF16),
        sds((chunks, 2) + half, BF16),
        sds((chunks, 2) + half, F32),
    ]
    v = pltpu.VMEM
    dma = pltpu.SemaphoreType.DMA
    scratch = [
        v((tokens, width), BF16),
        v((3, channels_up, width), BF16),
        v((channels_up, width), BF16),
        v((width, hidden), BF16),
        v((hidden, width), BF16),
        v((layers, chunks) + half, F32),
        v((layers, chunks) + half, F32),
        v((chunks, 2) + half, BF16),
        v((chunks, 2) + half, BF16),
        v((2, 2) + half, BF16),
        v(head_chunks, BF16),
        v(head_window, BF16),
        v(head_window, BF16),
        v(head_chunks, BF16),
        v((layers, heads, chunks, 1, CHUNK), F32),
        v((HEAD_VECTORS, layers, slots), F32),
        v((chunks, CHUNK, hidden), BF16),
        v((chunks, CHUNK, hidden), BF16),
        v((chunks, CHUNK, LANES), BF16),
        v((chunks, CHUNK, LANES), BF16),
        v((chunks, CHUNK, LANES), F32),
        v((8, tokens), F32),
        v((tokens, LANES), F32),
        v((chunks, 2) + half, F32),
        v((2,) + half, F32),
        v((2, chunks) + half, F32),
        v((2,) + half, F32),
        v(half, F32),
        v((chunks,) + half, F32),
        v((2, heads, CHUNK, LANES), F32),
        v((2, heads, CHUNK, LANES), F32),
        v((heads, WINDOW, CHUNK, LANES), F32),
        v((heads, WINDOW, CHUNK, LANES), F32),
        v((layers, n_dp, block, 2 * hidden), F32),
        v((layers, n_dp, block, attn_cols), F32),
        v((n_dp - 1, block, 2 * hidden), F32),
        v((n_dp - 1, block, attn_cols), F32),
        v((layers, VEC_ROWS, width), F32),
        v((bits + 1, layers, VEC_ROWS, width), F32),
        v((2, 2) + half, F32),
        v((layers, 3, block, channels), F32),
        v((layers, channels, block), F32),
        dma((5,)),
        dma((5,)),
        dma((2,)),
        dma((2,)),
        dma((2,)),
        dma((2, chunks)),
        dma((2, chunks)),
        dma((2,)),
        dma((2,)),
        dma((n_dp - 1,)),
        dma((n_dp - 1,)),
        dma((n_dp - 1,)),
        dma((n_dp - 1,)),
        pltpu.SemaphoreType.REGULAR((bits,)),
        pltpu.SemaphoreType.REGULAR((bits,)),
        dma((bits + 1,)),
        dma((bits + 1,)),
        dma((layers, 4)),
    ]
    results = pl.pallas_call(
        make_kernel(n_dp, tokens, width, hidden, heads, layers),
        out_shape=out_shape,
        in_specs=[vmem] * 5 + [any_space] * 6,
        out_specs=[any_space] * 6 + [vmem] * 3 + [any_space] * (len(out_shape) - 9),
        scratch_shapes=scratch,
        compiler_params=pltpu.CompilerParams(
            collective_id=0, has_side_effects=True, vmem_limit_bytes=64 * 2**20 - 2**16
        ),
    )(patch_keep, patch_segment, hv, up_bias, rv, patches, cotangent, wq, w_out, w_up, w_down)
    packed, grad_patches, grad_qkv, grad_out, grad_up, grad_down, head_grads, bias_grads, row_grads = results[:9]
    return (
        packed.reshape(tokens, width),
        grad_patches.reshape(tokens, width),
        grad_qkv,
        grad_out,
        grad_up,
        jnp.transpose(grad_down, (0, 2, 1)),
        jnp.transpose(head_grads, (1, 0, 2)),
        bias_grads,
        jnp.transpose(row_grads, (1, 0, 2)),
    )


def solution(mesh):
    n_dp = mesh.shape["dp"]

    def step(*args):
        return body(n_dp, *args)

    return jax.shard_map(
        step,
        mesh=mesh,
        in_specs=(
            P("dp", None),
            P("dp", None),
            P("dp", None),
            P("dp", None),
            P(None, None, None, "mp"),
            P(None, "mp", None),
            P(None, None, "mp"),
            P(None, "mp", None),
            P(None, None, "mp"),
            P(None, "mp"),
            P(),
        ),
        out_specs=(
            P("dp", None),
            P("dp", None),
            P(None, None, "dp", "mp"),
            P(None, "mp", "dp"),
            P(None, "dp", "mp"),
            P(None, "mp", "dp"),
            P(None, None, ("mp", "dp")),
            P(None, ("mp", "dp")),
            P(None, None, "dp"),
        ),
        check_vma=False,
    )
```

```python
import math

import jax
import jax.numpy as jnp
from jax import lax
from jax.experimental import pallas as pl
from jax.experimental.pallas import tpu as pltpu
from jax.sharding import PartitionSpec as P

MESH = pl.DeviceIdType.MESH
F32, BF16 = jnp.float32, jnp.bfloat16
HEAD = 64
LANES = 128
EPS = 1e-6
SCALE = HEAD**-0.5
EXP2_SCALE = SCALE / math.log(2.0)
CHUNK = 256
HALF = CHUNK // 2
WINDOW = 3
IMAGES = 8
EMPTY = HEAD + IMAGES
PAD = EMPTY + 1
APART = 2048.0
ROW_VECTORS, HEAD_VECTORS = 6, 6
UP_BIAS_ROW, HEAD_ROW, VEC_ROWS = 8, 9, 16


def mm(left, right):
    return jnp.dot(left, right, preferred_element_type=F32)


def mt(left, right):
    return lax.dot_general(left, right, (((1,), (1,)), ((), ())), preferred_element_type=F32)


def tm(left, right):
    return lax.dot_general(left, right, (((0,), (0,)), ((), ())), preferred_element_type=F32)


def norm_rows(values):
    center = values - jnp.mean(values, axis=-1, keepdims=True)
    rstd = lax.rsqrt(jnp.mean(center * center, axis=-1, keepdims=True) + EPS)
    return center * rstd, rstd


def norm_back(grad, hat, rstd):
    mean_grad = jnp.mean(grad, axis=-1, keepdims=True)
    mean_cross = jnp.mean(grad * hat, axis=-1, keepdims=True)
    return rstd * (grad - mean_grad - hat * mean_cross)


def pieces(values, count):
    found, rest = [], values
    for _ in range(count):
        found.append(rest.astype(BF16))
        rest = rest - found[-1].astype(F32)
    return found


def mm_exact(values, right, count):
    return sum(mm(piece, right) for piece in pieces(values, count))


def column_sum(values):
    return jnp.sum(values, axis=0, keepdims=True)


def bit_of(index, bit):
    return (index // (1 << bit)) % 2


def flipped(index, bits):
    for bit in bits:
        index = index + (1 << bit) * (1 - 2 * bit_of(index, bit))
    return index


class GradSum:
    def __init__(self, n_dp, me, mp, order, grad, landing, send_sem, recv_sem, credit, next_order, finish):
        self.me, self.mp, self.order = me, mp, order
        self.steps = len(order)
        self.counts = [n_dp >> (k + 1) for k in range(self.steps)]
        self.offsets = [sum(self.counts[:k]) for k in range(self.steps)]
        self.grad, self.landing = grad, landing
        self.send_sem, self.recv_sem, self.credit = send_sem, recv_sem, credit
        self.next_order, self.finish = next_order, finish
        self.after, self.taken = {}, set()

    def turn(self, k):
        return sorted(range(self.counts[k]), key=lambda m: (m % 2 == 0, -m))

    def events(self):
        return [(k, m) for k in range(self.steps) for m in self.turn(k)]

    def later_bits(self, k, m):
        return [self.order[k + 1 + t] for t in range(self.steps - k - 1) if (m >> t) & 1]

    def partner(self, k, order=None):
        return (flipped(self.me, [(order or self.order)[k]]), self.mp)

    def copy(self, k, m):
        slot = self.offsets[k] + m
        block = flipped(self.me, [self.order[k]] + self.later_bits(k, m))
        return pltpu.make_async_remote_copy(
            src_ref=self.grad.at[block],
            dst_ref=self.landing.at[slot],
            send_sem=self.send_sem.at[slot],
            recv_sem=self.recv_sem.at[slot],
            device_id=self.partner(k),
            device_id_type=MESH,
        )

    def prepare(self, events):
        taken, sent = set(), set()
        for event in events:
            taken.add(event)
            sends = []
            for step in range(1, self.steps):
                for index in self.turn(step):
                    before = {(j, 1 << (step - 1 - j) | index << (step - j)) for j in range(step)}
                    if (step, index) not in sent and before <= taken:
                        first = all(step != other for other, _ in sent)
                        sends.append((step, index, first))
                        sent.add((step, index))
            k = event[0]
            freed = sum(step == k for step, _ in taken) == self.counts[k]
            self.after[event] = (sends, freed, len(taken) == sum(self.counts))

    def send(self, k, m, first):
        if first and self.next_order is None:
            pl.semaphore_wait(self.credit.at[k], 1)
        self.copy(k, m).start()

    def start(self):
        for position, m in enumerate(self.turn(0)):
            self.send(0, m, position == 0)

    def take(self, k, m):
        sends, freed, done = self.after[k, m]
        self.copy(k, m).wait()
        block = flipped(self.me, self.later_bits(k, m))
        self.grad[block] += self.landing[self.offsets[k] + m]
        self.taken.add((k, m))
        for step, index, first in sends:
            self.send(step, index, first)
        if self.next_order is not None and freed:
            target = self.partner(k, self.next_order)
            pl.semaphore_signal(self.credit.at[k], inc=1, device_id=target, device_id_type=MESH)
        if done:
            self.finish()


TAKEN = {
    (0, 1): [(("a1m", 1), (0, 3)), (("a1m", 2), (0, 1)), (("a1", 2), (0, 2)), (("a1", 3), (0, 0)), (("m0", 0), (1, 1)), (("m0", 2), (1, 0)), (("a0m", 0), (2, 0))],
    (1, 1): [(("a1m", 1), (0, 3)), (("a1m", 2), (0, 1)), (("a1", 2), (0, 2)), (("a1", 3), (0, 0)), (("m0", 0), (1, 1)), (("m0", 2), (1, 0)), (("a0m", 1), (2, 0))],
    (2, 1): [(("m0", 3), (0, 3)), (("a0m", 0), (0, 1)), (("a0", 0), (0, 2)), (("a0", 0), (1, 1)), (("a0m", 1), (0, 0)), (("a0", 4), (1, 0)), (("end", 2), (2, 0))],
    (0, 0): [(("a0m", 2), (0, 3)), (("a0m", 3), (0, 1)), (("a0", 3), (0, 2)), (("a0", 4), (0, 0)), (("end", 2), (1, 1)), (("end", 3), (1, 0)), (("tail", 3), (2, 0))],
    (1, 0): [(("a0m", 1), (0, 3)), (("a0m", 2), (0, 1)), (("a0m", 3), (0, 2)), (("a0", 3), (0, 0)), (("end", 1), (1, 1)), (("end", 2), (1, 0)), (("tail", 1), (2, 0))],
    (2, 0): [(("end", 3), (0, 3)), (("end", 3), (0, 1)), (("tail", 1), (0, 2)), (("tail", 2), (0, 0)), (("tail", 2), (1, 1)), (("tail", 3), (1, 0)), (("tail", 4), (2, 0))],
}
PHASES = ["a1", "m0", "a0", "end", "tail"]
NEAR_FIRST = {(0, 1): 0, (1, 1): 1, (2, 1): 0, (0, 0): 0, (1, 0): 1, (2, 0): 0}
SPREAD = {
    (0, 1): [("a1", 2), ("a1", 3), ("a1", 4), ("m0", 0), ("m0", 1), ("m0", 2), ("m0", 3)],
    (1, 1): [("a1", 2), ("a1", 3), ("a1", 4), ("m0", 0), ("m0", 1), ("m0", 2), ("m0", 3)],
    (2, 1): [("m0", 2), ("m0", 3), ("a0", 0), ("a0", 1), ("a0", 2)],
    (0, 0): [("a0", 2), ("a0", 3), ("a0", 4), ("end", 0), ("end", 1), ("end", 2), ("end", 3), ("tail", 0)],
    (1, 0): [("a0", 2), ("a0", 3), ("a0", 4), ("end", 0), ("end", 1), ("end", 2), ("end", 3), ("tail", 0)],
    (2, 0): [("end", 2), ("end", 3), ("tail", 0), ("tail", 1), ("tail", 2), ("tail", 3), ("tail", 4)],
}


def comes_at(place):
    phase, slot = place
    return (PHASES.index(phase.removesuffix("m")), slot, not phase.endswith("m"))


def plan_sums(sums, last):
    plan = {}
    for (kind, layer), job in sums.items():
        events, which = job.events(), (kind, int(layer == last))
        taken = TAKEN[which]
        if len(taken) != len(events):
            places = SPREAD[which]
            taken = [(places[n * len(places) // len(events)], event) for n, event in enumerate(events)]
        taken = sorted(taken, key=lambda entry: comes_at(entry[0]))
        job.prepare([event for _, event in taken])
        for place, event in taken:
            plan.setdefault(place, []).append((job, event))
    return plan


def make_kernel(n_dp, tokens, width, hidden, heads, layers):
    chunks = tokens // CHUNK
    bits = n_dp.bit_length() - 1
    block = width // n_dp
    channels = heads * HEAD
    attn_cols = 4 * channels
    last = layers - 1

    def kernel(
        keep_ref,
        seg_ref,
        hv_ref,
        ub_ref,
        rv_ref,
        patches_in,
        cot_in,
        wq_in,
        wo_in,
        wu_in,
        wd_in,
        packed_out,
        gpatch_out,
        qkv_out,
        wo_out,
        up_out,
        down_out,
        head_out,
        bias_out,
        row_out,
        spill_q,
        spill_k,
        spill_v,
        spill_o,
        spill_a,
        spill_y,
        INP,
        WQ,
        WO,
        WU,
        WD,
        X,
        X1,
        A,
        C0,
        CT,
        Q,
        K,
        V,
        O,
        LSE,
        HV,
        BLOCKS,
        G0,
        GP0,
        QA,
        KA,
        LIVE,
        TROW,
        TCOL,
        PART,
        DBUF,
        YBUF,
        CBUF,
        CSEND,
        DX,
        WOB,
        OD,
        DQ,
        HATS,
        DK,
        DV,
        GU,
        GD,
        GA,
        RU,
        RD,
        RA,
        VEC,
        VLAND,
        STAGE,
        QKV_STAGE,
        WO_STAGE,
        load_sem,
        spill_sem,
        stage_sem,
        d_send,
        d_recv,
        y_send,
        y_recv,
        c_send,
        c_recv,
        o_send,
        o_recv,
        w_send,
        w_recv,
        g_send,
        g_recv,
        credit,
        v_send,
        v_recv,
        out_sem,
    ):
        dp = lax.axis_index("dp")
        mp = lax.axis_index("mp")
        core = mp % 2
        sibling = mp + 1 - 2 * core
        across = (mp + 2) % 4
        diagonal = (sibling + 2) % 4

        barrier = pltpu.get_barrier_semaphore()
        for other in (sibling, across, diagonal):
            pl.semaphore_signal(barrier, inc=1, device_id=(dp, other), device_id_type=MESH)
        for flips in [[bit] for bit in range(bits)] + [[0, 1]]:
            pl.semaphore_signal(barrier, inc=1, device_id=(flipped(dp, flips), mp), device_id_type=MESH)

        lane = lax.broadcasted_iota(jnp.int32, (1, LANES), 1)
        real = (lane < HEAD).astype(F32)

        def load(source, target, index):
            return pltpu.make_async_copy(source, target, load_sem.at[index])

        def load_wq(layer):
            return load(wq_in.at[layer], WQ.at[:, 0:channels], 0)

        def load_wo(layer):
            return load(wo_in.at[layer], WO.at[0:channels], 1)

        def load_mlp(layer):
            return [load(wu_in.at[layer], WU, 2), load(wd_in.at[layer], WD, 3)]

        def spills(back):
            pairs = [(Q, spill_q), (K, spill_k), (V, spill_v), (O, spill_o), (A, spill_a)]
            return [
                pltpu.make_async_copy(*((far, near) if back else (near, far)), spill_sem.at[index])
                for index, (near, far) in enumerate(pairs)
            ]

        def start(copies):
            for copy in copies:
                copy.start()

        def wait(copies):
            for copy in copies:
                copy.wait()

        def to_sibling(chunk):
            slot = chunk % 2
            return pltpu.make_async_remote_copy(
                src_ref=PART.at[chunk, 1 - core],
                dst_ref=DBUF.at[slot],
                send_sem=d_send.at[slot],
                recv_sem=d_recv.at[slot],
                device_id=(dp, sibling),
                device_id_type=MESH,
            )

        def to_across(phase, chunk):
            slot = phase % 2
            return pltpu.make_async_remote_copy(
                src_ref=PART.at[chunk, core],
                dst_ref=YBUF.at[slot, chunk],
                send_sem=y_send.at[slot, chunk],
                recv_sem=y_recv.at[slot, chunk],
                device_id=(dp, across),
                device_id_type=MESH,
            )

        def to_gather(turn):
            return pltpu.make_async_remote_copy(
                src_ref=CSEND,
                dst_ref=CBUF.at[turn],
                send_sem=c_send.at[turn],
                recv_sem=c_recv.at[turn],
                device_id=(dp, sibling),
                device_id_type=MESH,
            )

        def put_part(chunk, values):
            PART[chunk] = values.reshape(2, HALF, width)
            to_sibling(chunk).start()

        def send_part(phase, chunk):
            to_sibling(chunk).wait()
            PART[chunk, core] += DBUF[chunk % 2]
            to_across(phase, chunk).start()

        def total_of(phase, chunk):
            to_across(phase, chunk).wait()
            return PART[chunk, core] + YBUF[phase % 2, chunk]

        def open_gather(turn, own, target):
            CSEND[...] = own
            to_gather(turn).start()
            target[core] = own.astype(target.dtype)

        def close_gather(turn, target):
            to_gather(turn).wait()
            target[1 - core] = CBUF[turn].astype(target.dtype)

        def whole(ref, chunk):
            return ref[chunk].reshape(CHUNK, width)

        def add_vec(layer, row, values):
            VEC[layer, row : row + 1, 0 : values.shape[1]] += values

        def rv(layer, row):
            return rv_ref[row, layer : layer + 1, :]

        def hv(layer, row):
            return HV[row, layer : layer + 1, :]

        def norm_heads(values):
            center = values - mm_exact(values, BLOCKS[...], 3)
            rstd = lax.rsqrt(mm_exact(center * center, BLOCKS[...], 2) + EPS)
            return center * rstd, rstd

        def norm_heads_back(grad, hat, rstd):
            mean_grad = mm_exact(grad, BLOCKS[...], 2)
            mean_cross = mm_exact(grad * hat, BLOCKS[...], 2)
            return rstd * (grad - mean_grad - hat * mean_cross)

        def swap_halves(tile):
            return pltpu.roll(tile, HEAD, 1)

        def apart_heads(values):
            tiles = []
            for head in range(heads):
                tile = values[:, head // 2 * LANES : (head // 2 + 1) * LANES]
                tiles.append((swap_halves(tile) if head % 2 else tile) * real)
            return tiles

        def joined_heads(tiles):
            pairs = [
                tiles[first] + swap_halves(tiles[first + 1]) if first + 1 < len(tiles) else tiles[first]
                for first in range(0, len(tiles), 2)
            ]
            return jnp.concatenate(pairs, axis=1)

        def pack(chunk):
            rows = lax.broadcasted_iota(jnp.int32, (CHUNK, tokens), 0) + chunk * CHUNK
            chosen = (TROW[0:1, :].astype(jnp.int32) == rows).astype(F32).astype(BF16)
            values = mm(chosen, INP[...])
            classes = mm(chosen, QA[...].reshape(tokens, LANES))
            alive = jnp.sum(classes, axis=-1, keepdims=True)
            LIVE[chunk] = jnp.broadcast_to(alive, (CHUNK, LANES))
            KA[chunk] = (classes + jnp.where(lane == EMPTY, 1.0 - alive, 0.0)).astype(BF16)
            PART[chunk] = values.reshape(2, HALF, width)
            X[0, chunk] = PART[chunk, core]
            hat, _ = norm_rows(values)
            A[chunk] = (hat * (1.0 + rv(0, 0)) + rv(0, 1)).astype(BF16).reshape(2, HALF, width)

        def apart_of(chunk):
            is_class = (lane >= HEAD) & (lane <= PAD)
            return jnp.where(is_class, -APART * (1.0 - KA[chunk].astype(F32)), 0.0)

        def project(layer, chunk):
            normed = whole(A, chunk)
            apart = apart_of(chunk).astype(BF16)
            classes = KA[chunk]
            ones = (lane == HEAD).astype(F32)
            hat, _ = norm_heads(mt(normed, WQ[0]) + hv(layer, 0))
            for head, tile in enumerate(apart_heads(hat * (1.0 + hv(layer, 3)) + hv(layer, 5))):
                Q[head, chunk] = tile.astype(BF16) + apart
            hat, _ = norm_heads(mt(normed, WQ[1]) + hv(layer, 1))
            for head, tile in enumerate(apart_heads(hat * (1.0 + hv(layer, 4)))):
                K[head, chunk + 1] = tile.astype(BF16) + classes
            for head, tile in enumerate(apart_heads(mt(normed, WQ[2]) + hv(layer, 2))):
                V[head, chunk + 1] = (tile + ones).astype(BF16)

        def window(ref, head, chunk):
            return ref[head, pl.ds(chunk, WINDOW)].reshape(WINDOW * CHUNK, LANES)

        def dq_rows(turn, head):
            return pl.ds(pl.multiple_of((turn * heads + head) * CHUNK, CHUNK), CHUNK)

        def dk_rows(head, place):
            return pl.ds(pl.multiple_of((head * WINDOW + place) * CHUNK, CHUNK), CHUNK)

        def sent_at(chunk, half):
            return pl.multiple_of((chunk * 2 + half) * channels, HEAD)

        def landed_at(source, chunk):
            return pl.multiple_of((source * chunks + chunk) * channels, HEAD)

        def o_copies(chunk):
            return [
                pltpu.make_async_remote_copy(
                    src_ref=DQ.at[pl.ds(sent_at(chunk, half), channels)],
                    dst_ref=DK.at[pl.ds(landed_at(source, chunk), channels)],
                    send_sem=o_send.at[source, chunk],
                    recv_sem=o_recv.at[source, chunk],
                    device_id=(dp, other),
                    device_id_type=MESH,
                )
                for source, (other, half) in enumerate(((sibling, 1 - core), (across, core), (diagonal, 1 - core)))
            ]

        def attend(layer, chunk):
            outs = []
            for head in range(heads):
                keys, values = window(K, head, chunk), window(V, head, chunk)
                scores = mt(keys, Q[head, chunk])
                expo = jnp.exp2(scores * EXP2_SCALE).astype(BF16)
                out = tm(values, expo)
                total = out[HEAD : HEAD + 1, :]
                LSE[layer, head, chunk] = jnp.log(total) * (1.0 / math.log(2.0))
                out = (out * (1.0 / total)).T
                out = jnp.where(lane < HEAD, out, 0.0).astype(BF16)
                O[head, chunk] = out
                outs.append(out.astype(F32))
            pair, third = outs[0] + swap_halves(outs[1]), outs[2]
            for half in range(2):
                first, row = sent_at(chunk, half), half * HALF
                DQ[pl.ds(first, HALF)] = pair[row : row + HALF]
                DQ[pl.ds(first + HALF, HALF // 2)] = third[row : row + HALF // 2] + swap_halves(
                    third[row + HALF // 2 : row + HALF]
                )
            start(o_copies(chunk))

        share = n_dp // 4

        quarter_of = bit_of(dp, 0) + 2 * bit_of(dp, 1)
        near = [[0], [1], [0, 1]]

        def w_quarter(layer, holder, quarter):
            if share >= 4:
                return GA.at[layer, pl.ds(holder * share + quarter * (share // 4), share // 4)]
            per = 4 // share
            rows = pl.ds(pl.multiple_of(quarter % per * (block // per), 8), block // per)
            return GA.at[layer, pl.ds(holder * share + quarter // per, 1), rows]

        def w_copy(layer, step):
            holder, target = (mp if step < 2 else across), (dp, sibling)
            if step == 0:
                target = (dp, across)
            elif 2 <= step < 5:
                target = (flipped(dp, near[step - 2]), mp)
            if step in (1, 5):
                part = GA.at[layer, pl.ds(holder * share, share)]
            else:
                part = w_quarter(layer, holder, quarter_of)
            return pltpu.make_async_remote_copy(
                src_ref=part,
                dst_ref=part,
                send_sem=w_send.at[layer, step],
                recv_sem=w_recv.at[layer, step],
                device_id=target,
                device_id_type=MESH,
            )

        def open_w(layer):
            GA[layer, pl.ds(mp * share, share)] = WO[0:channels].astype(F32).reshape(share, block, width)
            w_copy(layer, 0).start()
            w_copy(layer, 1).start()

        def spread_w(layer):
            w_copy(layer, 0).wait()
            start([w_copy(layer, step) for step in (2, 3, 4)])

        def forward_w(layer):
            wait([w_copy(layer, step) for step in (1, 2, 3, 4)])
            w_copy(layer, 5).start()

        def close_w(layer):
            w_copy(layer, 5).wait()
            for holder in range(4):
                rows = GA[layer, holder * share : (holder + 1) * share].reshape(channels, width).astype(BF16)
                WOB[holder * LANES : (holder + 1) * LANES] = rows[0:LANES]
                WOB[4 * LANES + holder * HEAD : 4 * LANES + (holder + 1) * HEAD] = rows[LANES:channels]

        def attn_out(chunk):
            wait(o_copies(chunk))
            places = [(DQ, sent_at(chunk, core))] + [(DK, landed_at(source, chunk)) for source in range(3)]
            thirds = []
            for holder, (ref, first) in zip((mp, sibling, across, diagonal), places):
                OD[holder] = ref[pl.ds(first, HALF)].astype(BF16)
                both = ref[pl.ds(first + HALF, HALF // 2)]
                thirds.append(jnp.concatenate([both * real, swap_halves(both) * real], axis=0))
            chip = mp // 2
            for place, (same, other) in ((chip, thirds[:2]), (1 - chip, thirds[2:])):
                low, high = jnp.where(core == 0, same, other), jnp.where(core == 0, other, same)
                OD[4 + place] = (low + swap_halves(high)).astype(BF16)
            return mm(jnp.concatenate([OD[tile] for tile in range(6)], axis=1), WOB[...])

        def open_middle(layer, chunk, turn, target):
            x1 = X[layer, chunk] + attn_out(chunk) + rv(layer, 4)
            X1[layer, chunk] = x1
            hat, _ = norm_rows(x1)
            own = (hat * (1.0 + rv(layer, 2)) + rv(layer, 3)).astype(BF16).astype(F32)
            open_gather(turn, own, target)

        def up(layer, second):
            before = mm(second, WU[...]) + ub_ref[layer : layer + 1, :]
            cdf = 0.5 * (1.0 + lax.erf(before * math.sqrt(0.5)))
            density = jnp.exp(before * before * -0.5) * (1.0 / math.sqrt(2.0 * math.pi))
            return (before * cdf).astype(BF16), cdf + before * density

        def forward_first():
            def slot(i, carry):
                @pl.when(i == 1)
                def _():
                    spread_w(0)

                @pl.when(i < chunks)
                def _():
                    pack(i)
                    project(0, i)

                @pl.when((i > 0) & (i <= chunks))
                def _():
                    attend(0, i - 1)

                @pl.when(i == 2)
                def _():
                    forward_w(0)
                    wait(load_mlp(0))
                    close_w(0)

                @pl.when(i == chunks)
                def _():
                    load_wo(last).wait()
                    open_w(last)
                    start([load_wq(last)] + cot_load)

                @pl.when(i > chunks)
                def _():
                    start(spills(False))
                    spread_w(last)

                @pl.when(i >= 2)
                def _():
                    j = i - 2
                    turn = j % 2
                    open_middle(0, j, turn, C0.at[j])
                    close_gather(turn, C0.at[j])
                    act, slope = up(0, whole(C0, j))
                    G0[j] = act
                    GP0[j] = slope.astype(BF16)
                    put_part(j, mm(act, WD[...]))
                    send_part(0, j)

                return carry

            lax.fori_loop(0, chunks + 2, slot, 0)

        def up_grads(layer, second, grad_before):
            GU[layer] += tm(second, grad_before).reshape(n_dp, block, hidden)
            add_vec(layer, UP_BIAS_ROW, column_sum(grad_before.astype(F32)))

        def down_grads(layer, act, grad_out):
            GD[layer] += tm(grad_out, act).reshape(n_dp, block, hidden)

        def pump(name, i):
            for (where, index), events in plan.items():
                if where == name:

                    @pl.when(i == index)
                    def _():
                        for grad_sum, event in events:
                            grad_sum.take(*event)

        def mlp_turn(layer, phase, chunk):
            second = whole(CT, 0)
            act, slope = up(layer, second)

            @pl.when(chunk > 0)
            def _():
                pltpu.make_async_copy(STAGE.at[0], spill_y.at[chunk - 1], stage_sem.at[0]).wait()

            STAGE[0] = mm(act, WD[...]).reshape(2, HALF, width)
            pltpu.make_async_copy(STAGE.at[0], spill_y.at[chunk], stage_sem.at[0]).start()
            grad = INP[pl.ds(chunk * CHUNK, CHUNK), :].astype(F32) * LIVE[chunk, :, 0:1]
            CT[1] = grad.astype(BF16).reshape(2, HALF, width)
            own = CT[1, core].astype(F32)
            DX[chunk] = own
            add_vec(layer, 5, column_sum(own))
            grad = grad.astype(BF16)
            grad_before = (mt(grad, WD[...]) * slope).astype(BF16)
            put_part(chunk, mt(grad_before, WU[...]))
            up_grads(layer, second, grad_before)
            down_grads(layer, act, grad)
            send_part(phase, chunk)

        def forward_last():
            GU[last] = jnp.zeros((n_dp, block, hidden), F32)
            GD[last] = jnp.zeros((n_dp, block, hidden), F32)

            def slot(i, carry):
                j = i - 2
                turn = 1 - (j // 2) * (1 - j % 2)

                @pl.when(i < chunks)
                def _():
                    x = X1[last - 1, i] + total_of(0, i) + rv(last - 1, 5)
                    X[last, i] = x
                    hat, _ = norm_rows(x)
                    own = (hat * (1.0 + rv(last, 0)) + rv(last, 1)).astype(BF16).astype(F32)
                    early = (i % 2) * (1 - i // 2)
                    open_gather(early, own, A.at[i])
                    close_gather(early, A.at[i])

                @pl.when(i == 1)
                def _():
                    forward_w(last)

                @pl.when(i == 2)
                def _():
                    close_w(last)
                    wait(load_mlp(last) + cot_load)

                @pl.when(i >= 2)
                def _():
                    open_middle(last, j, turn, CT.at[0])

                @pl.when(i < chunks)
                def _():
                    project(last, i)

                @pl.when((i > 0) & (i <= chunks))
                def _():
                    attend(last, i - 1)

                @pl.when(i >= 2)
                def _():
                    close_gather(turn, CT.at[0])
                    mlp_turn(last, 1, j)

                return carry

            lax.fori_loop(0, chunks + 2, slot, 0)
            pltpu.make_async_copy(STAGE.at[0], spill_y.at[chunks - 1], stage_sem.at[0]).wait()

        def input_back(layer, phase, chunk):
            grad_normed = total_of(phase - 1, chunk)
            hat, rstd = norm_rows(X[layer, chunk])
            add_vec(layer, 0, column_sum(grad_normed * hat))
            add_vec(layer, 1, column_sum(grad_normed))
            return DX[chunk] + norm_back(grad_normed * (1.0 + rv(layer, 0)), hat, rstd)

        def mlp_backward(layer, phase, name):
            GU[layer] = jnp.zeros((n_dp, block, hidden), F32)
            GD[layer] = jnp.zeros((n_dp, block, hidden), F32)

            def slot(i, carry):
                grad = input_back(layer + 1, phase, i)
                DX[i] = grad
                own = grad.astype(BF16).astype(F32)
                add_vec(layer, 5, column_sum(own))
                turn = i % 2
                open_gather(turn, own, CT.at[turn])

                @pl.when(i > 0)
                def _():
                    down_grads(layer, G0[i - 1], whole(CT, 1 - turn))

                close_gather(turn, CT.at[turn])
                grad_before = (mt(whole(CT, turn), WD[...]) * GP0[i].astype(F32)).astype(BF16)
                put_part(i, mt(grad_before, WU[...]))
                up_grads(layer, whole(C0, i), grad_before)
                send_part(phase, i)
                pump(name, i)
                return carry

            lax.fori_loop(0, chunks, slot, 0)
            down_grads(layer, G0[chunks - 1], whole(CT, (chunks - 1) % 2))

        def attend_back(layer, chunk):
            grad = whole(CT, chunk % 2)
            grad_heads = [tile.astype(BF16) for tile in apart_heads(mt(grad, WO[...]))]
            ring = chunk % WINDOW
            for head in range(heads):
                grad_o = grad_heads[head]
                query = Q[head, chunk]
                keys, values = window(K, head, chunk), window(V, head, chunk)
                cross = O[head, chunk].astype(F32) * grad_o.astype(F32)
                delta = sum(mt(jnp.ones((8, LANES), BF16), piece) for piece in pieces(cross, 2))[0:1]
                probs = jnp.exp2(mt(keys, query) * EXP2_SCALE - LSE[layer, head, chunk])
                grad_scores = (probs * (mt(values, grad_o) - delta)).astype(BF16)
                grad_v = mm(probs.astype(BF16), grad_o)
                grad_k = mm(grad_scores, query)
                DQ[dq_rows(chunk % 2, head)] = tm(grad_scores, keys) * SCALE
                for part in range(WINDOW):
                    place = (ring + part + WINDOW - 1) % WINDOW
                    rows = slice(part * CHUNK, (part + 1) * CHUNK)
                    if part < WINDOW - 1:
                        DV[head, place] += grad_v[rows]
                        DK[dk_rows(head, place)] += grad_k[rows]
                    else:
                        DV[head, place] = grad_v[rows]
                        DK[dk_rows(head, place)] = grad_k[rows]

        def between_back(layer, chunk):
            out = [O[head, chunk].astype(F32) for head in range(heads)]
            packed = joined_heads([jnp.zeros_like(out[0])] + out).astype(BF16)
            grad = whole(CT, chunk % 2)
            GA[layer, :, :, attn_cols - 2 * LANES :] += tm(grad, packed).reshape(n_dp, block, 2 * LANES)
            normed = whole(A, chunk)
            for kind in range(2):
                HATS[kind, 0], HATS[kind, 1] = norm_heads(mt(normed, WQ[kind]) + hv(layer, kind))

        def project_back(layer, chunk):
            ring, turn = chunk % WINDOW, chunk % 2
            grad_q = joined_heads([DQ[dq_rows(turn, head)] * real for head in range(heads)])
            grad_k = joined_heads([DK[dk_rows(head, ring)] * (real * SCALE) for head in range(heads)])
            grad_v = joined_heads([DV[head, ring] for head in range(heads)])
            parts = []
            for kind, grad in enumerate((grad_q, grad_k)):
                hat, rstd = HATS[kind, 0], HATS[kind, 1]
                inner = norm_heads_back(grad * (1.0 + hv(layer, 3 + kind)), hat, rstd)
                add_vec(layer, HEAD_ROW + kind, column_sum(inner))
                add_vec(layer, HEAD_ROW + 3 + kind, column_sum(grad * hat))
                parts.append(inner)
            add_vec(layer, HEAD_ROW + 5, column_sum(grad_q))
            add_vec(layer, HEAD_ROW + 2, column_sum(grad_v))
            parts.append(grad_v)
            put_part(chunk, sum(mm(part.astype(BF16), WQ[kind]) for kind, part in enumerate(parts)))
            firsts = [part[:, 0:LANES] for part in parts]
            third_q, third_k, third_v = (part[:, LANES:] for part in parts)
            packed = jnp.concatenate(firsts + [third_q + swap_halves(third_k), third_v], axis=1).astype(BF16)
            cols = packed.shape[1]
            GA[layer, :, :, 0:cols] += tm(whole(A, chunk), packed).reshape(n_dp, block, cols)

        def attn_backward(layer, phase, name):
            GA[layer] = jnp.zeros((n_dp, block, attn_cols), F32)
            DK[...] = jnp.zeros_like(DK)
            DV[...] = jnp.zeros_like(DV)

            def slot(i, carry):
                @pl.when(i < chunks)
                def _():
                    grad_second = total_of(phase - 1, i)
                    hat, rstd = norm_rows(X1[layer, i])
                    add_vec(layer, 2, column_sum(grad_second * hat))
                    add_vec(layer, 3, column_sum(grad_second))
                    grad = DX[i] + norm_back(grad_second * (1.0 + rv(layer, 2)), hat, rstd)
                    DX[i] = grad
                    own = grad.astype(BF16).astype(F32)
                    add_vec(layer, 4, column_sum(own))
                    open_gather(i % 2, own, CT.at[i % 2])

                @pl.when(i > 0)
                def _():
                    between_back(layer, i - 1)

                @pl.when(i < chunks)
                def _():
                    close_gather(i % 2, CT.at[i % 2])
                    attend_back(layer, i)

                pump(name + "m", i)

                @pl.when(i > 0)
                def _():
                    project_back(layer, i - 1)
                    send_part(phase, i - 1)

                pump(name, i)
                return carry

            lax.fori_loop(0, chunks + 1, slot, 0)

        near_first = [1, 0] + list(range(2, bits)) if bits > 1 else list(range(bits))

        def results(layer, kinds):
            pairs = [
                (GU.at[layer, dp], up_out),
                (GD.at[layer, dp], down_out),
                (QKV_STAGE.at[layer], qkv_out),
                (WO_STAGE.at[layer], wo_out),
            ]
            return [
                pltpu.make_async_copy(pairs[kind][0], pairs[kind][1].at[layer], out_sem.at[layer, kind]) for kind in kinds
            ]

        def finish_attn(layer):
            tiles = [GA[layer, dp, :, t * LANES : (t + 1) * LANES] for t in range(attn_cols // LANES)]
            thirds = [tiles[3], swap_halves(tiles[3]), tiles[4]]
            for kind in range(3):
                QKV_STAGE[layer, kind, :, 0:LANES] = tiles[kind]
                QKV_STAGE[layer, kind, :, LANES:channels] = thirds[kind][:, 0 : channels - LANES]
            later = swap_halves(tiles[5])
            WO_STAGE[layer, 0:LANES, :] = jnp.where(lane < HEAD, swap_halves(tiles[4]), later).T
            WO_STAGE[layer, LANES:channels, :] = later.T[0 : channels - LANES]
            start(results(layer, (2, 3)))

        def order_of(kind, layer):
            return near_first if NEAR_FIRST[kind, int(layer == last)] else list(range(bits))

        def grad_sum(kind, layer):
            order = order_of(kind, layer)
            next_order = order_of(kind, 0) if layer == last else None
            grad, landing = ((GU, RU), (GD, RD), (GA, RA))[kind]

            def finish():
                if kind < 2:
                    start(results(layer, (kind,)))
                else:
                    finish_attn(layer)

            return GradSum(
                n_dp, dp, mp, order, grad.at[layer], landing, g_send.at[kind], g_recv.at[kind], credit.at[kind],
                next_order, finish,
            )

        sums = {(kind, layer): grad_sum(kind, layer) for layer in (last, 0) for kind in range(3)}
        plan = plan_sums(sums, last)

        first_loads = [load(patches_in, INP, 4), load_wq(0)]
        cot_load = [load(cot_in, INP, 4)]
        load_wo(0).start()
        start(first_loads + load_mlp(0))
        load_wo(0).wait()
        pl.semaphore_wait(barrier, 4 + bits)
        open_w(0)
        load_wo(last).start()
        VEC[...] = jnp.zeros_like(VEC)
        WQ[:, channels:] = jnp.zeros((3, WQ.shape[1] - channels, width), BF16)
        WO[channels:] = jnp.zeros((WO.shape[0] - channels, width), BF16)
        HV[...] = jnp.zeros_like(HV)
        HV[:, :, 0:channels] = hv_ref[...]
        across_lanes = lax.broadcasted_iota(jnp.int32, BLOCKS.shape, 0) // HEAD
        same_head = across_lanes == lax.broadcasted_iota(jnp.int32, BLOCKS.shape, 1) // HEAD
        BLOCKS[...] = jnp.where(same_head, 1.0 / HEAD, 0.0).astype(BF16)
        keep = jnp.broadcast_to(keep_ref[...].astype(F32), (8, tokens))
        earlier = lax.broadcasted_iota(jnp.int32, (tokens, tokens), 0)
        later = lax.broadcasted_iota(jnp.int32, (tokens, tokens), 1)
        count = mm(keep.astype(BF16), (earlier <= later).astype(F32).astype(BF16))
        place = jnp.where(keep > 0.0, count - 1.0, 2.0 * tokens)
        TROW[...] = place
        TCOL[...] = jnp.broadcast_to(place[0:1, :], (LANES, tokens)).T
        segment = jnp.broadcast_to(seg_ref[...].astype(F32), (LANES, tokens)).T
        QA[...] = (segment.astype(jnp.int32) == lane - HEAD).astype(F32).astype(BF16).reshape(chunks, CHUNK, LANES)
        padding = jnp.broadcast_to((lane == PAD).astype(F32), (CHUNK, LANES)).astype(BF16)
        for head in range(heads):
            for edge in (0, chunks + 1):
                K[head, edge] = padding
                V[head, edge] = jnp.zeros((CHUNK, LANES), BF16)
        wait(first_loads)

        forward_first()
        wait(spills(False) + [load_wq(last)])
        start(load_mlp(last))
        forward_last()
        start(load_mlp(0))
        sums[0, last].start()
        sums[1, last].start()
        attn_backward(last, 2, "a1")
        sums[2, last].start()
        start(spills(True) + [load_wq(0), load_wo(0)])
        wait(load_mlp(0))
        mlp_backward(0, 3, "m0")
        sums[0, 0].start()
        sums[1, 0].start()
        wait(spills(True) + [load_wq(0), load_wo(0)])
        attn_backward(0, 4, "a0")
        sums[2, 0].start()

        def end_slot(i, carry):
            rows = input_back(0, 5, i)
            reload = pltpu.make_async_copy(spill_y.at[i], PART.at[i], stage_sem.at[0])
            reload.start()
            halves = X.at[:, i]
            open_gather(i % 2, rows, halves)
            reload.wait()
            to_sibling(i).start()
            close_gather(i % 2, halves)
            send_part(5, i)
            pump("end", i)
            return carry

        lax.fori_loop(0, chunks, end_slot, 0)

        def vec_copy(step, target):
            return pltpu.make_async_remote_copy(
                src_ref=VEC,
                dst_ref=VLAND.at[step],
                send_sem=v_send.at[step],
                recv_sem=v_recv.at[step],
                device_id=target,
                device_id_type=MESH,
            )

        def unpack(patch_chunk, stage):
            stage[...] = jnp.zeros(stage.shape, F32)
            place = TCOL[pl.ds(patch_chunk * CHUNK, CHUNK), 0:1].astype(jnp.int32)

            def add_slots(chunk, carry):
                slot = lax.broadcasted_iota(jnp.int32, (CHUNK, CHUNK), 1) + chunk * CHUNK
                chosen = (place == slot).astype(F32).astype(BF16)
                rest = jnp.concatenate([X[0, chunk], X[1, chunk]], axis=0)
                for piece in pieces(rest, 3):
                    stage[...] += mm(chosen, piece).reshape(stage.shape)
                return carry

            lax.fori_loop(0, patch_chunk + 1, add_slots, 0)

        def patch_copy(patch_chunk, turn):
            return pltpu.make_async_copy(STAGE.at[turn], gpatch_out.at[patch_chunk], stage_sem.at[turn])

        def out_copy(chunk):
            return pltpu.make_async_copy(A.at[chunk], packed_out.at[chunk], spill_sem.at[chunk])

        def chosen_part(values, share):
            column = lax.broadcasted_iota(jnp.int32, (values.shape[1], LANES), 0)
            wanted = lax.broadcasted_iota(jnp.int32, (values.shape[1], LANES), 1)
            chosen = ((column == wanted + dp * share) & (wanted < share)).astype(F32).astype(BF16)
            return mm_exact(values, chosen, 3)[:, 0:share]

        def vec_results():
            for layer in range(layers):
                rows = chosen_part(VEC[layer, 0:UP_BIAS_ROW, :], block)
                for row in range(ROW_VECTORS):
                    row_out[row, layer : layer + 1, :] = rows[row : row + 1]
                rows = chosen_part(VEC[layer, UP_BIAS_ROW : 2 * UP_BIAS_ROW, 0:hidden], hidden // n_dp)
                bias_out[layer : layer + 1, :] = rows[0:1]
                rows = chosen_part(VEC[layer, UP_BIAS_ROW : 2 * UP_BIAS_ROW, 0 : HV.shape[2]], channels // n_dp)
                for row in range(HEAD_VECTORS):
                    place = HEAD_ROW - UP_BIAS_ROW + row
                    head_out[row, layer : layer + 1, :] = rows[place : place + 1]

        def vec_partner(step):
            return (dp, sibling) if step == 0 else (flipped(dp, [step - 1]), mp)

        def vec_step(step):
            vec_copy(step, vec_partner(step)).wait()
            if step == 0:
                VEC[:, 0:UP_BIAS_ROW, :] += VLAND[0, :, 0:UP_BIAS_ROW, :]
            else:
                VEC[...] += VLAND[step]
            if step < bits:
                vec_copy(step + 1, vec_partner(step + 1)).start()
            else:
                vec_results()

        def unpack_next(step):
            turn = step % 2
            if step >= 2:
                patch_copy(step - 2, turn).wait()
            unpack(step, STAGE.at[turn])
            patch_copy(step, turn).start()

        vec_copy(0, vec_partner(0)).start()
        unpack_next(0)
        for step in range(chunks):
            if step <= bits:
                vec_step(step)
            for job, event in plan.get(("tail", step), []):
                job.take(*event)
            rows = (X1[last, step] + total_of(5, step) + rv(last, 5)) * LIVE[step, pl.ds(core * HALF, HALF), 0:1]
            open_gather(step % 2, rows.astype(BF16).astype(F32), A.at[step])
            if step + 1 < chunks:
                unpack_next(step + 1)
            close_gather(step % 2, A.at[step])
            out_copy(step).start()
        for step in range(chunks, bits + 1):
            vec_step(step)
        for job, event in plan.get(("tail", chunks), []):
            job.take(*event)

        for step in range(max(0, chunks - 2), chunks):
            patch_copy(step, step % 2).wait()
        for step in range(chunks):
            out_copy(step).wait()
        for job in sums.values():
            assert len(job.taken) == n_dp - 1
        for layer in range(layers):
            wait(results(layer, range(4)))

    return kernel


def body(n_dp, patches, patch_keep, patch_segment, cotangent, w_qkv, w_out, w_up, w_down, head_vectors, up_bias, row_vectors):
    tokens, width = patches.shape
    layers = w_qkv.shape[0]
    channels = w_qkv.shape[3]
    heads = channels // HEAD
    hidden = w_up.shape[2]
    chunks = tokens // CHUNK
    bits = n_dp.bit_length() - 1
    block = width // n_dp
    attn_cols = 4 * channels

    channels_up = (heads + 1) // 2 * LANES
    wq = jnp.transpose(w_qkv, (0, 1, 3, 2))
    hv = jnp.transpose(head_vectors, (1, 0, 2))
    rv = jnp.transpose(row_vectors, (1, 0, 2))
    any_space = pl.BlockSpec(memory_space=pl.ANY)
    vmem = pl.BlockSpec(memory_space=pltpu.VMEM)
    sds = jax.ShapeDtypeStruct
    half = (HALF, width)
    head_chunks = (heads, chunks, CHUNK, LANES)
    head_window = (heads, chunks + 2, CHUNK, LANES)
    out_shape = [
        sds((chunks, 2) + half, BF16),
        sds((chunks, 2) + half, F32),
        sds((layers, 3, block, channels), F32),
        sds((layers, channels, block), F32),
        sds((layers, block, hidden), F32),
        sds((layers, block, hidden), F32),
        sds((HEAD_VECTORS, layers, channels // n_dp), F32),
        sds((layers, hidden // n_dp), F32),
        sds((ROW_VECTORS, layers, block), F32),
        sds(head_chunks, BF16),
        sds(head_window, BF16),
        sds(head_window, BF16),
        sds(head_chunks, BF16),
        sds((chunks, 2) + half, BF16),
        sds((chunks, 2) + half, F32),
    ]
    v = pltpu.VMEM
    dma = pltpu.SemaphoreType.DMA
    scratch = [
        v((tokens, width), BF16),
        v((3, channels_up, width), BF16),
        v((channels_up, width), BF16),
        v((width, hidden), BF16),
        v((hidden, width), BF16),
        v((layers, chunks) + half, F32),
        v((layers, chunks) + half, F32),
        v((chunks, 2) + half, BF16),
        v((chunks, 2) + half, BF16),
        v((2, 2) + half, BF16),
        v(head_chunks, BF16),
        v(head_window, BF16),
        v(head_window, BF16),
        v(head_chunks, BF16),
        v((layers, heads, chunks, 1, CHUNK), F32),
        v((HEAD_VECTORS, layers, channels_up), F32),
        v((channels_up, channels_up), BF16),
        v((chunks, CHUNK, hidden), BF16),
        v((chunks, CHUNK, hidden), BF16),
        v((chunks, CHUNK, LANES), BF16),
        v((chunks, CHUNK, LANES), BF16),
        v((chunks, CHUNK, LANES), F32),
        v((8, tokens), F32),
        v((tokens, LANES), F32),
        v((chunks, 2) + half, F32),
        v((2,) + half, F32),
        v((2, chunks) + half, F32),
        v((2,) + half, F32),
        v(half, F32),
        v((chunks,) + half, F32),
        v((width, width), BF16),
        v((6, HALF, LANES), BF16),
        v((2 * heads * CHUNK, LANES), F32),
        v((2, 2, CHUNK, channels_up), F32),
        v((heads * WINDOW * CHUNK, LANES), F32),
        v((heads, WINDOW, CHUNK, LANES), F32),
        v((layers, n_dp, block, hidden), F32),
        v((layers, n_dp, block, hidden), F32),
        v((layers, n_dp, block, attn_cols), F32),
        v((n_dp - 1, block, hidden), F32),
        v((n_dp - 1, block, hidden), F32),
        v((n_dp - 1, block, attn_cols), F32),
        v((layers, VEC_ROWS, width), F32),
        v((bits + 1, layers, VEC_ROWS, width), F32),
        v((2, 2) + half, F32),
        v((layers, 3, block, channels), F32),
        v((layers, channels, block), F32),
        dma((5,)),
        dma((5,)),
        dma((2,)),
        dma((2,)),
        dma((2,)),
        dma((2, chunks)),
        dma((2, chunks)),
        dma((2,)),
        dma((2,)),
        dma((3, chunks)),
        dma((3, chunks)),
        dma((layers, 6)),
        dma((layers, 6)),
        dma((3, n_dp - 1)),
        dma((3, n_dp - 1)),
        pltpu.SemaphoreType.REGULAR((3, bits)),
        dma((bits + 1,)),
        dma((bits + 1,)),
        dma((layers, 4)),
    ]
    results = pl.pallas_call(
        make_kernel(n_dp, tokens, width, hidden, heads, layers),
        out_shape=out_shape,
        in_specs=[vmem] * 5 + [any_space] * 6,
        out_specs=[any_space] * 6 + [vmem] * 3 + [any_space] * (len(out_shape) - 9),
        scratch_shapes=scratch,
        compiler_params=pltpu.CompilerParams(
            collective_id=0, has_side_effects=True, vmem_limit_bytes=64 * 2**20 - 2**16
        ),
    )(patch_keep, patch_segment, hv, up_bias, rv, patches, cotangent, wq, w_out, w_up, w_down)
    packed, grad_patches, grad_qkv, grad_out, grad_up, grad_down, head_grads, bias_grads, row_grads = results[:9]
    return (
        packed.reshape(tokens, width),
        grad_patches.reshape(tokens, width),
        grad_qkv,
        grad_out,
        grad_up,
        jnp.transpose(grad_down, (0, 2, 1)),
        jnp.transpose(head_grads, (1, 0, 2)),
        bias_grads,
        jnp.transpose(row_grads, (1, 0, 2)),
    )


def solution(mesh):
    n_dp = mesh.shape["dp"]

    def step(*args):
        return body(n_dp, *args)

    return jax.shard_map(
        step,
        mesh=mesh,
        in_specs=(
            P("dp", None),
            P("dp", None),
            P("dp", None),
            P("dp", None),
            P(None, None, None, "mp"),
            P(None, "mp", None),
            P(None, None, "mp"),
            P(None, "mp", None),
            P(None, None, "mp"),
            P(None, "mp"),
            P(),
        ),
        out_specs=(
            P("dp", None),
            P("dp", None),
            P(None, None, "dp", "mp"),
            P(None, "mp", "dp"),
            P(None, "dp", "mp"),
            P(None, "mp", "dp"),
            P(None, None, ("mp", "dp")),
            P(None, ("mp", "dp")),
            P(None, None, "dp"),
        ),
        check_vma=False,
    )
```

```python
import math

import jax
import jax.numpy as jnp
from jax import lax
from jax.experimental import pallas as pl
from jax.experimental.pallas import tpu as pltpu
from jax.sharding import PartitionSpec as P

MESH = pl.DeviceIdType.MESH
F32, BF16 = jnp.float32, jnp.bfloat16
HEAD = 64
LANES = 128
EPS = 1e-6
SCALE = HEAD**-0.5
EXP2_SCALE = SCALE / math.log(2.0)
CHUNK = 256
HALF = CHUNK // 2
WINDOW = 3
IMAGES = 8
EMPTY = HEAD + IMAGES
PAD = EMPTY + 1
APART = 2048.0
ROW_VECTORS, HEAD_VECTORS = 6, 6
UP_BIAS_ROW, HEAD_ROW, VEC_ROWS = 8, 9, 16


def mm(left, right):
    return jnp.dot(left, right, preferred_element_type=F32)


def mt(left, right):
    return lax.dot_general(left, right, (((1,), (1,)), ((), ())), preferred_element_type=F32)


def tm(left, right):
    return lax.dot_general(left, right, (((0,), (0,)), ((), ())), preferred_element_type=F32)


def norm_rows(values):
    center = values - jnp.mean(values, axis=-1, keepdims=True)
    rstd = lax.rsqrt(jnp.mean(center * center, axis=-1, keepdims=True) + EPS)
    return center * rstd, rstd


def norm_back(grad, hat, rstd):
    mean_grad = jnp.mean(grad, axis=-1, keepdims=True)
    mean_cross = jnp.mean(grad * hat, axis=-1, keepdims=True)
    return rstd * (grad - mean_grad - hat * mean_cross)


def pieces(values, count):
    found, rest = [], values
    for _ in range(count):
        found.append(rest.astype(BF16))
        rest = rest - found[-1].astype(F32)
    return found


def mm_exact(values, right, count):
    return sum(mm(piece, right) for piece in pieces(values, count))


def column_sum(values):
    return jnp.sum(values, axis=0, keepdims=True)


def bit_of(index, bit):
    return (index // (1 << bit)) % 2


def flipped(index, bits):
    for bit in bits:
        index = index + (1 << bit) * (1 - 2 * bit_of(index, bit))
    return index


class GradSum:
    def __init__(self, n_dp, me, mp, order, grad, landing, send_sem, recv_sem, credit, next_order, finish):
        self.me, self.mp, self.order = me, mp, order
        self.steps = len(order)
        self.counts = [n_dp >> (k + 1) for k in range(self.steps)]
        self.offsets = [sum(self.counts[:k]) for k in range(self.steps)]
        self.grad, self.landing = grad, landing
        self.send_sem, self.recv_sem, self.credit = send_sem, recv_sem, credit
        self.next_order, self.finish = next_order, finish
        self.after, self.taken = {}, set()

    def turn(self, k):
        return sorted(range(self.counts[k]), key=lambda m: (m % 2 == 0, -m))

    def events(self):
        return [(k, m) for k in range(self.steps) for m in self.turn(k)]

    def later_bits(self, k, m):
        return [self.order[k + 1 + t] for t in range(self.steps - k - 1) if (m >> t) & 1]

    def partner(self, k, order=None):
        return (flipped(self.me, [(order or self.order)[k]]), self.mp)

    def copy(self, k, m):
        slot = self.offsets[k] + m
        block = flipped(self.me, [self.order[k]] + self.later_bits(k, m))
        return pltpu.make_async_remote_copy(
            src_ref=self.grad.at[block],
            dst_ref=self.landing.at[slot],
            send_sem=self.send_sem.at[slot],
            recv_sem=self.recv_sem.at[slot],
            device_id=self.partner(k),
            device_id_type=MESH,
        )

    def prepare(self, events):
        taken, sent = set(), set()
        for event in events:
            taken.add(event)
            sends = []
            for step in range(1, self.steps):
                for index in self.turn(step):
                    before = {(j, 1 << (step - 1 - j) | index << (step - j)) for j in range(step)}
                    if (step, index) not in sent and before <= taken:
                        first = all(step != other for other, _ in sent)
                        sends.append((step, index, first))
                        sent.add((step, index))
            k = event[0]
            freed = sum(step == k for step, _ in taken) == self.counts[k]
            self.after[event] = (sends, freed, len(taken) == sum(self.counts))

    def send(self, k, m, first):
        if first and self.next_order is None:
            pl.semaphore_wait(self.credit.at[k], 1)
        self.copy(k, m).start()

    def start(self):
        for position, m in enumerate(self.turn(0)):
            self.send(0, m, position == 0)

    def take(self, k, m):
        sends, freed, done = self.after[k, m]
        self.copy(k, m).wait()
        block = flipped(self.me, self.later_bits(k, m))
        self.grad[block] += self.landing[self.offsets[k] + m]
        self.taken.add((k, m))
        for step, index, first in sends:
            self.send(step, index, first)
        if self.next_order is not None and freed:
            target = self.partner(k, self.next_order)
            pl.semaphore_signal(self.credit.at[k], inc=1, device_id=target, device_id_type=MESH)
        if done:
            self.finish()


TAKEN = {
    (0, 1): [(("a1m", 1), (0, 3)), (("a1m", 2), (0, 1)), (("a1", 2), (0, 2)), (("a1", 3), (0, 0)), (("m0", 0), (1, 1)), (("m0", 2), (1, 0)), (("a0m", 0), (2, 0))],
    (1, 1): [(("a1m", 1), (0, 3)), (("a1m", 2), (0, 1)), (("a1", 2), (0, 2)), (("a1", 3), (0, 0)), (("m0", 0), (1, 1)), (("m0", 2), (1, 0)), (("a0m", 1), (2, 0))],
    (2, 1): [(("m0", 3), (0, 3)), (("a0m", 0), (0, 1)), (("a0", 0), (0, 2)), (("a0", 0), (1, 1)), (("a0m", 1), (0, 0)), (("a0", 4), (1, 0)), (("end", 2), (2, 0))],
    (0, 0): [(("a0m", 2), (0, 3)), (("a0m", 3), (0, 1)), (("a0", 3), (0, 2)), (("a0", 4), (0, 0)), (("end", 2), (1, 1)), (("end", 3), (1, 0)), (("tail", 3), (2, 0))],
    (1, 0): [(("a0m", 1), (0, 3)), (("a0m", 2), (0, 1)), (("a0m", 3), (0, 2)), (("a0", 3), (0, 0)), (("end", 1), (1, 1)), (("end", 2), (1, 0)), (("tail", 1), (2, 0))],
    (2, 0): [(("end", 3), (0, 3)), (("end", 3), (0, 1)), (("tail", 1), (0, 2)), (("tail", 2), (0, 0)), (("tail", 2), (1, 1)), (("tail", 3), (1, 0)), (("tail", 4), (2, 0))],
}
PHASES = ["a1", "m0", "a0", "end", "tail"]
NEAR_FIRST = {(0, 1): 0, (1, 1): 1, (2, 1): 0, (0, 0): 0, (1, 0): 1, (2, 0): 0}
SPREAD = {
    (0, 1): [("a1", 2), ("a1", 3), ("a1", 4), ("m0", 0), ("m0", 1), ("m0", 2), ("m0", 3)],
    (1, 1): [("a1", 2), ("a1", 3), ("a1", 4), ("m0", 0), ("m0", 1), ("m0", 2), ("m0", 3)],
    (2, 1): [("m0", 2), ("m0", 3), ("a0", 0), ("a0", 1), ("a0", 2)],
    (0, 0): [("a0", 2), ("a0", 3), ("a0", 4), ("end", 0), ("end", 1), ("end", 2), ("end", 3), ("tail", 0)],
    (1, 0): [("a0", 2), ("a0", 3), ("a0", 4), ("end", 0), ("end", 1), ("end", 2), ("end", 3), ("tail", 0)],
    (2, 0): [("end", 2), ("end", 3), ("tail", 0), ("tail", 1), ("tail", 2), ("tail", 3), ("tail", 4)],
}


def comes_at(place):
    phase, slot = place
    return (PHASES.index(phase.removesuffix("m")), slot, not phase.endswith("m"))


def plan_sums(sums, last):
    plan = {}
    for (kind, layer), job in sums.items():
        events, which = job.events(), (kind, int(layer == last))
        taken = TAKEN[which]
        if len(taken) != len(events):
            places = SPREAD[which]
            taken = [(places[n * len(places) // len(events)], event) for n, event in enumerate(events)]
        taken = sorted(taken, key=lambda entry: comes_at(entry[0]))
        job.prepare([event for _, event in taken])
        for place, event in taken:
            plan.setdefault(place, []).append((job, event))
    return plan


def make_kernel(n_dp, tokens, width, hidden, heads, layers):
    chunks = tokens // CHUNK
    bits = n_dp.bit_length() - 1
    block = width // n_dp
    channels = heads * HEAD
    attn_cols = 4 * channels
    last = layers - 1

    def kernel(
        keep_ref,
        seg_ref,
        hv_ref,
        ub_ref,
        rv_ref,
        patches_in,
        cot_in,
        wq_in,
        wo_in,
        wu_in,
        wd_in,
        packed_out,
        gpatch_out,
        qkv_out,
        wo_out,
        up_out,
        down_out,
        head_out,
        bias_out,
        row_out,
        spill_q,
        spill_k,
        spill_v,
        spill_o,
        spill_a,
        spill_y,
        INP,
        WQ,
        WO,
        WU,
        WD,
        X,
        X1,
        A,
        C0,
        CT,
        Q,
        K,
        V,
        O,
        LSE,
        HV,
        BLOCKS,
        G0,
        GP0,
        QA,
        KA,
        LIVE,
        TROW,
        TCOL,
        PART,
        DBUF,
        YBUF,
        CBUF,
        CSEND,
        DX,
        WOB,
        OD,
        DQ,
        HATS,
        DK,
        DV,
        GU,
        GD,
        GA,
        RU,
        RD,
        RA,
        VEC,
        VLAND,
        STAGE,
        QKV_STAGE,
        WO_STAGE,
        load_sem,
        spill_sem,
        stage_sem,
        d_send,
        d_recv,
        y_send,
        y_recv,
        c_send,
        c_recv,
        o_send,
        o_recv,
        w_send,
        w_recv,
        g_send,
        g_recv,
        credit,
        v_send,
        v_recv,
        out_sem,
    ):
        dp = lax.axis_index("dp")
        mp = lax.axis_index("mp")
        core = mp % 2
        sibling = mp + 1 - 2 * core
        across = (mp + 2) % 4
        diagonal = (sibling + 2) % 4

        barrier = pltpu.get_barrier_semaphore()
        for other in (sibling, across, diagonal):
            pl.semaphore_signal(barrier, inc=1, device_id=(dp, other), device_id_type=MESH)
        for flips in [[bit] for bit in range(bits)] + [[0, 1]]:
            pl.semaphore_signal(barrier, inc=1, device_id=(flipped(dp, flips), mp), device_id_type=MESH)

        lane = lax.broadcasted_iota(jnp.int32, (1, LANES), 1)
        real = (lane < HEAD).astype(F32)

        def load(source, target, index):
            return pltpu.make_async_copy(source, target, load_sem.at[index])

        def load_wq(layer):
            return load(wq_in.at[layer], WQ.at[:, 0:channels], 0)

        def load_wo(layer):
            return load(wo_in.at[layer], WO.at[0:channels], 1)

        def load_mlp(layer):
            return [load(wu_in.at[layer], WU, 2), load(wd_in.at[layer], WD, 3)]

        def spills(back):
            pairs = [(Q, spill_q), (K, spill_k), (V, spill_v), (O, spill_o), (A, spill_a)]
            return [
                pltpu.make_async_copy(*((far, near) if back else (near, far)), spill_sem.at[index])
                for index, (near, far) in enumerate(pairs)
            ]

        def start(copies):
            for copy in copies:
                copy.start()

        def wait(copies):
            for copy in copies:
                copy.wait()

        def to_sibling(chunk):
            slot = chunk % 2
            return pltpu.make_async_remote_copy(
                src_ref=PART.at[chunk, 1 - core],
                dst_ref=DBUF.at[slot],
                send_sem=d_send.at[slot],
                recv_sem=d_recv.at[slot],
                device_id=(dp, sibling),
                device_id_type=MESH,
            )

        def to_across(phase, chunk):
            slot = phase % 2
            return pltpu.make_async_remote_copy(
                src_ref=PART.at[chunk, core],
                dst_ref=YBUF.at[slot, chunk],
                send_sem=y_send.at[slot, chunk],
                recv_sem=y_recv.at[slot, chunk],
                device_id=(dp, across),
                device_id_type=MESH,
            )

        def to_gather(turn):
            return pltpu.make_async_remote_copy(
                src_ref=CSEND,
                dst_ref=CBUF.at[turn],
                send_sem=c_send.at[turn],
                recv_sem=c_recv.at[turn],
                device_id=(dp, sibling),
                device_id_type=MESH,
            )

        def put_part(chunk, values):
            PART[chunk] = values.reshape(2, HALF, width)
            to_sibling(chunk).start()

        def send_part(phase, chunk):
            to_sibling(chunk).wait()
            PART[chunk, core] += DBUF[chunk % 2]
            to_across(phase, chunk).start()

        def total_of(phase, chunk):
            to_across(phase, chunk).wait()
            return PART[chunk, core] + YBUF[phase % 2, chunk]

        def open_gather(turn, own, target):
            CSEND[...] = own
            to_gather(turn).start()
            target[core] = own.astype(target.dtype)

        def close_gather(turn, target):
            to_gather(turn).wait()
            target[1 - core] = CBUF[turn].astype(target.dtype)

        def whole(ref, chunk):
            return ref[chunk].reshape(CHUNK, width)

        def add_vec(layer, row, values):
            VEC[layer, row : row + 1, 0 : values.shape[1]] += values

        def rv(layer, row):
            return rv_ref[row, layer : layer + 1, :]

        def hv(layer, row):
            return HV[row, layer : layer + 1, :]

        def norm_heads(values):
            center = values - mm_exact(values, BLOCKS[...], 3)
            rstd = lax.rsqrt(mm_exact(center * center, BLOCKS[...], 2) + EPS)
            return center * rstd, rstd

        def norm_heads_back(grad, hat, rstd):
            mean_grad = mm_exact(grad, BLOCKS[...], 2)
            mean_cross = mm_exact(grad * hat, BLOCKS[...], 2)
            return rstd * (grad - mean_grad - hat * mean_cross)

        def swap_halves(tile):
            return pltpu.roll(tile, HEAD, 1)

        def apart_heads(values):
            tiles = []
            for head in range(heads):
                tile = values[:, head // 2 * LANES : (head // 2 + 1) * LANES]
                tiles.append((swap_halves(tile) if head % 2 else tile) * real)
            return tiles

        def joined_heads(tiles):
            pairs = [
                tiles[first] + swap_halves(tiles[first + 1]) if first + 1 < len(tiles) else tiles[first]
                for first in range(0, len(tiles), 2)
            ]
            return jnp.concatenate(pairs, axis=1)

        def pack(chunk):
            rows = lax.broadcasted_iota(jnp.int32, (CHUNK, tokens), 0) + chunk * CHUNK
            chosen = (TROW[0:1, :].astype(jnp.int32) == rows).astype(F32).astype(BF16)
            values = mm(chosen, INP[...])
            classes = mm(chosen, QA[...].reshape(tokens, LANES))
            alive = jnp.sum(classes, axis=-1, keepdims=True)
            LIVE[chunk] = jnp.broadcast_to(alive, (CHUNK, LANES))
            KA[chunk] = (classes + jnp.where(lane == EMPTY, 1.0 - alive, 0.0)).astype(BF16)
            PART[chunk] = values.reshape(2, HALF, width)
            X[0, chunk] = PART[chunk, core]
            hat, _ = norm_rows(values)
            A[chunk] = (hat * (1.0 + rv(0, 0)) + rv(0, 1)).astype(BF16).reshape(2, HALF, width)

        def apart_of(chunk):
            is_class = (lane >= HEAD) & (lane <= PAD)
            return jnp.where(is_class, -APART * (1.0 - KA[chunk].astype(F32)), 0.0)

        def project(layer, chunk):
            normed = whole(A, chunk)
            apart = apart_of(chunk).astype(BF16)
            classes = KA[chunk]
            ones = (lane == HEAD).astype(F32)
            hat, _ = norm_heads(mt(normed, WQ[0]) + hv(layer, 0))
            for head, tile in enumerate(apart_heads(hat * (1.0 + hv(layer, 3)) + hv(layer, 5))):
                Q[head, chunk] = tile.astype(BF16) + apart
            hat, _ = norm_heads(mt(normed, WQ[1]) + hv(layer, 1))
            for head, tile in enumerate(apart_heads(hat * (1.0 + hv(layer, 4)))):
                K[head, chunk + 1] = tile.astype(BF16) + classes
            for head, tile in enumerate(apart_heads(mt(normed, WQ[2]) + hv(layer, 2))):
                V[head, chunk + 1] = (tile + ones).astype(BF16)

        def window(ref, head, chunk):
            return ref[head, pl.ds(chunk, WINDOW)].reshape(WINDOW * CHUNK, LANES)

        def dq_rows(turn, head):
            return pl.ds(pl.multiple_of((turn * heads + head) * CHUNK, CHUNK), CHUNK)

        def dk_rows(head, place):
            return pl.ds(pl.multiple_of((head * WINDOW + place) * CHUNK, CHUNK), CHUNK)

        def sent_at(chunk, half):
            return pl.multiple_of((chunk * 2 + half) * channels, HEAD)

        def landed_at(source, chunk):
            return pl.multiple_of((source * chunks + chunk) * channels, HEAD)

        def o_copies(chunk):
            return [
                pltpu.make_async_remote_copy(
                    src_ref=DQ.at[pl.ds(sent_at(chunk, half), channels)],
                    dst_ref=DK.at[pl.ds(landed_at(source, chunk), channels)],
                    send_sem=o_send.at[source, chunk],
                    recv_sem=o_recv.at[source, chunk],
                    device_id=(dp, other),
                    device_id_type=MESH,
                )
                for source, (other, half) in enumerate(((sibling, 1 - core), (across, core), (diagonal, 1 - core)))
            ]

        def attend(layer, chunk):
            outs = []
            for head in range(heads):
                keys, values = window(K, head, chunk), window(V, head, chunk)
                scores = mt(keys, Q[head, chunk])
                expo = jnp.exp2(scores * EXP2_SCALE).astype(BF16)
                out = tm(values, expo)
                total = out[HEAD : HEAD + 1, :]
                LSE[layer, head, chunk] = jnp.log(total) * (1.0 / math.log(2.0))
                out = (out * (1.0 / total)).T
                out = jnp.where(lane < HEAD, out, 0.0).astype(BF16)
                O[head, chunk] = out
                outs.append(out.astype(F32))
            pair, third = outs[0] + swap_halves(outs[1]), outs[2]
            for half in range(2):
                first, row = sent_at(chunk, half), half * HALF
                DQ[pl.ds(first, HALF)] = pair[row : row + HALF]
                DQ[pl.ds(first + HALF, HALF // 2)] = third[row : row + HALF // 2] + swap_halves(
                    third[row + HALF // 2 : row + HALF]
                )
            start(o_copies(chunk))

        share = n_dp // 4

        quarter_of = bit_of(dp, 0) + 2 * bit_of(dp, 1)
        near = [[0], [1], [0, 1]]

        def w_quarter(layer, holder, quarter):
            if share >= 4:
                return GA.at[layer, pl.ds(holder * share + quarter * (share // 4), share // 4)]
            per = 4 // share
            rows = pl.ds(pl.multiple_of(quarter % per * (block // per), 8), block // per)
            return GA.at[layer, pl.ds(holder * share + quarter // per, 1), rows]

        def w_copy(layer, step):
            holder, target = (mp if step < 2 else across), (dp, sibling)
            if step == 0:
                target = (dp, across)
            elif 2 <= step < 5:
                target = (flipped(dp, near[step - 2]), mp)
            if step in (1, 5):
                part = GA.at[layer, pl.ds(holder * share, share)]
            else:
                part = w_quarter(layer, holder, quarter_of)
            return pltpu.make_async_remote_copy(
                src_ref=part,
                dst_ref=part,
                send_sem=w_send.at[layer, step],
                recv_sem=w_recv.at[layer, step],
                device_id=target,
                device_id_type=MESH,
            )

        def open_w(layer):
            GA[layer, pl.ds(mp * share, share)] = WO[0:channels].astype(F32).reshape(share, block, width)
            w_copy(layer, 0).start()
            w_copy(layer, 1).start()

        def spread_w(layer):
            w_copy(layer, 0).wait()
            start([w_copy(layer, step) for step in (2, 3, 4)])

        def forward_w(layer):
            wait([w_copy(layer, step) for step in (1, 2, 3, 4)])
            w_copy(layer, 5).start()

        def close_w(layer):
            w_copy(layer, 5).wait()
            for holder in range(4):
                rows = GA[layer, holder * share : (holder + 1) * share].reshape(channels, width).astype(BF16)
                WOB[holder * LANES : (holder + 1) * LANES] = rows[0:LANES]
                WOB[4 * LANES + holder * HEAD : 4 * LANES + (holder + 1) * HEAD] = rows[LANES:channels]

        def attn_out(chunk):
            wait(o_copies(chunk))
            places = [(DQ, sent_at(chunk, core))] + [(DK, landed_at(source, chunk)) for source in range(3)]
            thirds = []
            for holder, (ref, first) in zip((mp, sibling, across, diagonal), places):
                OD[holder] = ref[pl.ds(first, HALF)].astype(BF16)
                both = ref[pl.ds(first + HALF, HALF // 2)]
                thirds.append(jnp.concatenate([both * real, swap_halves(both) * real], axis=0))
            chip = mp // 2
            for place, (same, other) in ((chip, thirds[:2]), (1 - chip, thirds[2:])):
                low, high = jnp.where(core == 0, same, other), jnp.where(core == 0, other, same)
                OD[4 + place] = (low + swap_halves(high)).astype(BF16)
            return mm(jnp.concatenate([OD[tile] for tile in range(6)], axis=1), WOB[...])

        def open_middle(layer, chunk, turn, target):
            x1 = X[layer, chunk] + attn_out(chunk) + rv(layer, 4)
            X1[layer, chunk] = x1
            hat, _ = norm_rows(x1)
            own = (hat * (1.0 + rv(layer, 2)) + rv(layer, 3)).astype(BF16).astype(F32)
            open_gather(turn, own, target)

        def up(layer, second):
            before = mm(second, WU[...]) + ub_ref[layer : layer + 1, :]
            cdf = 0.5 * (1.0 + lax.erf(before * math.sqrt(0.5)))
            density = jnp.exp(before * before * -0.5) * (1.0 / math.sqrt(2.0 * math.pi))
            return (before * cdf).astype(BF16), cdf + before * density

        LAG = 3

        def forward_first():
            def slot(i, carry):
                @pl.when(i == 1)
                def _():
                    spread_w(0)

                @pl.when(i < chunks)
                def _():
                    pack(i)
                    project(0, i)

                @pl.when((i > 0) & (i <= chunks))
                def _():
                    attend(0, i - 1)

                @pl.when(i == LAG)
                def _():
                    forward_w(0)
                    wait(load_mlp(0))
                    close_w(0)

                @pl.when(i == chunks)
                def _():
                    load_wo(last).wait()
                    open_w(last)
                    start([load_wq(last)] + cot_load)

                @pl.when(i == chunks + 1)
                def _():
                    start(spills(False))
                    spread_w(last)

                @pl.when(i >= LAG)
                def _():
                    j = i - LAG
                    turn = j % 2
                    open_middle(0, j, turn, C0.at[j])
                    close_gather(turn, C0.at[j])
                    act, slope = up(0, whole(C0, j))
                    G0[j] = act
                    GP0[j] = slope.astype(BF16)
                    put_part(j, mm(act, WD[...]))
                    send_part(0, j)

                return carry

            lax.fori_loop(0, chunks + LAG, slot, 0)

        def up_grads(layer, second, grad_before):
            GU[layer] += tm(second, grad_before).reshape(n_dp, block, hidden)
            add_vec(layer, UP_BIAS_ROW, column_sum(grad_before.astype(F32)))

        def down_grads(layer, act, grad_out):
            GD[layer] += tm(grad_out, act).reshape(n_dp, block, hidden)

        def pump(name, i):
            for (where, index), events in plan.items():
                if where == name:

                    @pl.when(i == index)
                    def _():
                        for grad_sum, event in events:
                            grad_sum.take(*event)

        def mlp_turn(layer, phase, chunk):
            second = whole(CT, 0)
            act, slope = up(layer, second)

            @pl.when(chunk > 0)
            def _():
                pltpu.make_async_copy(STAGE.at[0], spill_y.at[chunk - 1], stage_sem.at[0]).wait()

            STAGE[0] = mm(act, WD[...]).reshape(2, HALF, width)
            pltpu.make_async_copy(STAGE.at[0], spill_y.at[chunk], stage_sem.at[0]).start()
            grad = INP[pl.ds(chunk * CHUNK, CHUNK), :].astype(F32) * LIVE[chunk, :, 0:1]
            CT[1] = grad.astype(BF16).reshape(2, HALF, width)
            own = CT[1, core].astype(F32)
            DX[chunk] = own
            add_vec(layer, 5, column_sum(own))
            grad = grad.astype(BF16)
            grad_before = (mt(grad, WD[...]) * slope).astype(BF16)
            put_part(chunk, mt(grad_before, WU[...]))
            up_grads(layer, second, grad_before)
            down_grads(layer, act, grad)
            send_part(phase, chunk)

        def forward_last():
            GU[last] = jnp.zeros((n_dp, block, hidden), F32)
            GD[last] = jnp.zeros((n_dp, block, hidden), F32)

            def slot(i, carry):
                j = i - LAG
                turn = (i + LAG) % 2

                @pl.when(i < chunks)
                def _():
                    x = X1[last - 1, i] + total_of(0, i) + rv(last - 1, 5)
                    X[last, i] = x
                    hat, _ = norm_rows(x)
                    own = (hat * (1.0 + rv(last, 0)) + rv(last, 1)).astype(BF16).astype(F32)
                    open_gather(i % 2, own, A.at[i])
                    close_gather(i % 2, A.at[i])

                @pl.when(i == 1)
                def _():
                    forward_w(last)

                @pl.when(i == LAG)
                def _():
                    close_w(last)
                    wait(load_mlp(last) + cot_load)

                @pl.when(i >= LAG)
                def _():
                    open_middle(last, j, turn, CT.at[0])

                @pl.when(i < chunks)
                def _():
                    project(last, i)

                @pl.when((i > 0) & (i <= chunks))
                def _():
                    attend(last, i - 1)

                @pl.when(i >= LAG)
                def _():
                    close_gather(turn, CT.at[0])
                    mlp_turn(last, 1, j)

                return carry

            lax.fori_loop(0, chunks + LAG, slot, 0)
            pltpu.make_async_copy(STAGE.at[0], spill_y.at[chunks - 1], stage_sem.at[0]).wait()

        def input_back(layer, phase, chunk):
            grad_normed = total_of(phase - 1, chunk)
            hat, rstd = norm_rows(X[layer, chunk])
            add_vec(layer, 0, column_sum(grad_normed * hat))
            add_vec(layer, 1, column_sum(grad_normed))
            return DX[chunk] + norm_back(grad_normed * (1.0 + rv(layer, 0)), hat, rstd)

        def mlp_backward(layer, phase, name):
            GU[layer] = jnp.zeros((n_dp, block, hidden), F32)
            GD[layer] = jnp.zeros((n_dp, block, hidden), F32)

            def slot(i, carry):
                grad = input_back(layer + 1, phase, i)
                DX[i] = grad
                own = grad.astype(BF16).astype(F32)
                add_vec(layer, 5, column_sum(own))
                turn = i % 2
                open_gather(turn, own, CT.at[turn])

                @pl.when(i > 0)
                def _():
                    down_grads(layer, G0[i - 1], whole(CT, 1 - turn))

                close_gather(turn, CT.at[turn])
                grad_before = (mt(whole(CT, turn), WD[...]) * GP0[i].astype(F32)).astype(BF16)
                put_part(i, mt(grad_before, WU[...]))
                up_grads(layer, whole(C0, i), grad_before)
                send_part(phase, i)
                pump(name, i)
                return carry

            lax.fori_loop(0, chunks, slot, 0)
            down_grads(layer, G0[chunks - 1], whole(CT, (chunks - 1) % 2))

        def attend_back(layer, chunk):
            grad = whole(CT, chunk % 2)
            grad_heads = [tile.astype(BF16) for tile in apart_heads(mt(grad, WO[...]))]
            ring = chunk % WINDOW
            for head in range(heads):
                grad_o = grad_heads[head]
                query = Q[head, chunk]
                keys, values = window(K, head, chunk), window(V, head, chunk)
                cross = O[head, chunk].astype(F32) * grad_o.astype(F32)
                delta = sum(mt(jnp.ones((8, LANES), BF16), piece) for piece in pieces(cross, 2))[0:1]
                probs = jnp.exp2(mt(keys, query) * EXP2_SCALE - LSE[layer, head, chunk])
                grad_scores = (probs * (mt(values, grad_o) - delta)).astype(BF16)
                grad_v = mm(probs.astype(BF16), grad_o)
                grad_k = mm(grad_scores, query)
                DQ[dq_rows(chunk % 2, head)] = tm(grad_scores, keys) * SCALE
                for part in range(WINDOW):
                    place = (ring + part + WINDOW - 1) % WINDOW
                    rows = slice(part * CHUNK, (part + 1) * CHUNK)
                    if part < WINDOW - 1:
                        DV[head, place] += grad_v[rows]
                        DK[dk_rows(head, place)] += grad_k[rows]
                    else:
                        DV[head, place] = grad_v[rows]
                        DK[dk_rows(head, place)] = grad_k[rows]

        def between_back(layer, chunk):
            out = [O[head, chunk].astype(F32) for head in range(heads)]
            packed = joined_heads([jnp.zeros_like(out[0])] + out).astype(BF16)
            grad = whole(CT, chunk % 2)
            GA[layer, :, :, attn_cols - 2 * LANES :] += tm(grad, packed).reshape(n_dp, block, 2 * LANES)
            normed = whole(A, chunk)
            for kind in range(2):
                HATS[kind, 0], HATS[kind, 1] = norm_heads(mt(normed, WQ[kind]) + hv(layer, kind))

        def project_back(layer, chunk):
            ring, turn = chunk % WINDOW, chunk % 2
            grad_q = joined_heads([DQ[dq_rows(turn, head)] * real for head in range(heads)])
            grad_k = joined_heads([DK[dk_rows(head, ring)] * (real * SCALE) for head in range(heads)])
            grad_v = joined_heads([DV[head, ring] for head in range(heads)])
            parts = []
            for kind, grad in enumerate((grad_q, grad_k)):
                hat, rstd = HATS[kind, 0], HATS[kind, 1]
                inner = norm_heads_back(grad * (1.0 + hv(layer, 3 + kind)), hat, rstd)
                add_vec(layer, HEAD_ROW + kind, column_sum(inner))
                add_vec(layer, HEAD_ROW + 3 + kind, column_sum(grad * hat))
                parts.append(inner)
            add_vec(layer, HEAD_ROW + 5, column_sum(grad_q))
            add_vec(layer, HEAD_ROW + 2, column_sum(grad_v))
            parts.append(grad_v)
            put_part(chunk, sum(mm(part.astype(BF16), WQ[kind]) for kind, part in enumerate(parts)))
            firsts = [part[:, 0:LANES] for part in parts]
            third_q, third_k, third_v = (part[:, LANES:] for part in parts)
            packed = jnp.concatenate(firsts + [third_q + swap_halves(third_k), third_v], axis=1).astype(BF16)
            cols = packed.shape[1]
            GA[layer, :, :, 0:cols] += tm(whole(A, chunk), packed).reshape(n_dp, block, cols)

        def attn_backward(layer, phase, name):
            GA[layer] = jnp.zeros((n_dp, block, attn_cols), F32)
            DK[...] = jnp.zeros_like(DK)
            DV[...] = jnp.zeros_like(DV)

            def slot(i, carry):
                @pl.when(i < chunks)
                def _():
                    grad_second = total_of(phase - 1, i)
                    hat, rstd = norm_rows(X1[layer, i])
                    add_vec(layer, 2, column_sum(grad_second * hat))
                    add_vec(layer, 3, column_sum(grad_second))
                    grad = DX[i] + norm_back(grad_second * (1.0 + rv(layer, 2)), hat, rstd)
                    DX[i] = grad
                    own = grad.astype(BF16).astype(F32)
                    add_vec(layer, 4, column_sum(own))
                    open_gather(i % 2, own, CT.at[i % 2])

                @pl.when(i > 0)
                def _():
                    between_back(layer, i - 1)

                @pl.when(i < chunks)
                def _():
                    close_gather(i % 2, CT.at[i % 2])
                    attend_back(layer, i)

                pump(name + "m", i)

                @pl.when(i > 0)
                def _():
                    project_back(layer, i - 1)
                    send_part(phase, i - 1)

                pump(name, i)
                return carry

            lax.fori_loop(0, chunks + 1, slot, 0)

        near_first = [1, 0] + list(range(2, bits)) if bits > 1 else list(range(bits))

        def results(layer, kinds):
            pairs = [
                (GU.at[layer, dp], up_out),
                (GD.at[layer, dp], down_out),
                (QKV_STAGE.at[layer], qkv_out),
                (WO_STAGE.at[layer], wo_out),
            ]
            return [
                pltpu.make_async_copy(pairs[kind][0], pairs[kind][1].at[layer], out_sem.at[layer, kind]) for kind in kinds
            ]

        def finish_attn(layer):
            tiles = [GA[layer, dp, :, t * LANES : (t + 1) * LANES] for t in range(attn_cols // LANES)]
            thirds = [tiles[3], swap_halves(tiles[3]), tiles[4]]
            for kind in range(3):
                QKV_STAGE[layer, kind, :, 0:LANES] = tiles[kind]
                QKV_STAGE[layer, kind, :, LANES:channels] = thirds[kind][:, 0 : channels - LANES]
            later = swap_halves(tiles[5])
            WO_STAGE[layer, 0:LANES, :] = jnp.where(lane < HEAD, swap_halves(tiles[4]), later).T
            WO_STAGE[layer, LANES:channels, :] = later.T[0 : channels - LANES]
            start(results(layer, (2, 3)))

        def order_of(kind, layer):
            return near_first if NEAR_FIRST[kind, int(layer == last)] else list(range(bits))

        def grad_sum(kind, layer):
            order = order_of(kind, layer)
            next_order = order_of(kind, 0) if layer == last else None
            grad, landing = ((GU, RU), (GD, RD), (GA, RA))[kind]

            def finish():
                if kind < 2:
                    start(results(layer, (kind,)))
                else:
                    finish_attn(layer)

            return GradSum(
                n_dp, dp, mp, order, grad.at[layer], landing, g_send.at[kind], g_recv.at[kind], credit.at[kind],
                next_order, finish,
            )

        sums = {(kind, layer): grad_sum(kind, layer) for layer in (last, 0) for kind in range(3)}
        plan = plan_sums(sums, last)

        first_loads = [load(patches_in, INP, 4), load_wq(0)]
        cot_load = [load(cot_in, INP, 4)]
        load_wo(0).start()
        start(first_loads + load_mlp(0))
        load_wo(0).wait()
        pl.semaphore_wait(barrier, 4 + bits)
        open_w(0)
        load_wo(last).start()
        VEC[...] = jnp.zeros_like(VEC)
        WQ[:, channels:] = jnp.zeros((3, WQ.shape[1] - channels, width), BF16)
        WO[channels:] = jnp.zeros((WO.shape[0] - channels, width), BF16)
        HV[...] = jnp.zeros_like(HV)
        HV[:, :, 0:channels] = hv_ref[...]
        across_lanes = lax.broadcasted_iota(jnp.int32, BLOCKS.shape, 0) // HEAD
        same_head = across_lanes == lax.broadcasted_iota(jnp.int32, BLOCKS.shape, 1) // HEAD
        BLOCKS[...] = jnp.where(same_head, 1.0 / HEAD, 0.0).astype(BF16)
        keep = jnp.broadcast_to(keep_ref[...].astype(F32), (8, tokens))
        earlier = lax.broadcasted_iota(jnp.int32, (tokens, tokens), 0)
        later = lax.broadcasted_iota(jnp.int32, (tokens, tokens), 1)
        count = mm(keep.astype(BF16), (earlier <= later).astype(F32).astype(BF16))
        place = jnp.where(keep > 0.0, count - 1.0, 2.0 * tokens)
        TROW[...] = place
        TCOL[...] = jnp.broadcast_to(place[0:1, :], (LANES, tokens)).T
        segment = jnp.broadcast_to(seg_ref[...].astype(F32), (LANES, tokens)).T
        QA[...] = (segment.astype(jnp.int32) == lane - HEAD).astype(F32).astype(BF16).reshape(chunks, CHUNK, LANES)
        padding = jnp.broadcast_to((lane == PAD).astype(F32), (CHUNK, LANES)).astype(BF16)
        for head in range(heads):
            for edge in (0, chunks + 1):
                K[head, edge] = padding
                V[head, edge] = jnp.zeros((CHUNK, LANES), BF16)
        wait(first_loads)

        forward_first()
        wait(spills(False) + [load_wq(last)])
        start(load_mlp(last))
        forward_last()
        start(load_mlp(0))
        sums[0, last].start()
        sums[1, last].start()
        attn_backward(last, 2, "a1")
        sums[2, last].start()
        start(spills(True) + [load_wq(0), load_wo(0)])
        wait(load_mlp(0))
        mlp_backward(0, 3, "m0")
        sums[0, 0].start()
        sums[1, 0].start()
        wait(spills(True) + [load_wq(0), load_wo(0)])
        attn_backward(0, 4, "a0")
        sums[2, 0].start()

        def end_slot(i, carry):
            rows = input_back(0, 5, i)
            reload = pltpu.make_async_copy(spill_y.at[i], PART.at[i], stage_sem.at[0])
            reload.start()
            halves = X.at[:, i]
            open_gather(i % 2, rows, halves)
            reload.wait()
            to_sibling(i).start()
            close_gather(i % 2, halves)
            send_part(5, i)
            pump("end", i)
            return carry

        lax.fori_loop(0, chunks, end_slot, 0)

        def vec_copy(step, target):
            return pltpu.make_async_remote_copy(
                src_ref=VEC,
                dst_ref=VLAND.at[step],
                send_sem=v_send.at[step],
                recv_sem=v_recv.at[step],
                device_id=target,
                device_id_type=MESH,
            )

        def unpack(patch_chunk, stage):
            stage[...] = jnp.zeros(stage.shape, F32)
            place = TCOL[pl.ds(patch_chunk * CHUNK, CHUNK), 0:1].astype(jnp.int32)

            def add_slots(chunk, carry):
                slot = lax.broadcasted_iota(jnp.int32, (CHUNK, CHUNK), 1) + chunk * CHUNK
                chosen = (place == slot).astype(F32).astype(BF16)
                rest = jnp.concatenate([X[0, chunk], X[1, chunk]], axis=0)
                for piece in pieces(rest, 3):
                    stage[...] += mm(chosen, piece).reshape(stage.shape)
                return carry

            lax.fori_loop(0, patch_chunk + 1, add_slots, 0)

        def patch_copy(patch_chunk, turn):
            return pltpu.make_async_copy(STAGE.at[turn], gpatch_out.at[patch_chunk], stage_sem.at[turn])

        def out_copy(chunk):
            return pltpu.make_async_copy(A.at[chunk], packed_out.at[chunk], spill_sem.at[chunk])

        def chosen_part(values, share):
            column = lax.broadcasted_iota(jnp.int32, (values.shape[1], LANES), 0)
            wanted = lax.broadcasted_iota(jnp.int32, (values.shape[1], LANES), 1)
            chosen = ((column == wanted + dp * share) & (wanted < share)).astype(F32).astype(BF16)
            return mm_exact(values, chosen, 3)[:, 0:share]

        def vec_results():
            for layer in range(layers):
                rows = chosen_part(VEC[layer, 0:UP_BIAS_ROW, :], block)
                for row in range(ROW_VECTORS):
                    row_out[row, layer : layer + 1, :] = rows[row : row + 1]
                rows = chosen_part(VEC[layer, UP_BIAS_ROW : 2 * UP_BIAS_ROW, 0:hidden], hidden // n_dp)
                bias_out[layer : layer + 1, :] = rows[0:1]
                rows = chosen_part(VEC[layer, UP_BIAS_ROW : 2 * UP_BIAS_ROW, 0 : HV.shape[2]], channels // n_dp)
                for row in range(HEAD_VECTORS):
                    place = HEAD_ROW - UP_BIAS_ROW + row
                    head_out[row, layer : layer + 1, :] = rows[place : place + 1]

        def vec_partner(step):
            return (dp, sibling) if step == 0 else (flipped(dp, [step - 1]), mp)

        def vec_step(step):
            vec_copy(step, vec_partner(step)).wait()
            if step == 0:
                VEC[:, 0:UP_BIAS_ROW, :] += VLAND[0, :, 0:UP_BIAS_ROW, :]
            else:
                VEC[...] += VLAND[step]
            if step < bits:
                vec_copy(step + 1, vec_partner(step + 1)).start()
            else:
                vec_results()

        def unpack_next(step):
            turn = step % 2
            if step >= 2:
                patch_copy(step - 2, turn).wait()
            unpack(step, STAGE.at[turn])
            patch_copy(step, turn).start()

        vec_copy(0, vec_partner(0)).start()
        unpack_next(0)
        for step in range(chunks):
            if step <= bits:
                vec_step(step)
            for job, event in plan.get(("tail", step), []):
                job.take(*event)
            rows = (X1[last, step] + total_of(5, step) + rv(last, 5)) * LIVE[step, pl.ds(core * HALF, HALF), 0:1]
            open_gather(step % 2, rows.astype(BF16).astype(F32), A.at[step])
            if step + 1 < chunks:
                unpack_next(step + 1)
            close_gather(step % 2, A.at[step])
            out_copy(step).start()
        for step in range(chunks, bits + 1):
            vec_step(step)
        for job, event in plan.get(("tail", chunks), []):
            job.take(*event)

        for step in range(max(0, chunks - 2), chunks):
            patch_copy(step, step % 2).wait()
        for step in range(chunks):
            out_copy(step).wait()
        for job in sums.values():
            assert len(job.taken) == n_dp - 1
        for layer in range(layers):
            wait(results(layer, range(4)))

    return kernel


def body(n_dp, patches, patch_keep, patch_segment, cotangent, w_qkv, w_out, w_up, w_down, head_vectors, up_bias, row_vectors):
    tokens, width = patches.shape
    layers = w_qkv.shape[0]
    channels = w_qkv.shape[3]
    heads = channels // HEAD
    hidden = w_up.shape[2]
    chunks = tokens // CHUNK
    bits = n_dp.bit_length() - 1
    block = width // n_dp
    attn_cols = 4 * channels

    channels_up = (heads + 1) // 2 * LANES
    wq = jnp.transpose(w_qkv, (0, 1, 3, 2))
    hv = jnp.transpose(head_vectors, (1, 0, 2))
    rv = jnp.transpose(row_vectors, (1, 0, 2))
    any_space = pl.BlockSpec(memory_space=pl.ANY)
    vmem = pl.BlockSpec(memory_space=pltpu.VMEM)
    sds = jax.ShapeDtypeStruct
    half = (HALF, width)
    head_chunks = (heads, chunks, CHUNK, LANES)
    head_window = (heads, chunks + 2, CHUNK, LANES)
    out_shape = [
        sds((chunks, 2) + half, BF16),
        sds((chunks, 2) + half, F32),
        sds((layers, 3, block, channels), F32),
        sds((layers, channels, block), F32),
        sds((layers, block, hidden), F32),
        sds((layers, block, hidden), F32),
        sds((HEAD_VECTORS, layers, channels // n_dp), F32),
        sds((layers, hidden // n_dp), F32),
        sds((ROW_VECTORS, layers, block), F32),
        sds(head_chunks, BF16),
        sds(head_window, BF16),
        sds(head_window, BF16),
        sds(head_chunks, BF16),
        sds((chunks, 2) + half, BF16),
        sds((chunks, 2) + half, F32),
    ]
    v = pltpu.VMEM
    dma = pltpu.SemaphoreType.DMA
    scratch = [
        v((tokens, width), BF16),
        v((3, channels_up, width), BF16),
        v((channels_up, width), BF16),
        v((width, hidden), BF16),
        v((hidden, width), BF16),
        v((layers, chunks) + half, F32),
        v((layers, chunks) + half, F32),
        v((chunks, 2) + half, BF16),
        v((chunks, 2) + half, BF16),
        v((2, 2) + half, BF16),
        v(head_chunks, BF16),
        v(head_window, BF16),
        v(head_window, BF16),
        v(head_chunks, BF16),
        v((layers, heads, chunks, 1, CHUNK), F32),
        v((HEAD_VECTORS, layers, channels_up), F32),
        v((channels_up, channels_up), BF16),
        v((chunks, CHUNK, hidden), BF16),
        v((chunks, CHUNK, hidden), BF16),
        v((chunks, CHUNK, LANES), BF16),
        v((chunks, CHUNK, LANES), BF16),
        v((chunks, CHUNK, LANES), F32),
        v((8, tokens), F32),
        v((tokens, LANES), F32),
        v((chunks, 2) + half, F32),
        v((2,) + half, F32),
        v((2, chunks) + half, F32),
        v((2,) + half, F32),
        v(half, F32),
        v((chunks,) + half, F32),
        v((width, width), BF16),
        v((6, HALF, LANES), BF16),
        v((2 * heads * CHUNK, LANES), F32),
        v((2, 2, CHUNK, channels_up), F32),
        v((heads * WINDOW * CHUNK, LANES), F32),
        v((heads, WINDOW, CHUNK, LANES), F32),
        v((layers, n_dp, block, hidden), F32),
        v((layers, n_dp, block, hidden), F32),
        v((layers, n_dp, block, attn_cols), F32),
        v((n_dp - 1, block, hidden), F32),
        v((n_dp - 1, block, hidden), F32),
        v((n_dp - 1, block, attn_cols), F32),
        v((layers, VEC_ROWS, width), F32),
        v((bits + 1, layers, VEC_ROWS, width), F32),
        v((2, 2) + half, F32),
        v((layers, 3, block, channels), F32),
        v((layers, channels, block), F32),
        dma((5,)),
        dma((5,)),
        dma((2,)),
        dma((2,)),
        dma((2,)),
        dma((2, chunks)),
        dma((2, chunks)),
        dma((2,)),
        dma((2,)),
        dma((3, chunks)),
        dma((3, chunks)),
        dma((layers, 6)),
        dma((layers, 6)),
        dma((3, n_dp - 1)),
        dma((3, n_dp - 1)),
        pltpu.SemaphoreType.REGULAR((3, bits)),
        dma((bits + 1,)),
        dma((bits + 1,)),
        dma((layers, 4)),
    ]
    results = pl.pallas_call(
        make_kernel(n_dp, tokens, width, hidden, heads, layers),
        out_shape=out_shape,
        in_specs=[vmem] * 5 + [any_space] * 6,
        out_specs=[any_space] * 6 + [vmem] * 3 + [any_space] * (len(out_shape) - 9),
        scratch_shapes=scratch,
        compiler_params=pltpu.CompilerParams(
            collective_id=0, has_side_effects=True, vmem_limit_bytes=64 * 2**20 - 2**16
        ),
    )(patch_keep, patch_segment, hv, up_bias, rv, patches, cotangent, wq, w_out, w_up, w_down)
    packed, grad_patches, grad_qkv, grad_out, grad_up, grad_down, head_grads, bias_grads, row_grads = results[:9]
    return (
        packed.reshape(tokens, width),
        grad_patches.reshape(tokens, width),
        grad_qkv,
        grad_out,
        grad_up,
        jnp.transpose(grad_down, (0, 2, 1)),
        jnp.transpose(head_grads, (1, 0, 2)),
        bias_grads,
        jnp.transpose(row_grads, (1, 0, 2)),
    )


def solution(mesh):
    n_dp = mesh.shape["dp"]

    def step(*args):
        return body(n_dp, *args)

    return jax.shard_map(
        step,
        mesh=mesh,
        in_specs=(
            P("dp", None),
            P("dp", None),
            P("dp", None),
            P("dp", None),
            P(None, None, None, "mp"),
            P(None, "mp", None),
            P(None, None, "mp"),
            P(None, "mp", None),
            P(None, None, "mp"),
            P(None, "mp"),
            P(),
        ),
        out_specs=(
            P("dp", None),
            P("dp", None),
            P(None, None, "dp", "mp"),
            P(None, "mp", "dp"),
            P(None, "dp", "mp"),
            P(None, "mp", "dp"),
            P(None, None, ("mp", "dp")),
            P(None, ("mp", "dp")),
            P(None, None, "dp"),
        ),
        check_vma=False,
    )
```

```python
import math

import jax
import jax.numpy as jnp
from jax import lax
from jax.experimental import pallas as pl
from jax.experimental.pallas import tpu as pltpu
from jax.sharding import PartitionSpec as P

MESH = pl.DeviceIdType.MESH
F32, BF16 = jnp.float32, jnp.bfloat16
HEAD = 64
LANES = 128
EPS = 1e-6
SCALE = HEAD**-0.5
EXP2_SCALE = SCALE / math.log(2.0)
CHUNK = 256
HALF = CHUNK // 2
WINDOW = 3
IMAGES = 8
EMPTY = HEAD + IMAGES
PAD = EMPTY + 1
APART = 2048.0
ROW_VECTORS, HEAD_VECTORS = 6, 6
UP_BIAS_ROW, HEAD_ROW, VEC_ROWS = 8, 9, 16


def mm(left, right):
    return jnp.dot(left, right, preferred_element_type=F32)


def mt(left, right):
    return lax.dot_general(left, right, (((1,), (1,)), ((), ())), preferred_element_type=F32)


def tm(left, right):
    return lax.dot_general(left, right, (((0,), (0,)), ((), ())), preferred_element_type=F32)


def norm_rows(values):
    center = values - jnp.mean(values, axis=-1, keepdims=True)
    rstd = lax.rsqrt(jnp.mean(center * center, axis=-1, keepdims=True) + EPS)
    return center * rstd, rstd


def norm_back(grad, hat, rstd):
    mean_grad = jnp.mean(grad, axis=-1, keepdims=True)
    mean_cross = jnp.mean(grad * hat, axis=-1, keepdims=True)
    return rstd * (grad - mean_grad - hat * mean_cross)


def pieces(values, count):
    found, rest = [], values
    for _ in range(count):
        found.append(rest.astype(BF16))
        rest = rest - found[-1].astype(F32)
    return found


def mm_exact(values, right, count):
    return sum(mm(piece, right) for piece in pieces(values, count))


def column_sum(values):
    return jnp.sum(values, axis=0, keepdims=True)


def bit_of(index, bit):
    return (index // (1 << bit)) % 2


def flipped(index, bits):
    for bit in bits:
        index = index + (1 << bit) * (1 - 2 * bit_of(index, bit))
    return index


class GradSum:
    def __init__(self, n_dp, me, mp, order, grad, landing, send_sem, recv_sem, credit, next_order, finish):
        self.me, self.mp, self.order = me, mp, order
        self.steps = len(order)
        self.counts = [n_dp >> (k + 1) for k in range(self.steps)]
        self.offsets = [sum(self.counts[:k]) for k in range(self.steps)]
        self.grad, self.landing = grad, landing
        self.send_sem, self.recv_sem, self.credit = send_sem, recv_sem, credit
        self.next_order, self.finish = next_order, finish
        self.after, self.taken = {}, set()

    def turn(self, k):
        return sorted(range(self.counts[k]), key=lambda m: (m % 2 == 0, -m))

    def events(self):
        return [(k, m) for k in range(self.steps) for m in self.turn(k)]

    def later_bits(self, k, m):
        return [self.order[k + 1 + t] for t in range(self.steps - k - 1) if (m >> t) & 1]

    def partner(self, k, order=None):
        return (flipped(self.me, [(order or self.order)[k]]), self.mp)

    def copy(self, k, m):
        slot = self.offsets[k] + m
        block = flipped(self.me, [self.order[k]] + self.later_bits(k, m))
        return pltpu.make_async_remote_copy(
            src_ref=self.grad.at[block],
            dst_ref=self.landing.at[slot],
            send_sem=self.send_sem.at[slot],
            recv_sem=self.recv_sem.at[slot],
            device_id=self.partner(k),
            device_id_type=MESH,
        )

    def prepare(self, events):
        taken, sent = set(), set()
        for event in events:
            taken.add(event)
            sends = []
            for step in range(1, self.steps):
                for index in self.turn(step):
                    before = {(j, 1 << (step - 1 - j) | index << (step - j)) for j in range(step)}
                    if (step, index) not in sent and before <= taken:
                        first = all(step != other for other, _ in sent)
                        sends.append((step, index, first))
                        sent.add((step, index))
            k = event[0]
            freed = sum(step == k for step, _ in taken) == self.counts[k]
            self.after[event] = (sends, freed, len(taken) == sum(self.counts))

    def send(self, k, m, first):
        if first and self.next_order is None:
            pl.semaphore_wait(self.credit.at[k], 1)
        self.copy(k, m).start()

    def start(self):
        for position, m in enumerate(self.turn(0)):
            self.send(0, m, position == 0)

    def take(self, k, m):
        sends, freed, done = self.after[k, m]
        self.copy(k, m).wait()
        block = flipped(self.me, self.later_bits(k, m))
        self.grad[block] += self.landing[self.offsets[k] + m]
        self.taken.add((k, m))
        for step, index, first in sends:
            self.send(step, index, first)
        if self.next_order is not None and freed:
            target = self.partner(k, self.next_order)
            pl.semaphore_signal(self.credit.at[k], inc=1, device_id=target, device_id_type=MESH)
        if done:
            self.finish()


TAKEN = {
    (0, 1): [(("a1", 0), (0, 3)), (("a1", 1), (0, 1)), (("a1", 2), (0, 2)), (("a1", 3), (0, 0)), (("a1", 4), (1, 1)), (("m0", 1), (1, 0)), (("a0m", 0), (2, 0))],
    (1, 1): [(("a1", 0), (0, 3)), (("a1", 1), (0, 1)), (("a1", 2), (0, 2)), (("a1", 3), (0, 0)), (("a1", 4), (1, 1)), (("m0", 1), (1, 0)), (("a0m", 1), (2, 0))],
    (2, 1): [(("m0", 3), (0, 3)), (("a0m", 0), (0, 1)), (("a0m", 0), (0, 2)), (("a0m", 0), (1, 1)), (("a0m", 1), (0, 0)), (("a0", 4), (1, 0)), (("end", 2), (2, 0))],
    (0, 0): [(("a0", 1), (0, 3)), (("a0", 2), (0, 1)), (("a0m", 3), (0, 2)), (("a0", 4), (0, 0)), (("end", 2), (1, 1)), (("end", 2), (1, 0)), (("tail", 2), (2, 0))],
    (1, 0): [(("a0m", 1), (0, 3)), (("a0", 1), (0, 1)), (("a0", 2), (0, 2)), (("a0m", 3), (0, 0)), (("end", 0), (1, 1)), (("end", 2), (1, 0)), (("tail", 0), (2, 0))],
    (2, 0): [(("end", 2), (0, 3)), (("end", 3), (0, 1)), (("tail", 0), (0, 2)), (("tail", 1), (0, 0)), (("tail", 1), (1, 1)), (("tail", 2), (1, 0)), (("tail", 4), (2, 0))],
}
PHASES = ["a1", "m0", "a0", "end", "tail"]
NEAR_FIRST = {(0, 1): 0, (1, 1): 1, (2, 1): 0, (0, 0): 0, (1, 0): 1, (2, 0): 0}
SPREAD = {
    (0, 1): [("a1", 2), ("a1", 3), ("a1", 4), ("m0", 0), ("m0", 1), ("m0", 2), ("m0", 3)],
    (1, 1): [("a1", 2), ("a1", 3), ("a1", 4), ("m0", 0), ("m0", 1), ("m0", 2), ("m0", 3)],
    (2, 1): [("m0", 2), ("m0", 3), ("a0", 0), ("a0", 1), ("a0", 2)],
    (0, 0): [("a0", 2), ("a0", 3), ("a0", 4), ("end", 0), ("end", 1), ("end", 2), ("end", 3), ("tail", 0)],
    (1, 0): [("a0", 2), ("a0", 3), ("a0", 4), ("end", 0), ("end", 1), ("end", 2), ("end", 3), ("tail", 0)],
    (2, 0): [("end", 2), ("end", 3), ("tail", 0), ("tail", 1), ("tail", 2), ("tail", 3), ("tail", 4)],
}


def comes_at(place):
    phase, slot = place
    return (PHASES.index(phase.removesuffix("m")), slot, not phase.endswith("m"))


def plan_sums(sums, last):
    plan = {}
    for (kind, layer), job in sums.items():
        events, which = job.events(), (kind, int(layer == last))
        taken = TAKEN[which]
        if len(taken) != len(events):
            places = SPREAD[which]
            taken = [(places[n * len(places) // len(events)], event) for n, event in enumerate(events)]
        taken = sorted(taken, key=lambda entry: comes_at(entry[0]))
        job.prepare([event for _, event in taken])
        for place, event in taken:
            plan.setdefault(place, []).append((job, event))
    return plan


def make_kernel(n_dp, tokens, width, hidden, heads, layers):
    chunks = tokens // CHUNK
    bits = n_dp.bit_length() - 1
    block = width // n_dp
    channels = heads * HEAD
    attn_cols = 4 * channels
    last = layers - 1

    def kernel(
        keep_ref,
        seg_ref,
        hv_ref,
        ub_ref,
        rv_ref,
        patches_in,
        cot_in,
        wq_in,
        wo_in,
        wu_in,
        wd_in,
        packed_out,
        gpatch_out,
        qkv_out,
        wo_out,
        up_out,
        down_out,
        head_out,
        bias_out,
        row_out,
        spill_q,
        spill_k,
        spill_v,
        spill_o,
        spill_a,
        spill_y,
        INP,
        WQ,
        WO,
        WU,
        WD,
        X,
        X1,
        A,
        C0,
        CT,
        Q,
        K,
        V,
        O,
        LSE,
        HV,
        BLOCKS,
        G0,
        GP0,
        QA,
        KA,
        LIVE,
        TROW,
        TCOL,
        PART,
        DBUF,
        YBUF,
        CBUF,
        CSEND,
        DX,
        WOB,
        OD,
        DQ,
        HATS,
        DK,
        DV,
        GU,
        GD,
        GA,
        RU,
        RD,
        RA,
        VEC,
        VLAND,
        STAGE,
        QKV_STAGE,
        WO_STAGE,
        load_sem,
        spill_sem,
        stage_sem,
        d_send,
        d_recv,
        y_send,
        y_recv,
        c_send,
        c_recv,
        o_send,
        o_recv,
        w_send,
        w_recv,
        g_send,
        g_recv,
        credit,
        v_send,
        v_recv,
        out_sem,
    ):
        dp = lax.axis_index("dp")
        mp = lax.axis_index("mp")
        core = mp % 2
        sibling = mp + 1 - 2 * core
        across = (mp + 2) % 4
        diagonal = (sibling + 2) % 4

        barrier = pltpu.get_barrier_semaphore()
        for other in (sibling, across, diagonal):
            pl.semaphore_signal(barrier, inc=1, device_id=(dp, other), device_id_type=MESH)
        for flips in [[bit] for bit in range(bits)] + [[0, 1]]:
            pl.semaphore_signal(barrier, inc=1, device_id=(flipped(dp, flips), mp), device_id_type=MESH)

        lane = lax.broadcasted_iota(jnp.int32, (1, LANES), 1)
        real = (lane < HEAD).astype(F32)

        def load(source, target, index):
            return pltpu.make_async_copy(source, target, load_sem.at[index])

        def load_wq(layer):
            return load(wq_in.at[layer], WQ.at[:, 0:channels], 0)

        def load_wo(layer):
            return load(wo_in.at[layer], WO.at[0:channels], 1)

        def load_mlp(layer):
            return [load(wu_in.at[layer], WU, 2), load(wd_in.at[layer], WD, 3)]

        def spills(back):
            pairs = [(Q, spill_q), (K, spill_k), (V, spill_v), (O, spill_o), (A, spill_a)]
            return [
                pltpu.make_async_copy(*((far, near) if back else (near, far)), spill_sem.at[index])
                for index, (near, far) in enumerate(pairs)
            ]

        def start(copies):
            for copy in copies:
                copy.start()

        def wait(copies):
            for copy in copies:
                copy.wait()

        def to_sibling(chunk):
            slot = chunk % 2
            return pltpu.make_async_remote_copy(
                src_ref=PART.at[chunk, 1 - core],
                dst_ref=DBUF.at[slot],
                send_sem=d_send.at[slot],
                recv_sem=d_recv.at[slot],
                device_id=(dp, sibling),
                device_id_type=MESH,
            )

        def to_across(phase, chunk):
            slot = phase % 2
            return pltpu.make_async_remote_copy(
                src_ref=PART.at[chunk, core],
                dst_ref=YBUF.at[slot, chunk],
                send_sem=y_send.at[slot, chunk],
                recv_sem=y_recv.at[slot, chunk],
                device_id=(dp, across),
                device_id_type=MESH,
            )

        def to_gather(turn):
            return pltpu.make_async_remote_copy(
                src_ref=CSEND,
                dst_ref=CBUF.at[turn],
                send_sem=c_send.at[turn],
                recv_sem=c_recv.at[turn],
                device_id=(dp, sibling),
                device_id_type=MESH,
            )

        def put_part(chunk, values):
            PART[chunk] = values.reshape(2, HALF, width)
            to_sibling(chunk).start()

        def send_part(phase, chunk):
            to_sibling(chunk).wait()
            PART[chunk, core] += DBUF[chunk % 2]
            to_across(phase, chunk).start()

        def total_of(phase, chunk):
            to_across(phase, chunk).wait()
            return PART[chunk, core] + YBUF[phase % 2, chunk]

        def open_gather(turn, own, target):
            CSEND[...] = own
            to_gather(turn).start()
            target[core] = own.astype(target.dtype)

        def close_gather(turn, target):
            to_gather(turn).wait()
            target[1 - core] = CBUF[turn].astype(target.dtype)

        def whole(ref, chunk):
            return ref[chunk].reshape(CHUNK, width)

        def add_vec(layer, row, values):
            VEC[layer, row : row + 1, 0 : values.shape[1]] += values

        def rv(layer, row):
            return rv_ref[row, layer : layer + 1, :]

        def hv(layer, row):
            return HV[row, layer : layer + 1, :]

        def norm_heads(values):
            center = values - mm_exact(values, BLOCKS[...], 3)
            rstd = lax.rsqrt(mm_exact(center * center, BLOCKS[...], 2) + EPS)
            return center * rstd, rstd

        def norm_heads_back(grad, hat, rstd):
            mean_grad = mm_exact(grad, BLOCKS[...], 2)
            mean_cross = mm_exact(grad * hat, BLOCKS[...], 2)
            return rstd * (grad - mean_grad - hat * mean_cross)

        def swap_halves(tile):
            return pltpu.roll(tile, HEAD, 1)

        def apart_heads(values):
            tiles = []
            for head in range(heads):
                tile = values[:, head // 2 * LANES : (head // 2 + 1) * LANES]
                tiles.append((swap_halves(tile) if head % 2 else tile) * real)
            return tiles

        def joined_heads(tiles):
            pairs = [
                tiles[first] + swap_halves(tiles[first + 1]) if first + 1 < len(tiles) else tiles[first]
                for first in range(0, len(tiles), 2)
            ]
            return jnp.concatenate(pairs, axis=1)

        def pack(chunk):
            rows = lax.broadcasted_iota(jnp.int32, (CHUNK, tokens), 0) + chunk * CHUNK
            chosen = (TROW[0:1, :].astype(jnp.int32) == rows).astype(F32).astype(BF16)
            values = mm(chosen, INP[...])
            classes = mm(chosen, QA[...].reshape(tokens, LANES))
            alive = jnp.sum(classes, axis=-1, keepdims=True)
            LIVE[chunk] = jnp.broadcast_to(alive, (CHUNK, LANES))
            KA[chunk] = (classes + jnp.where(lane == EMPTY, 1.0 - alive, 0.0)).astype(BF16)
            PART[chunk] = values.reshape(2, HALF, width)
            X[0, chunk] = PART[chunk, core]
            hat, _ = norm_rows(values)
            A[chunk] = (hat * (1.0 + rv(0, 0)) + rv(0, 1)).astype(BF16).reshape(2, HALF, width)

        def apart_of(chunk):
            is_class = (lane >= HEAD) & (lane <= PAD)
            return jnp.where(is_class, -APART * (1.0 - KA[chunk].astype(F32)), 0.0)

        def project(layer, chunk):
            normed = whole(A, chunk)
            apart = apart_of(chunk).astype(BF16)
            classes = KA[chunk]
            ones = (lane == HEAD).astype(F32)
            hat, _ = norm_heads(mt(normed, WQ[0]) + hv(layer, 0))
            for head, tile in enumerate(apart_heads(hat * (1.0 + hv(layer, 3)) + hv(layer, 5))):
                Q[head, chunk] = tile.astype(BF16) + apart
            hat, _ = norm_heads(mt(normed, WQ[1]) + hv(layer, 1))
            for head, tile in enumerate(apart_heads(hat * (1.0 + hv(layer, 4)))):
                K[head, chunk + 1] = tile.astype(BF16) + classes
            for head, tile in enumerate(apart_heads(mt(normed, WQ[2]) + hv(layer, 2))):
                V[head, chunk + 1] = (tile + ones).astype(BF16)

        def window(ref, head, chunk):
            return ref[head, pl.ds(chunk, WINDOW)].reshape(WINDOW * CHUNK, LANES)

        def dq_rows(turn, head):
            return pl.ds(pl.multiple_of((turn * heads + head) * CHUNK, CHUNK), CHUNK)

        def dk_rows(head, place):
            return pl.ds(pl.multiple_of((head * WINDOW + place) * CHUNK, CHUNK), CHUNK)

        def sent_at(chunk, half):
            return pl.multiple_of((chunk * 2 + half) * channels, HEAD)

        def landed_at(source, chunk):
            return pl.multiple_of((source * chunks + chunk) * channels, HEAD)

        def o_copies(chunk):
            return [
                pltpu.make_async_remote_copy(
                    src_ref=DQ.at[pl.ds(sent_at(chunk, half), channels)],
                    dst_ref=DK.at[pl.ds(landed_at(source, chunk), channels)],
                    send_sem=o_send.at[source, chunk],
                    recv_sem=o_recv.at[source, chunk],
                    device_id=(dp, other),
                    device_id_type=MESH,
                )
                for source, (other, half) in enumerate(((sibling, 1 - core), (across, core), (diagonal, 1 - core)))
            ]

        def attend(layer, chunk):
            outs = []
            for head in range(heads):
                keys, values = window(K, head, chunk), window(V, head, chunk)
                scores = mt(keys, Q[head, chunk])
                expo = jnp.exp2(scores * EXP2_SCALE).astype(BF16)
                out = tm(values, expo)
                total = out[HEAD : HEAD + 1, :]
                LSE[layer, head, chunk] = jnp.log(total) * (1.0 / math.log(2.0))
                out = (out * (1.0 / total)).T
                out = jnp.where(lane < HEAD, out, 0.0).astype(BF16)
                O[head, chunk] = out
                outs.append(out.astype(F32))
            pair, third = outs[0] + swap_halves(outs[1]), outs[2]
            for half in range(2):
                first, row = sent_at(chunk, half), half * HALF
                DQ[pl.ds(first, HALF)] = pair[row : row + HALF]
                DQ[pl.ds(first + HALF, HALF // 2)] = third[row : row + HALF // 2] + swap_halves(
                    third[row + HALF // 2 : row + HALF]
                )
            start(o_copies(chunk))

        share = n_dp // 4

        quarter_of = bit_of(dp, 0) + 2 * bit_of(dp, 1)
        near = [[0], [1], [0, 1]]

        def w_quarter(layer, holder, quarter):
            if share >= 4:
                return GA.at[layer, pl.ds(holder * share + quarter * (share // 4), share // 4)]
            per = 4 // share
            rows = pl.ds(pl.multiple_of(quarter % per * (block // per), 8), block // per)
            return GA.at[layer, pl.ds(holder * share + quarter // per, 1), rows]

        def w_copy(layer, step):
            holder, target = (mp if step < 2 else across), (dp, sibling)
            if step == 0:
                target = (dp, across)
            elif 2 <= step < 5:
                target = (flipped(dp, near[step - 2]), mp)
            if step in (1, 5):
                part = GA.at[layer, pl.ds(holder * share, share)]
            else:
                part = w_quarter(layer, holder, quarter_of)
            return pltpu.make_async_remote_copy(
                src_ref=part,
                dst_ref=part,
                send_sem=w_send.at[layer, step],
                recv_sem=w_recv.at[layer, step],
                device_id=target,
                device_id_type=MESH,
            )

        def open_w(layer):
            GA[layer, pl.ds(mp * share, share)] = WO[0:channels].astype(F32).reshape(share, block, width)
            w_copy(layer, 0).start()
            w_copy(layer, 1).start()

        def spread_w(layer):
            w_copy(layer, 0).wait()
            start([w_copy(layer, step) for step in (2, 3, 4)])

        def forward_w(layer):
            wait([w_copy(layer, step) for step in (1, 2, 3, 4)])
            w_copy(layer, 5).start()

        def close_w(layer):
            w_copy(layer, 5).wait()
            for holder in range(4):
                rows = GA[layer, holder * share : (holder + 1) * share].reshape(channels, width).astype(BF16)
                WOB[holder * LANES : (holder + 1) * LANES] = rows[0:LANES]
                WOB[4 * LANES + holder * HEAD : 4 * LANES + (holder + 1) * HEAD] = rows[LANES:channels]

        def attn_out(chunk):
            wait(o_copies(chunk))
            places = [(DQ, sent_at(chunk, core))] + [(DK, landed_at(source, chunk)) for source in range(3)]
            thirds = []
            for holder, (ref, first) in zip((mp, sibling, across, diagonal), places):
                OD[holder] = ref[pl.ds(first, HALF)].astype(BF16)
                both = ref[pl.ds(first + HALF, HALF // 2)]
                thirds.append(jnp.concatenate([both * real, swap_halves(both) * real], axis=0))
            chip = mp // 2
            for place, (same, other) in ((chip, thirds[:2]), (1 - chip, thirds[2:])):
                low, high = jnp.where(core == 0, same, other), jnp.where(core == 0, other, same)
                OD[4 + place] = (low + swap_halves(high)).astype(BF16)
            return mm(jnp.concatenate([OD[tile] for tile in range(6)], axis=1), WOB[...])

        def open_middle(layer, chunk, turn, target):
            x1 = X[layer, chunk] + attn_out(chunk) + rv(layer, 4)
            X1[layer, chunk] = x1
            hat, _ = norm_rows(x1)
            own = (hat * (1.0 + rv(layer, 2)) + rv(layer, 3)).astype(BF16).astype(F32)
            open_gather(turn, own, target)

        def up(layer, second):
            before = mm(second, WU[...]) + ub_ref[layer : layer + 1, :]
            cdf = 0.5 * (1.0 + lax.erf(before * math.sqrt(0.5)))
            density = jnp.exp(before * before * -0.5) * (1.0 / math.sqrt(2.0 * math.pi))
            return (before * cdf).astype(BF16), cdf + before * density

        LAG = 3

        def forward_first():
            def slot(i, carry):
                @pl.when(i == 1)
                def _():
                    spread_w(0)

                @pl.when(i < chunks)
                def _():
                    pack(i)
                    project(0, i)

                @pl.when((i > 0) & (i <= chunks))
                def _():
                    attend(0, i - 1)

                @pl.when(i == LAG)
                def _():
                    forward_w(0)
                    wait(load_mlp(0))
                    close_w(0)

                @pl.when(i == chunks)
                def _():
                    load_wo(last).wait()
                    open_w(last)
                    start([load_wq(last)] + cot_load)

                @pl.when(i == chunks + 1)
                def _():
                    start(spills(False))
                    spread_w(last)

                @pl.when(i >= LAG)
                def _():
                    j = i - LAG
                    turn = j % 2
                    open_middle(0, j, turn, C0.at[j])
                    close_gather(turn, C0.at[j])
                    act, slope = up(0, whole(C0, j))
                    G0[j] = act
                    GP0[j] = slope.astype(BF16)
                    put_part(j, mm(act, WD[...]))
                    send_part(0, j)

                return carry

            lax.fori_loop(0, chunks + LAG, slot, 0)

        def up_grads(layer, second, grad_before):
            GU[layer] += tm(second, grad_before).reshape(n_dp, block, hidden)
            add_vec(layer, UP_BIAS_ROW, column_sum(grad_before.astype(F32)))

        def down_grads(layer, act, grad_out):
            GD[layer] += tm(grad_out, act).reshape(n_dp, block, hidden)

        def pump(name, i):
            for (where, index), events in plan.items():
                if where == name:

                    @pl.when(i == index)
                    def _():
                        for grad_sum, event in events:
                            grad_sum.take(*event)

        def mlp_turn(layer, phase, chunk):
            second = whole(CT, 0)
            act, slope = up(layer, second)

            @pl.when(chunk > 0)
            def _():
                pltpu.make_async_copy(STAGE.at[0], spill_y.at[chunk - 1], stage_sem.at[0]).wait()

            STAGE[0] = mm(act, WD[...]).reshape(2, HALF, width)
            pltpu.make_async_copy(STAGE.at[0], spill_y.at[chunk], stage_sem.at[0]).start()
            grad = INP[pl.ds(chunk * CHUNK, CHUNK), :].astype(F32) * LIVE[chunk, :, 0:1]
            CT[1] = grad.astype(BF16).reshape(2, HALF, width)
            own = CT[1, core].astype(F32)
            DX[chunk] = own
            add_vec(layer, 5, column_sum(own))
            grad = grad.astype(BF16)
            grad_before = (mt(grad, WD[...]) * slope).astype(BF16)
            put_part(chunk, mt(grad_before, WU[...]))
            up_grads(layer, second, grad_before)
            down_grads(layer, act, grad)
            send_part(phase, chunk)

        def forward_last():
            GU[last] = jnp.zeros((n_dp, block, hidden), F32)
            GD[last] = jnp.zeros((n_dp, block, hidden), F32)

            def slot(i, carry):
                j = i - LAG
                turn = (i + LAG) % 2

                @pl.when(i < chunks)
                def _():
                    x = X1[last - 1, i] + total_of(0, i) + rv(last - 1, 5)
                    X[last, i] = x
                    hat, _ = norm_rows(x)
                    own = (hat * (1.0 + rv(last, 0)) + rv(last, 1)).astype(BF16).astype(F32)
                    open_gather(i % 2, own, A.at[i])
                    close_gather(i % 2, A.at[i])

                @pl.when(i == 1)
                def _():
                    forward_w(last)

                @pl.when(i == LAG)
                def _():
                    close_w(last)
                    wait(load_mlp(last) + cot_load)

                @pl.when(i >= LAG)
                def _():
                    open_middle(last, j, turn, CT.at[0])

                @pl.when(i < chunks)
                def _():
                    project(last, i)

                @pl.when((i > 0) & (i <= chunks))
                def _():
                    attend(last, i - 1)

                @pl.when(i >= LAG)
                def _():
                    close_gather(turn, CT.at[0])
                    mlp_turn(last, 1, j)

                return carry

            lax.fori_loop(0, chunks + LAG, slot, 0)
            pltpu.make_async_copy(STAGE.at[0], spill_y.at[chunks - 1], stage_sem.at[0]).wait()

        def input_back(layer, phase, chunk):
            grad_normed = total_of(phase - 1, chunk)
            hat, rstd = norm_rows(X[layer, chunk])
            add_vec(layer, 0, column_sum(grad_normed * hat))
            add_vec(layer, 1, column_sum(grad_normed))
            return DX[chunk] + norm_back(grad_normed * (1.0 + rv(layer, 0)), hat, rstd)

        def mlp_backward(layer, phase, name):
            GU[layer] = jnp.zeros((n_dp, block, hidden), F32)
            GD[layer] = jnp.zeros((n_dp, block, hidden), F32)

            def slot(i, carry):
                grad = input_back(layer + 1, phase, i)
                DX[i] = grad
                own = grad.astype(BF16).astype(F32)
                add_vec(layer, 5, column_sum(own))
                turn = i % 2
                open_gather(turn, own, CT.at[turn])

                @pl.when(i > 0)
                def _():
                    down_grads(layer, G0[i - 1], whole(CT, 1 - turn))

                close_gather(turn, CT.at[turn])
                grad_before = (mt(whole(CT, turn), WD[...]) * GP0[i].astype(F32)).astype(BF16)
                put_part(i, mt(grad_before, WU[...]))
                up_grads(layer, whole(C0, i), grad_before)
                send_part(phase, i)
                pump(name, i)
                return carry

            lax.fori_loop(0, chunks, slot, 0)
            down_grads(layer, G0[chunks - 1], whole(CT, (chunks - 1) % 2))

        def attend_back(layer, chunk):
            grad = whole(CT, chunk % 2)
            grad_heads = [tile.astype(BF16) for tile in apart_heads(mt(grad, WO[...]))]
            ring = chunk % WINDOW
            for head in range(heads):
                grad_o = grad_heads[head]
                query = Q[head, chunk]
                keys, values = window(K, head, chunk), window(V, head, chunk)
                cross = O[head, chunk].astype(F32) * grad_o.astype(F32)
                delta = sum(mt(jnp.ones((8, LANES), BF16), piece) for piece in pieces(cross, 2))[0:1]
                probs = jnp.exp2(mt(keys, query) * EXP2_SCALE - LSE[layer, head, chunk])
                grad_scores = (probs * (mt(values, grad_o) - delta)).astype(BF16)
                grad_v = mm(probs.astype(BF16), grad_o)
                grad_k = mm(grad_scores, query)
                DQ[dq_rows(chunk % 2, head)] = tm(grad_scores, keys) * SCALE
                for part in range(WINDOW):
                    place = (ring + part + WINDOW - 1) % WINDOW
                    rows = slice(part * CHUNK, (part + 1) * CHUNK)
                    if part < WINDOW - 1:
                        DV[head, place] += grad_v[rows]
                        DK[dk_rows(head, place)] += grad_k[rows]
                    else:
                        DV[head, place] = grad_v[rows]
                        DK[dk_rows(head, place)] = grad_k[rows]

        def between_back(layer, chunk):
            out = [O[head, chunk].astype(F32) for head in range(heads)]
            packed = joined_heads([jnp.zeros_like(out[0])] + out).astype(BF16)
            grad = whole(CT, chunk % 2)
            GA[layer, :, :, attn_cols - 2 * LANES :] += tm(grad, packed).reshape(n_dp, block, 2 * LANES)
            normed = whole(A, chunk)
            for kind in range(2):
                HATS[kind, 0], HATS[kind, 1] = norm_heads(mt(normed, WQ[kind]) + hv(layer, kind))

        def project_back(layer, chunk):
            ring, turn = chunk % WINDOW, chunk % 2
            grad_q = joined_heads([DQ[dq_rows(turn, head)] * real for head in range(heads)])
            grad_k = joined_heads([DK[dk_rows(head, ring)] * (real * SCALE) for head in range(heads)])
            grad_v = joined_heads([DV[head, ring] for head in range(heads)])
            parts = []
            for kind, grad in enumerate((grad_q, grad_k)):
                hat, rstd = HATS[kind, 0], HATS[kind, 1]
                inner = norm_heads_back(grad * (1.0 + hv(layer, 3 + kind)), hat, rstd)
                add_vec(layer, HEAD_ROW + kind, column_sum(inner))
                add_vec(layer, HEAD_ROW + 3 + kind, column_sum(grad * hat))
                parts.append(inner)
            add_vec(layer, HEAD_ROW + 5, column_sum(grad_q))
            add_vec(layer, HEAD_ROW + 2, column_sum(grad_v))
            parts.append(grad_v)
            put_part(chunk, sum(mm(part.astype(BF16), WQ[kind]) for kind, part in enumerate(parts)))
            firsts = [part[:, 0:LANES] for part in parts]
            third_q, third_k, third_v = (part[:, LANES:] for part in parts)
            packed = jnp.concatenate(firsts + [third_q + swap_halves(third_k), third_v], axis=1).astype(BF16)
            cols = packed.shape[1]
            GA[layer, :, :, 0:cols] += tm(whole(A, chunk), packed).reshape(n_dp, block, cols)

        def attn_backward(layer, phase, name):
            GA[layer] = jnp.zeros((n_dp, block, attn_cols), F32)
            DK[...] = jnp.zeros_like(DK)
            DV[...] = jnp.zeros_like(DV)

            def slot(i, carry):
                @pl.when(i < chunks)
                def _():
                    grad_second = total_of(phase - 1, i)
                    hat, rstd = norm_rows(X1[layer, i])
                    add_vec(layer, 2, column_sum(grad_second * hat))
                    add_vec(layer, 3, column_sum(grad_second))
                    grad = DX[i] + norm_back(grad_second * (1.0 + rv(layer, 2)), hat, rstd)
                    DX[i] = grad
                    own = grad.astype(BF16).astype(F32)
                    add_vec(layer, 4, column_sum(own))
                    open_gather(i % 2, own, CT.at[i % 2])

                @pl.when(i > 0)
                def _():
                    between_back(layer, i - 1)

                @pl.when(i < chunks)
                def _():
                    close_gather(i % 2, CT.at[i % 2])
                    attend_back(layer, i)

                pump(name + "m", i)

                @pl.when(i > 0)
                def _():
                    project_back(layer, i - 1)
                    send_part(phase, i - 1)

                pump(name, i)
                return carry

            lax.fori_loop(0, chunks + 1, slot, 0)

        near_first = [1, 0] + list(range(2, bits)) if bits > 1 else list(range(bits))

        def results(layer, kinds):
            pairs = [
                (GU.at[layer, dp], up_out),
                (GD.at[layer, dp], down_out),
                (QKV_STAGE.at[layer], qkv_out),
                (WO_STAGE.at[layer], wo_out),
            ]
            return [
                pltpu.make_async_copy(pairs[kind][0], pairs[kind][1].at[layer], out_sem.at[layer, kind]) for kind in kinds
            ]

        def finish_attn(layer):
            tiles = [GA[layer, dp, :, t * LANES : (t + 1) * LANES] for t in range(attn_cols // LANES)]
            thirds = [tiles[3], swap_halves(tiles[3]), tiles[4]]
            for kind in range(3):
                QKV_STAGE[layer, kind, :, 0:LANES] = tiles[kind]
                QKV_STAGE[layer, kind, :, LANES:channels] = thirds[kind][:, 0 : channels - LANES]
            later = swap_halves(tiles[5])
            WO_STAGE[layer, 0:LANES, :] = jnp.where(lane < HEAD, swap_halves(tiles[4]), later).T
            WO_STAGE[layer, LANES:channels, :] = later.T[0 : channels - LANES]
            start(results(layer, (2, 3)))

        def order_of(kind, layer):
            return near_first if NEAR_FIRST[kind, int(layer == last)] else list(range(bits))

        def grad_sum(kind, layer):
            order = order_of(kind, layer)
            next_order = order_of(kind, 0) if layer == last else None
            grad, landing = ((GU, RU), (GD, RD), (GA, RA))[kind]

            def finish():
                if kind < 2:
                    start(results(layer, (kind,)))
                else:
                    finish_attn(layer)

            return GradSum(
                n_dp, dp, mp, order, grad.at[layer], landing, g_send.at[kind], g_recv.at[kind], credit.at[kind],
                next_order, finish,
            )

        sums = {(kind, layer): grad_sum(kind, layer) for layer in (last, 0) for kind in range(3)}
        plan = plan_sums(sums, last)

        first_loads = [load(patches_in, INP, 4), load_wq(0)]
        cot_load = [load(cot_in, INP, 4)]
        load_wo(0).start()
        start(first_loads + load_mlp(0))
        load_wo(0).wait()
        pl.semaphore_wait(barrier, 4 + bits)
        open_w(0)
        load_wo(last).start()
        VEC[...] = jnp.zeros_like(VEC)
        WQ[:, channels:] = jnp.zeros((3, WQ.shape[1] - channels, width), BF16)
        WO[channels:] = jnp.zeros((WO.shape[0] - channels, width), BF16)
        HV[...] = jnp.zeros_like(HV)
        HV[:, :, 0:channels] = hv_ref[...]
        across_lanes = lax.broadcasted_iota(jnp.int32, BLOCKS.shape, 0) // HEAD
        same_head = across_lanes == lax.broadcasted_iota(jnp.int32, BLOCKS.shape, 1) // HEAD
        BLOCKS[...] = jnp.where(same_head, 1.0 / HEAD, 0.0).astype(BF16)
        keep = jnp.broadcast_to(keep_ref[...].astype(F32), (8, tokens))
        earlier = lax.broadcasted_iota(jnp.int32, (tokens, tokens), 0)
        later = lax.broadcasted_iota(jnp.int32, (tokens, tokens), 1)
        count = mm(keep.astype(BF16), (earlier <= later).astype(F32).astype(BF16))
        place = jnp.where(keep > 0.0, count - 1.0, 2.0 * tokens)
        TROW[...] = place
        TCOL[...] = jnp.broadcast_to(place[0:1, :], (LANES, tokens)).T
        segment = jnp.broadcast_to(seg_ref[...].astype(F32), (LANES, tokens)).T
        QA[...] = (segment.astype(jnp.int32) == lane - HEAD).astype(F32).astype(BF16).reshape(chunks, CHUNK, LANES)
        padding = jnp.broadcast_to((lane == PAD).astype(F32), (CHUNK, LANES)).astype(BF16)
        for head in range(heads):
            for edge in (0, chunks + 1):
                K[head, edge] = padding
                V[head, edge] = jnp.zeros((CHUNK, LANES), BF16)
        wait(first_loads)

        forward_first()
        wait(spills(False) + [load_wq(last)])
        start(load_mlp(last))
        forward_last()
        start(load_mlp(0))
        sums[0, last].start()
        sums[1, last].start()
        attn_backward(last, 2, "a1")
        sums[2, last].start()
        start(spills(True) + [load_wq(0), load_wo(0)])
        wait(load_mlp(0))
        mlp_backward(0, 3, "m0")
        sums[0, 0].start()
        sums[1, 0].start()
        wait(spills(True) + [load_wq(0), load_wo(0)])
        attn_backward(0, 4, "a0")
        sums[2, 0].start()

        def end_slot(i, carry):
            rows = input_back(0, 5, i)
            reload = pltpu.make_async_copy(spill_y.at[i], PART.at[i], stage_sem.at[0])
            reload.start()
            halves = X.at[:, i]
            open_gather(i % 2, rows, halves)
            reload.wait()
            to_sibling(i).start()
            close_gather(i % 2, halves)
            send_part(5, i)
            pump("end", i)
            return carry

        lax.fori_loop(0, chunks, end_slot, 0)

        def vec_copy(step, target):
            return pltpu.make_async_remote_copy(
                src_ref=VEC,
                dst_ref=VLAND.at[step],
                send_sem=v_send.at[step],
                recv_sem=v_recv.at[step],
                device_id=target,
                device_id_type=MESH,
            )

        def unpack(patch_chunk, stage):
            stage[...] = jnp.zeros(stage.shape, F32)
            place = TCOL[pl.ds(patch_chunk * CHUNK, CHUNK), 0:1].astype(jnp.int32)

            def add_slots(chunk, carry):
                slot = lax.broadcasted_iota(jnp.int32, (CHUNK, CHUNK), 1) + chunk * CHUNK
                chosen = (place == slot).astype(F32).astype(BF16)
                rest = jnp.concatenate([X[0, chunk], X[1, chunk]], axis=0)
                for piece in pieces(rest, 3):
                    stage[...] += mm(chosen, piece).reshape(stage.shape)
                return carry

            lax.fori_loop(0, patch_chunk + 1, add_slots, 0)

        def patch_copy(patch_chunk, turn):
            return pltpu.make_async_copy(STAGE.at[turn], gpatch_out.at[patch_chunk], stage_sem.at[turn])

        def out_copy(chunk):
            return pltpu.make_async_copy(A.at[chunk], packed_out.at[chunk], spill_sem.at[chunk])

        def chosen_part(values, share):
            column = lax.broadcasted_iota(jnp.int32, (values.shape[1], LANES), 0)
            wanted = lax.broadcasted_iota(jnp.int32, (values.shape[1], LANES), 1)
            chosen = ((column == wanted + dp * share) & (wanted < share)).astype(F32).astype(BF16)
            return mm_exact(values, chosen, 3)[:, 0:share]

        def vec_results():
            for layer in range(layers):
                rows = chosen_part(VEC[layer, 0:UP_BIAS_ROW, :], block)
                for row in range(ROW_VECTORS):
                    row_out[row, layer : layer + 1, :] = rows[row : row + 1]
                rows = chosen_part(VEC[layer, UP_BIAS_ROW : 2 * UP_BIAS_ROW, 0:hidden], hidden // n_dp)
                bias_out[layer : layer + 1, :] = rows[0:1]
                rows = chosen_part(VEC[layer, UP_BIAS_ROW : 2 * UP_BIAS_ROW, 0 : HV.shape[2]], channels // n_dp)
                for row in range(HEAD_VECTORS):
                    place = HEAD_ROW - UP_BIAS_ROW + row
                    head_out[row, layer : layer + 1, :] = rows[place : place + 1]

        def vec_partner(step):
            return (dp, sibling) if step == 0 else (flipped(dp, [step - 1]), mp)

        def vec_step(step):
            vec_copy(step, vec_partner(step)).wait()
            if step == 0:
                VEC[:, 0:UP_BIAS_ROW, :] += VLAND[0, :, 0:UP_BIAS_ROW, :]
            else:
                VEC[...] += VLAND[step]
            if step < bits:
                vec_copy(step + 1, vec_partner(step + 1)).start()
            else:
                vec_results()

        def unpack_next(step):
            turn = step % 2
            if step >= 2:
                patch_copy(step - 2, turn).wait()
            unpack(step, STAGE.at[turn])
            patch_copy(step, turn).start()

        vec_copy(0, vec_partner(0)).start()
        unpack_next(0)
        for step in range(chunks):
            if step <= bits:
                vec_step(step)
            for job, event in plan.get(("tail", step), []):
                job.take(*event)
            rows = (X1[last, step] + total_of(5, step) + rv(last, 5)) * LIVE[step, pl.ds(core * HALF, HALF), 0:1]
            open_gather(step % 2, rows.astype(BF16).astype(F32), A.at[step])
            if step + 1 < chunks:
                unpack_next(step + 1)
            close_gather(step % 2, A.at[step])
            out_copy(step).start()
        for step in range(chunks, bits + 1):
            vec_step(step)
        for job, event in plan.get(("tail", chunks), []):
            job.take(*event)

        for step in range(max(0, chunks - 2), chunks):
            patch_copy(step, step % 2).wait()
        for step in range(chunks):
            out_copy(step).wait()
        for job in sums.values():
            assert len(job.taken) == n_dp - 1
        for layer in range(layers):
            wait(results(layer, range(4)))

    return kernel


def body(n_dp, patches, patch_keep, patch_segment, cotangent, w_qkv, w_out, w_up, w_down, head_vectors, up_bias, row_vectors):
    tokens, width = patches.shape
    layers = w_qkv.shape[0]
    channels = w_qkv.shape[3]
    heads = channels // HEAD
    hidden = w_up.shape[2]
    chunks = tokens // CHUNK
    bits = n_dp.bit_length() - 1
    block = width // n_dp
    attn_cols = 4 * channels

    channels_up = (heads + 1) // 2 * LANES
    wq = jnp.transpose(w_qkv, (0, 1, 3, 2))
    hv = jnp.transpose(head_vectors, (1, 0, 2))
    rv = jnp.transpose(row_vectors, (1, 0, 2))
    any_space = pl.BlockSpec(memory_space=pl.ANY)
    vmem = pl.BlockSpec(memory_space=pltpu.VMEM)
    sds = jax.ShapeDtypeStruct
    half = (HALF, width)
    head_chunks = (heads, chunks, CHUNK, LANES)
    head_window = (heads, chunks + 2, CHUNK, LANES)
    out_shape = [
        sds((chunks, 2) + half, BF16),
        sds((chunks, 2) + half, F32),
        sds((layers, 3, block, channels), F32),
        sds((layers, channels, block), F32),
        sds((layers, block, hidden), F32),
        sds((layers, block, hidden), F32),
        sds((HEAD_VECTORS, layers, channels // n_dp), F32),
        sds((layers, hidden // n_dp), F32),
        sds((ROW_VECTORS, layers, block), F32),
        sds(head_chunks, BF16),
        sds(head_window, BF16),
        sds(head_window, BF16),
        sds(head_chunks, BF16),
        sds((chunks, 2) + half, BF16),
        sds((chunks, 2) + half, F32),
    ]
    v = pltpu.VMEM
    dma = pltpu.SemaphoreType.DMA
    scratch = [
        v((tokens, width), BF16),
        v((3, channels_up, width), BF16),
        v((channels_up, width), BF16),
        v((width, hidden), BF16),
        v((hidden, width), BF16),
        v((layers, chunks) + half, F32),
        v((layers, chunks) + half, F32),
        v((chunks, 2) + half, BF16),
        v((chunks, 2) + half, BF16),
        v((2, 2) + half, BF16),
        v(head_chunks, BF16),
        v(head_window, BF16),
        v(head_window, BF16),
        v(head_chunks, BF16),
        v((layers, heads, chunks, 1, CHUNK), F32),
        v((HEAD_VECTORS, layers, channels_up), F32),
        v((channels_up, channels_up), BF16),
        v((chunks, CHUNK, hidden), BF16),
        v((chunks, CHUNK, hidden), BF16),
        v((chunks, CHUNK, LANES), BF16),
        v((chunks, CHUNK, LANES), BF16),
        v((chunks, CHUNK, LANES), F32),
        v((8, tokens), F32),
        v((tokens, LANES), F32),
        v((chunks, 2) + half, F32),
        v((2,) + half, F32),
        v((2, chunks) + half, F32),
        v((2,) + half, F32),
        v(half, F32),
        v((chunks,) + half, F32),
        v((width, width), BF16),
        v((6, HALF, LANES), BF16),
        v((2 * heads * CHUNK, LANES), F32),
        v((2, 2, CHUNK, channels_up), F32),
        v((heads * WINDOW * CHUNK, LANES), F32),
        v((heads, WINDOW, CHUNK, LANES), F32),
        v((layers, n_dp, block, hidden), F32),
        v((layers, n_dp, block, hidden), F32),
        v((layers, n_dp, block, attn_cols), F32),
        v((n_dp - 1, block, hidden), F32),
        v((n_dp - 1, block, hidden), F32),
        v((n_dp - 1, block, attn_cols), F32),
        v((layers, VEC_ROWS, width), F32),
        v((bits + 1, layers, VEC_ROWS, width), F32),
        v((2, 2) + half, F32),
        v((layers, 3, block, channels), F32),
        v((layers, channels, block), F32),
        dma((5,)),
        dma((5,)),
        dma((2,)),
        dma((2,)),
        dma((2,)),
        dma((2, chunks)),
        dma((2, chunks)),
        dma((2,)),
        dma((2,)),
        dma((3, chunks)),
        dma((3, chunks)),
        dma((layers, 6)),
        dma((layers, 6)),
        dma((3, n_dp - 1)),
        dma((3, n_dp - 1)),
        pltpu.SemaphoreType.REGULAR((3, bits)),
        dma((bits + 1,)),
        dma((bits + 1,)),
        dma((layers, 4)),
    ]
    results = pl.pallas_call(
        make_kernel(n_dp, tokens, width, hidden, heads, layers),
        out_shape=out_shape,
        in_specs=[vmem] * 5 + [any_space] * 6,
        out_specs=[any_space] * 6 + [vmem] * 3 + [any_space] * (len(out_shape) - 9),
        scratch_shapes=scratch,
        compiler_params=pltpu.CompilerParams(
            collective_id=0, has_side_effects=True, vmem_limit_bytes=64 * 2**20 - 2**16
        ),
    )(patch_keep, patch_segment, hv, up_bias, rv, patches, cotangent, wq, w_out, w_up, w_down)
    packed, grad_patches, grad_qkv, grad_out, grad_up, grad_down, head_grads, bias_grads, row_grads = results[:9]
    return (
        packed.reshape(tokens, width),
        grad_patches.reshape(tokens, width),
        grad_qkv,
        grad_out,
        grad_up,
        jnp.transpose(grad_down, (0, 2, 1)),
        jnp.transpose(head_grads, (1, 0, 2)),
        bias_grads,
        jnp.transpose(row_grads, (1, 0, 2)),
    )


def solution(mesh):
    n_dp = mesh.shape["dp"]

    def step(*args):
        return body(n_dp, *args)

    return jax.shard_map(
        step,
        mesh=mesh,
        in_specs=(
            P("dp", None),
            P("dp", None),
            P("dp", None),
            P("dp", None),
            P(None, None, None, "mp"),
            P(None, "mp", None),
            P(None, None, "mp"),
            P(None, "mp", None),
            P(None, None, "mp"),
            P(None, "mp"),
            P(),
        ),
        out_specs=(
            P("dp", None),
            P("dp", None),
            P(None, None, "dp", "mp"),
            P(None, "mp", "dp"),
            P(None, "dp", "mp"),
            P(None, "mp", "dp"),
            P(None, None, ("mp", "dp")),
            P(None, ("mp", "dp")),
            P(None, None, "dp"),
        ),
        check_vma=False,
    )
```
